32 devices in a mesh: section: 4 (over z), dp: 2 (over y), tensor: 4 (over x, core).
Axes of the slice: x: 2, y: 2, z: 4, core: 2. Of those that a mesh axis runs over, the one named last changes fastest.
Arguments:
- images: float32 [4, 732, 1152], P('dp', 'tensor'), may hold values from -6 to 6
- valid_len: int32 [4], P('dp'), may hold values from 366 to 732
- query_weight: bfloat16 [4, 1152, 1152], P('section', 'dp', 'tensor'), may hold values from -0.1875 to 0.1875
- key_weight: bfloat16 [4, 1152, 1152], P('section', 'dp', 'tensor'), may hold values from -0.1875 to 0.1875
- value_weight: bfloat16 [4, 1152, 1152], P('section', 'dp', 'tensor'), may hold values from -0.1875 to 0.1875
- output_weight: bfloat16 [4, 1152, 1152], P('section', 'tensor', 'dp'), may hold values from -1 to 1
- up_weight: bfloat16 [4, 1152, 4304], P('section', 'dp', 'tensor'), may hold values from -0.1875 to 0.1875
- down_weight: bfloat16 [4, 4304, 1152], P('section', 'tensor', 'dp'), may hold values from -0.09375 to 0.09375
- norm_gains: float32 [4, 2, 1152], P('section', None, ('dp', 'tensor')), may hold values from 0.5 to 1.5
- cotangent: float32 [4, 732, 1152], P('dp', 'tensor'), may hold values from -6 to 6
Outputs:
- activations: float32 [4, 4, 732, 1152], P('section', 'dp', 'tensor')
- input_grads: float32 [4, 4, 732, 1152], P('section', 'dp', 'tensor')
- grad_query: float32 [4, 1152, 1152], P('section', 'dp', 'tensor')
- grad_key: float32 [4, 1152, 1152], P('section', 'dp', 'tensor')
- grad_value: float32 [4, 1152, 1152], P('section', 'dp', 'tensor')
- grad_output: float32 [4, 1152, 1152], P('section', 'tensor', 'dp')
- grad_up: float32 [4, 1152, 4304], P('section', 'dp', 'tensor')
- grad_down: float32 [4, 4304, 1152], P('section', 'tensor', 'dp')
- grad_gains: float32 [4, 2, 1152], P('section', None, ('dp', 'tensor'))
The draws below stay inside these ranges and needn't reach their ends.
Inputs may be any that keep to these rules, and one draw needn't show every extreme that they name: `valid_len`: number of valid tokens of each image; the keys of later slots are masked.
All inputs are finite; a program needn't handle non-finite values.
Results may differ from the reference program's by a relative error of at most 0.025.
Values may be sent and summed in bfloat16 or wider, within the bound.
No kernel may reach another device: no remote copies, remote signals or barrier semaphores. Data moves between devices by JAX's collectives and lax.ppermute only.
A program may use at most 320 MiB of HBM per device.

```python
from functools import partial
import jax
import jax.numpy as jnp
from jax import lax

D = 1152
HEADS = 16
FF = 4304
HD = 72
SEQ = 732
LAYERS = 4
IMAGES = 4


def touch_ends(result, stream_key, least, high):
    place = [jax.random.randint(jax.random.fold_in(stream_key, axis), (), 0, length) for axis, length in enumerate(result.shape)]
    main_axis = result.shape.index(max(result.shape))
    beside = place[:main_axis] + [(place[main_axis] + 1) % result.shape[main_axis]] + place[main_axis + 1:]
    return result.at[tuple(place)].set(least).at[tuple(beside)].set(high)


def shard_levels(rng, extent, split, smallest, top_value):
    loudness = 1.0
    for position, shards_of in split:
        heights = jax.random.uniform(jax.random.fold_in(jax.random.fold_in(rng, 6), position), (shards_of,), jnp.float32, smallest / len(split), top_value / len(split))
        loudness = loudness * jnp.repeat(jnp.exp(heights), extent[position] // shards_of).reshape((-1,) + (1,) * (len(extent) - 1 - position))
    return loudness


def scatter_about(stream_key, extent, width, reach, cuts=(), dtype=jnp.bfloat16):
    level = shard_levels(stream_key, extent, cuts, -0.22, 0.18) if cuts else 1.0
    drawn = jax.random.normal(stream_key, extent, jnp.float32) * width * level
    return jnp.minimum(jnp.maximum(drawn, -reach), reach).astype(dtype)


def setup_inputs(seed: int = 0) -> dict:
    splits = jax.random.split(jax.random.key(seed), 11)
    return {
        "images": scatter_about(splits[0], (IMAGES, SEQ, D), 1.0, 6.0, ((0, 2), (1, 4)), jnp.float32),
        "valid_len": touch_ends(jax.random.randint(splits[1], (IMAGES,), SEQ // 2, SEQ + 1), jax.random.fold_in(splits[1], 1), SEQ // 2, SEQ).astype(jnp.int32),
        "query_weight": scatter_about(splits[2], (LAYERS, D, D), D ** -0.5, 0.1875, ((0, 4), (1, 2), (2, 4))),
        "key_weight": scatter_about(splits[3], (LAYERS, D, D), D ** -0.5, 0.1875, ((0, 4), (1, 2), (2, 4))),
        "value_weight": scatter_about(splits[4], (LAYERS, D, D), D ** -0.5, 0.1875, ((0, 4), (1, 2), (2, 4))),
        "output_weight": scatter_about(splits[5], (LAYERS, D, D), (max(D // 32, 1)) ** -0.5, 1.0, ((0, 4), (1, 4), (2, 2))),
        "up_weight": scatter_about(splits[6], (LAYERS, D, FF), D ** -0.5, 0.1875, ((0, 4), (1, 2), (2, 4))),
        "down_weight": scatter_about(splits[7], (LAYERS, FF, D), FF ** -0.5, 0.09375, ((0, 4), (1, 4), (2, 2))),
        "norm_gains": jnp.clip(0.5 + 1.0 * jax.random.uniform(splits[8], (LAYERS, 2, D), jnp.float32) ** shard_levels(splits[8], (LAYERS, 2, D), ((0, 4), (2, 8)), -0.2, 0.2), 0.5, 1.5),
        "cotangent": scatter_about(splits[9], (IMAGES, SEQ, D), 1.0, 6.0, ((0, 2), (1, 4)), jnp.float32),
    }


EPS = 1e-06
HIGH = lax.Precision.HIGHEST

@jax.custom_vjp
def low(v):
    return lax.optimization_barrier(v.astype(jnp.bfloat16)).astype(jnp.float32)

@jax.custom_vjp
def low_back(v):
    return v

def low_keep(v):
    return (low(v), None)

def low_pass(kept, grad):
    return (grad,)

def back_keep(v):
    return (v, None)

def back_low(kept, grad):
    return (low(grad),)
low.defvjp(low_keep, low_pass)
low_back.defvjp(back_keep, back_low)

def layer_norm(values, gain):
    centre = lax.optimization_barrier(jnp.mean(values, axis=-1, keepdims=True))
    centred = values - centre
    spread = lax.optimization_barrier(jnp.mean(centred * centred, axis=-1, keepdims=True))
    return centred * lax.rsqrt(spread + EPS) * gain

def one_image(params, pair):
    w_query, w_key, w_value, w_output, w_upper, w_lower, gains = params
    tokens, valid_count = pair
    seq_len = tokens.shape[0]
    normed_a = low(layer_norm(tokens, gains[0]))

    def project(weight):
        return low(low_back(jnp.dot(normed_a, weight, precision=HIGH))).reshape(seq_len, HEADS, HD)
    queries = project(w_query)
    keys_all = project(w_key)
    values_all = project(w_value)
    scores = low_back(jnp.einsum('qhd,khd->hqk', queries, keys_all, precision=HIGH) * HD ** (-0.5))
    live = jnp.arange(seq_len) < valid_count
    scores = jnp.where(live[None, None, :], scores, -1e+30)
    soft_low = low(jax.nn.softmax(scores, axis=-1))
    head_mix = low(low_back(jnp.einsum('hqk,khd->qhd', soft_low, values_all, precision=HIGH))).reshape(seq_len, HEADS * HD)
    hidden = tokens + low_back(jnp.dot(head_mix, w_output, precision=HIGH))
    normed_b = low(layer_norm(hidden, gains[1]))
    inner_pre = low_back(jnp.dot(normed_b, w_upper, precision=HIGH))
    activated = low(jax.nn.gelu(inner_pre, approximate=True))
    return hidden + low_back(jnp.dot(activated, w_lower, precision=HIGH))

def reference(images, valid_len, query_weight, key_weight, value_weight, output_weight, up_weight, down_weight, norm_gains, cotangent):
    weights = tuple((weight.astype(jnp.float32) for weight in (query_weight, key_weight, value_weight, output_weight, up_weight, down_weight)))
    gains_all = norm_gains.astype(jnp.float32)
    offsets = jnp.zeros((LAYERS,) + images.shape, jnp.float32)
    start = images.astype(jnp.float32)

    def forward(offsets, weights, gains_all):
        current = start
        outputs = []
        for layer in range(LAYERS):
            params = tuple((weight[layer] for weight in weights)) + (gains_all[layer],)
            stepper = jax.checkpoint(partial(one_image, params))
            current = lax.map(stepper, (current + offsets[layer], valid_len))
            outputs.append(current)
        return jnp.stack(outputs)
    activations, pull = jax.vjp(forward, offsets, weights, gains_all)
    last_cotangent = jnp.zeros_like(activations).at[LAYERS - 1].set(cotangent.astype(jnp.float32))
    input_grads, weight_grads, gain_grads = pull(last_cotangent)
    return (activations, input_grads, weight_grads[0], weight_grads[1], weight_grads[2], weight_grads[3], weight_grads[4], weight_grads[5], gain_grads)
```

```python
import jax
import jax.numpy as jnp
from jax import lax
from jax.experimental import pallas as pl
from jax.experimental.pallas import tpu as pltpu
from jax.sharding import PartitionSpec as P

HD = 72
EPS = 1e-06
SCALE = HD ** (-0.5)
LOG2E = 1.4426950408889634
BF = jnp.bfloat16
F32 = jnp.float32
WIN = 256
LANES = 128
K0 = 0.7978845608028654
K1 = 0.044715
VMEM = pl.BlockSpec(memory_space=pltpu.VMEM)
SMEM = pl.BlockSpec(memory_space=pltpu.SMEM)
ANY = pl.BlockSpec(memory_space=pl.ANY)


def swap_core(a):
    n = lax.axis_size("tensor")
    return lax.ppermute(a, "tensor", [(i, i ^ 1) for i in range(n)])


def swap_x(a):
    n = lax.axis_size("tensor")
    return lax.ppermute(a, "tensor", [(i, i ^ 2) for i in range(n)])


def swap_y(a):
    return lax.ppermute(a, "dp", [(0, 1), (1, 0)])


def shift(a, by):
    n = lax.axis_size("section")
    pairs = [(i, i + by) for i in range(n) if 0 <= i + by < n]
    return lax.ppermute(a, "section", pairs)


def two_rows():
    return lax.axis_size("dp") == 2


def half_cut(rows):
    return (rows // 2 + 15) // 16 * 16


def row_gather(rows):
    if not two_rows():
        return lax.all_gather(rows, ("dp", "tensor"), axis=0, tiled=True)
    cut = half_cut(rows.shape[0])
    from_x = swap_x(rows)
    from_y = swap_y(rows)
    four = jnp.concatenate((rows, from_x, from_y, swap_x(from_y[:cut]), swap_y(from_x[cut:])), axis=0)
    return jnp.concatenate((four, swap_core(four)), axis=0)


def up32(a):
    return a.astype(F32)


def low16(a):
    return a.astype(BF)


def dot(a, b):
    return jnp.dot(a, b, preferred_element_type=F32)


def dot_t(a, b):
    return lax.dot_general(a, b, (((1,), (1,)), ((), ())), preferred_element_type=F32)


def t_dot(a, b):
    return lax.dot_general(a, b, (((0,), (0,)), ((), ())), preferred_element_type=F32)


def spans(total, size):
    return [(at, min(size, total - at)) for at in range(0, total, size)]


def norm_parts(values):
    centre = jnp.mean(values, axis=-1, keepdims=True)
    centred = values - centre
    spread = jnp.mean(centred * centred, axis=-1, keepdims=True)
    inverse = lax.rsqrt(spread + EPS)
    return centred * inverse, inverse


def norm_back(grad, unit, inverse, gain):
    e = grad * gain
    return inverse * (e - jnp.mean(e, axis=-1, keepdims=True) - unit * jnp.mean(e * unit, axis=-1, keepdims=True))


def gelu_one(u):
    return u * (0.5 + 0.5 * jnp.tanh(u * (K0 + (K0 * K1) * (u * u))))


def gelu_both(u):
    sq = u * u
    th = jnp.tanh(u * (K0 + (K0 * K1) * sq))
    half = 0.5 + 0.5 * th
    return u * half, half + (0.5 * u) * (1.0 - th * th) * (K0 + (3.0 * K1 * K0) * sq)


def head_window(h, width):
    tile = min(h * HD // LANES, width // LANES - WIN // LANES)
    off = h * HD - tile * LANES
    lane = lax.broadcasted_iota(jnp.int32, (1, WIN), 1)
    return slice(tile * LANES, tile * LANES + WIN), (lane >= off) & (lane < off + HD)


def shape(dims, dtype):
    return jax.ShapeDtypeStruct(dims, dtype)


def call(kernel, name, outs, ins, scratch, args, flops, limit=60):
    moved = sum(a.size * a.dtype.itemsize for a in args) + sum(o.size * o.dtype.itemsize for o in outs)
    return pl.pallas_call(
        kernel,
        out_shape=tuple(outs),
        in_specs=ins,
        out_specs=tuple([VMEM] * len(outs)),
        scratch_shapes=scratch,
        compiler_params=pltpu.CompilerParams(vmem_limit_bytes=limit * 2**20),
        cost_estimate=pl.CostEstimate(flops=int(flops * 1.4), bytes_accessed=moved, transcendentals=0),
        name=name,
    )(*args)


def assemble(name, pieces, flags, place, out_dims, extra=()):
    flat = [a for by_x in pieces for by_core in by_x for a in by_core]
    count = len(pieces[0][0])

    def kernel(flag_ref, *refs):
        out = refs[-1]
        grid = [[[refs[(xr * 2 + cr) * count + i] for i in range(count)] for cr in (0, 1)] for xr in (0, 1)]
        first_row = flag_ref[0] == 0
        first_core = flag_ref[1] == 0

        def row(xr, cr, i):
            cell = grid[xr][cr]
            if count != 2:
                return cell[i][...]
            return jnp.where(first_row, cell[i][...], cell[1 - i][...])

        def by_core(xr, c, i):
            return jnp.where(first_core, row(xr, c, i), row(xr, 1 - c, i))

        place(out, row, by_core, count)

    outs = [shape(out_dims, BF)]
    return call(kernel, name, outs, [SMEM] + [VMEM] * len(flat), [], [flags] + flat, 0)[0]


def kv_kernel(*refs):
    held = len(refs) == 11
    if held:
        sel, got, old, gain, w_hbm, x_out, normed_out, kv_out, w, sem, _ = refs
        x = jnp.where(sel[0] == 1, up32(got[...]), old[...])
    else:
        old, gain, w_hbm, normed_out, kv_out, w, sem = refs
    width = w.shape[0]
    parts = spans(2 * width, 512)
    copies = [
        pltpu.make_async_copy(w_hbm.at[:, width + at : width + at + n], w.at[:, at : at + n], sem.at[i])
        for i, (at, n) in enumerate(parts)
    ]
    for copy in copies:
        copy.start()
    if held:
        x_out[...] = x
    else:
        x = old[...]
    normed = low16(norm_parts(x)[0] * gain[...])
    normed_out[...] = normed
    for copy, (at, n) in zip(copies, parts):
        copy.wait()
        kv_out[:, at : at + n] = low16(dot(normed, w[:, at : at + n]))


def project_kv(sel, got, old, gain, w_qkv):
    rows, width = old.shape
    scratch = [pltpu.VMEM((width, 2 * width), BF), pltpu.SemaphoreType.DMA((len(spans(2 * width, 512)),))]
    outs = [shape((rows, width), BF), shape((rows, 2 * width), BF)]
    flops = 4 * rows * width * width
    if got is None:
        return (old, *call(kv_kernel, "keys_values", outs, [VMEM, VMEM, ANY], scratch, [old, gain, w_qkv], flops))
    scratch.append(pltpu.SemaphoreType.DMA((1,)))
    outs = [shape((rows, width), F32)] + outs
    ins = [SMEM, VMEM, VMEM, VMEM, ANY]
    return call(kv_kernel, "keys_values", outs, ins, scratch, [sel, got, old, gain, w_qkv], flops)


def q_kernel(normed, w_hbm, q_out, w, sem):
    width = w.shape[0]
    parts = spans(width, 512)
    copies = [
        pltpu.make_async_copy(w_hbm.at[:, at : at + n], w.at[:, at : at + n], sem.at[i]) for i, (at, n) in enumerate(parts)
    ]
    for copy in copies:
        copy.start()
    for copy, (at, n) in zip(copies, parts):
        copy.wait()
        q_out[:, at : at + n] = low16(dot(normed[...], w[:, at : at + n]))


def project_q(normed, w_qkv):
    rows, width = normed.shape
    scratch = [pltpu.VMEM((width, width), BF), pltpu.SemaphoreType.DMA((len(spans(width, 512)),))]
    return call(
        q_kernel, "queries", [shape((rows, width), BF)], [VMEM, ANY], scratch, [normed, w_qkv], 2 * rows * width * width
    )[0]


def attend(q_ref, kv, bias, mix, lse_ref):
    rows, width = q_ref.shape
    lane = lax.broadcasted_iota(jnp.int32, (1, LANES), 1)
    for h in range(width // HD):
        win, live = head_window(h, width)
        keys = jnp.where(live, kv[:, win], jnp.zeros((), BF))
        vals = kv[:, width + win.start : width + win.stop]
        s = dot_t(q_ref[:, win], keys) * (SCALE * LOG2E) + bias
        top = jnp.max(s, axis=-1, keepdims=True)
        p = jnp.exp2(s - top)
        total = jnp.sum(p, axis=-1, keepdims=True)
        o = dot(low16(p), vals) * (1.0 / total)
        mix[:, win] = jnp.where(live, low16(o), mix[:, win])
        if lse_ref is not None:
            lse_ref[...] = jnp.where(lane == h, top + jnp.log2(total), lse_ref[...])


def feed(normed, hidden, w_up, w_down, act, ups, downs, slope_out, outs):
    units = w_up.shape[1]
    for copy, (at, n) in zip(ups, spans(units, 512)):
        copy.wait()
        u = dot(normed, w_up[:, at : at + n])
        if slope_out is None:
            act[:, at : at + n] = low16(gelu_one(u))
        else:
            a, slope = gelu_both(u)
            act[:, at : at + n] = low16(a)
            slope_out[:, at : at + n] = low16(slope)
    for copy in downs:
        copy.wait()
    for at, n in spans(w_down.shape[1], 256):
        total = hidden[:, at : at + n] + dot(act[...], w_down[:, at : at + n])
        for out in outs:
            out[:, at : at + n] = total.astype(out.dtype)


def layer_attention(q, own, far, bias, x, gain, w_o):
    rows, width = q.shape

    def kernel(q_ref, own_ref, far_ref, bias_ref, x_ref, gain_ref, wo_hbm, hid_ref, nb_ref, kv, wo, mix, sem):
        copies = [
            pltpu.make_async_copy(own_ref, kv.at[:rows], sem.at[0]),
            pltpu.make_async_copy(far_ref, kv.at[rows:], sem.at[1]),
            pltpu.make_async_copy(wo_hbm, wo, sem.at[2]),
        ]
        for copy in copies:
            copy.start()
        copies[0].wait()
        copies[1].wait()
        mix[...] = jnp.zeros_like(mix)
        attend(q_ref, kv, bias_ref[0:1, :], mix, None)
        copies[2].wait()
        hidden = x_ref[...] + dot(mix[...], wo[...])
        hid_ref[...] = hidden
        nb_ref[...] = low16(norm_parts(hidden)[0] * gain_ref[...])

    scratch = [
        pltpu.VMEM((2 * rows, 2 * width), BF),
        pltpu.VMEM((width, width), BF),
        pltpu.VMEM((rows, width), BF),
        pltpu.SemaphoreType.DMA((3,)),
    ]
    outs = [shape((rows, width), F32), shape((rows, width), BF)]
    ins = [VMEM, ANY, ANY, VMEM, VMEM, VMEM, ANY]
    flops = 16 * rows * 2 * rows * WIN * 4 + 2 * rows * width * width
    return call(kernel, "attention_part", outs, ins, scratch, [q, own, far, bias, x, gain, w_o], flops)


def layer_feed(hidden, normed, w_up, w_down):
    rows, width = hidden.shape
    units = w_up.shape[1]
    parts = spans(units, 512)

    def kernel(hid_ref, nb_ref, wu_hbm, wd_hbm, low_ref, wu, wd, act, sem):
        n = len(parts)
        ups = [pltpu.make_async_copy(wu_hbm.at[:, a : a + k], wu.at[:, a : a + k], sem.at[i]) for i, (a, k) in enumerate(parts)]
        downs = [pltpu.make_async_copy(wd_hbm.at[a : a + k], wd.at[a : a + k], sem.at[n + i]) for i, (a, k) in enumerate(parts)]
        for copy in ups + downs:
            copy.start()
        feed(nb_ref[...], hid_ref, wu, wd, act, ups, downs, None, [low_ref])

    scratch = [
        pltpu.VMEM((width, units), BF),
        pltpu.VMEM((units, width), BF),
        pltpu.VMEM((rows, units), BF),
        pltpu.SemaphoreType.DMA((2 * len(parts),)),
    ]
    return call(
        kernel, "feed_part", [shape((rows, width), BF)], [VMEM, VMEM, ANY, ANY], scratch, [hidden, normed, w_up, w_down],
        4 * rows * width * units,
    )[0]


def layer_whole(full, q, own, far, bias, x, gain, w_o, w_up, w_down):
    rows, width = q.shape
    units = w_up.shape[1]
    parts = spans(units, 512)

    def kernel(q_ref, own_ref, far_ref, bias_ref, x_ref, gain_ref, wo_hbm, wu_hbm, wd_hbm, *rest):
        if full:
            low_ref, out_ref, hid_ref, nb_ref, slope_ref, mix, lse_ref, kv, wo, wu, wd, act, sem = rest
        else:
            low_ref, kv, wo, wu, wd, act, sem, mix, hid_ref = rest
            slope_ref = lse_ref = None
        n = len(parts)
        first = [
            pltpu.make_async_copy(own_ref, kv.at[:rows], sem.at[0]),
            pltpu.make_async_copy(far_ref, kv.at[rows:], sem.at[1]),
            pltpu.make_async_copy(wo_hbm, wo, sem.at[2]),
        ]
        ups = [
            pltpu.make_async_copy(wu_hbm.at[:, a : a + k], wu.at[:, a : a + k], sem.at[3 + i]) for i, (a, k) in enumerate(parts)
        ]
        downs = [
            pltpu.make_async_copy(wd_hbm.at[a : a + k], wd.at[a : a + k], sem.at[3 + n + i]) for i, (a, k) in enumerate(parts)
        ]
        for copy in first + ups + downs:
            copy.start()
        first[0].wait()
        first[1].wait()
        mix[...] = jnp.zeros_like(mix)
        if full:
            lse_ref[...] = jnp.zeros_like(lse_ref)
        attend(q_ref, kv, bias_ref[0:1, :], mix, lse_ref)
        first[2].wait()
        hidden = x_ref[...] + dot(mix[...], wo[...])
        hid_ref[...] = hidden
        normed = low16(norm_parts(hidden)[0] * gain_ref[...])
        if full:
            nb_ref[...] = normed
        feed(normed, hid_ref, wu, wd, act, ups, downs, slope_ref, [low_ref, out_ref] if full else [low_ref])

    outs = [shape((rows, width), BF)]
    scratch = [
        pltpu.VMEM((2 * rows, 2 * width), BF),
        pltpu.VMEM((width, width), BF),
        pltpu.VMEM((width, units), BF),
        pltpu.VMEM((units, width), BF),
        pltpu.VMEM((rows, units), BF),
        pltpu.SemaphoreType.DMA((3 + 2 * len(parts),)),
    ]
    if full:
        outs += [shape((rows, width), F32), shape((rows, width), F32), shape((rows, width), BF)]
        outs += [shape((rows, units), BF), shape((rows, width), BF), shape((rows, LANES), F32)]
    else:
        scratch += [pltpu.VMEM((rows, width), BF), pltpu.VMEM((rows, width), F32)]
    ins = [VMEM, ANY, ANY, VMEM, VMEM, VMEM, ANY, ANY, ANY]
    flops = 16 * rows * 2 * rows * WIN * 4 + 2 * rows * width * width + 4 * rows * width * units
    return call(kernel, "layer", outs, ins, scratch, [q, own, far, bias, x, gain, w_o, w_up, w_down], flops)


def feed_back(full, sel, got, old, slope, hidden, gain, w_up, w_down, w_o):
    rows, width = old.shape
    units = w_up.shape[1]
    parts = spans(units, 512)
    bands = spans(width, 256)
    held = got is not None

    def kernel(*refs):
        if held:
            sel_ref, got_ref, refs = refs[0], refs[1], refs[2:]
        old_ref, slope_hbm, hid_ref, gain_ref, wu_hbm, wd_hbm, wo_hbm = refs[:7]
        refs = refs[7:]
        if held:
            dy_ref, refs = refs[0], refs[1:]
        hg_ref, do_ref, refs = refs[0], refs[1], refs[2:]
        if full:
            dyl_ref, ml_ref, gs_ref, refs = refs[0], refs[1], refs[2], refs[3:]
        wu, wd, wo, slope_s, ig, nbg, sem = refs
        n = len(parts)
        m = len(bands)
        downs = [pltpu.make_async_copy(wd_hbm.at[a : a + k], wd.at[a : a + k], sem.at[i]) for i, (a, k) in enumerate(parts)]
        slopes = [
            pltpu.make_async_copy(slope_hbm.at[:, a : a + k], slope_s.at[:, a : a + k], sem.at[n + i])
            for i, (a, k) in enumerate(parts)
        ]
        ups = [
            pltpu.make_async_copy(wu_hbm.at[a : a + k], wu.at[a : a + k], sem.at[2 * n + i]) for i, (a, k) in enumerate(bands)
        ]
        last = pltpu.make_async_copy(wo_hbm, wo, sem.at[2 * n + m])
        for a, b in zip(downs, slopes):
            a.start()
            b.start()
        for copy in ups + [last]:
            copy.start()
        dy = old_ref[...]
        if held:
            dy = jnp.where(sel_ref[0] == 1, up32(got_ref[...]), dy)
            dy_ref[...] = dy
        down_low = low16(dy)
        if full:
            dyl_ref[...] = down_low
        for i, (at, k) in enumerate(parts):
            downs[i].wait()
            slopes[i].wait()
            ig[:, at : at + k] = low16(dot_t(down_low, wd[at : at + k, :]) * up32(slope_s[:, at : at + k]))
        for i, (at, k) in enumerate(bands):
            ups[i].wait()
            nbg[:, at : at + k] = dot_t(ig[...], wu[at : at + k, :])
        unit, inverse = norm_parts(hid_ref[...])
        grad = nbg[...]
        if full:
            gs_ref[...] = jnp.sum(grad * unit, axis=0, keepdims=True)
        hidden_grad = dy + norm_back(grad, unit, inverse, gain_ref[...])
        hg_ref[...] = hidden_grad
        mix_low = low16(hidden_grad)
        if full:
            ml_ref[...] = mix_low
        last.wait()
        do_ref[...] = low16(dot_t(mix_low, wo[...]))

    ins = [VMEM, ANY, VMEM, VMEM, ANY, ANY, ANY]
    args = [old, slope, hidden, gain, w_up, w_down, w_o]
    outs = [shape((rows, width), F32), shape((rows, width), BF)]
    if held:
        ins = [SMEM, VMEM] + ins
        args = [sel, got] + args
        outs = [shape((rows, width), F32)] + outs
    if full:
        outs += [shape((rows, width), BF), shape((rows, width), BF), shape((1, width), F32)]
    scratch = [
        pltpu.VMEM((width, units), BF),
        pltpu.VMEM((units, width), BF),
        pltpu.VMEM((width, width), BF),
        pltpu.VMEM((rows, units), BF),
        pltpu.VMEM((rows, units), BF),
        pltpu.VMEM((rows, width), F32),
        pltpu.SemaphoreType.DMA((2 * len(parts) + len(bands) + 1,)),
    ]
    flops = 4 * rows * width * units + 2 * rows * width * width
    return call(kernel, "feed_back", outs, ins, scratch, args, flops)


def attention_back(q, own, far, do, mix, lse, bias):
    rows, width = q.shape
    keys_n = 2 * rows

    def kernel(q_ref, own_ref, far_ref, do_ref, o_ref, lse_ref, bias_ref, dq_ref, dkv_own, dkv_far, kv, qt, dt, dkt, dvt, sem):
        copies = [
            pltpu.make_async_copy(own_ref, kv.at[:rows], sem.at[0]),
            pltpu.make_async_copy(far_ref, kv.at[rows:], sem.at[1]),
        ]
        for copy in copies:
            copy.start()
        bias_row = bias_ref[0:1, :]
        qt[...] = up32(q_ref[...]).T
        dt[...] = up32(do_ref[...]).T
        dq_ref[...] = jnp.zeros_like(dq_ref)
        for copy in copies:
            copy.wait()
        zero = jnp.zeros((), BF)
        for h in range(width // HD):
            win, live = head_window(h, width)
            here = slice(h * HD, (h + 1) * HD)
            keys = jnp.where(live, kv[:, win], zero)
            vals = jnp.where(live, kv[:, width + win.start : width + win.stop], zero)
            d_out = do_ref[:, win]
            row_dot = jnp.sum(jnp.where(live, up32(d_out) * up32(o_ref[:, win]), 0.0), axis=-1, keepdims=True)
            s = dot_t(q_ref[:, win], keys) * (SCALE * LOG2E) + bias_row
            p = jnp.exp2(s - lse_ref[:, h : h + 1])
            ds = low16(p * (dot_t(d_out, vals) - row_dot))
            dq = dot(ds, keys) * SCALE
            dq_ref[:, win] = jnp.where(live, low16(dq), dq_ref[:, win])
            dkt[here, :] = dot(low16(qt[here, :]), ds) * SCALE
            dvt[here, :] = dot(low16(dt[here, :]), low16(p))
        dk = low16(dkt[...].T)
        dv = low16(dvt[...].T)
        dkv_own[:, :width] = dk[:rows]
        dkv_own[:, width:] = dv[:rows]
        dkv_far[:, :width] = dk[rows:]
        dkv_far[:, width:] = dv[rows:]

    outs = [shape((rows, width), BF), shape((rows, 2 * width), BF), shape((rows, 2 * width), BF)]
    scratch = [
        pltpu.VMEM((keys_n, 2 * width), BF),
        pltpu.VMEM((width, rows), F32),
        pltpu.VMEM((width, rows), F32),
        pltpu.VMEM((width, keys_n), F32),
        pltpu.VMEM((width, keys_n), F32),
        pltpu.SemaphoreType.DMA((2,)),
    ]
    ins = [VMEM, ANY, ANY, VMEM, VMEM, VMEM, VMEM]
    flops = 16 * rows * keys_n * WIN * 10
    return call(kernel, "attention_back", outs, ins, scratch, [q, own, far, do, mix, lse, bias], flops)


def qkv_back(full, dq, own, got, x, hidden_grad, gain, w_qkv, core):
    rows, width = dq.shape
    span = width // 4
    bands = spans(width, 256)

    def kernel(dq_ref, own_ref, got_ref, x_ref, hg_ref, gain_ref, w_hbm, *rest):
        if full:
            core_ref, rest = rest[0], rest[1:]
            dx_ref, low_ref, keep_ref, give_ref, gs_ref, w, grads, nag, sem = rest
        else:
            low_ref, w, grads, nag, sem = rest
        copies = [pltpu.make_async_copy(w_hbm.at[a : a + k], w.at[a : a + k], sem.at[i]) for i, (a, k) in enumerate(bands)]
        for copy in copies:
            copy.start()
        grads[:, :width] = dq_ref[...]
        grads[:, width:] = low16(up32(own_ref[...]) + up32(got_ref[...]))
        if full:
            mine = core_ref[0] == 0
            for i in range(3):
                for xr in (0, 1):
                    at = i * width + 2 * xr * span
                    lo = grads[:, at : at + span]
                    hi = grads[:, at + span : at + 2 * span]
                    to = xr * 3 * span + i * span
                    keep_ref[:, to : to + span] = jnp.where(mine, lo, hi)
                    give_ref[:, to : to + span] = jnp.where(mine, hi, lo)
        for copy, (at, k) in zip(copies, bands):
            copy.wait()
            nag[:, at : at + k] = dot_t(grads[...], w[at : at + k, :])
        unit, inverse = norm_parts(x_ref[...])
        grad = nag[...]
        if full:
            gs_ref[...] = jnp.sum(grad * unit, axis=0, keepdims=True)
        dx = hg_ref[...] + norm_back(grad, unit, inverse, gain_ref[...])
        low_ref[...] = low16(dx)
        if full:
            dx_ref[...] = dx

    outs = [shape((rows, width), BF)]
    ins = [VMEM, VMEM, VMEM, VMEM, VMEM, VMEM, ANY]
    args = [dq, own, got, x, hidden_grad, gain, w_qkv]
    if full:
        outs = [shape((rows, width), F32)] + outs
        outs += [shape((rows, 6 * span), BF), shape((rows, 6 * span), BF), shape((1, width), F32)]
        ins.append(SMEM)
        args.append(core)
    scratch = [
        pltpu.VMEM((width, 3 * width), BF),
        pltpu.VMEM((rows, 3 * width), BF),
        pltpu.VMEM((rows, width), F32),
        pltpu.SemaphoreType.DMA((len(bands),)),
    ]
    return call(kernel, "qkv_back", outs, ins, scratch, args, 6 * rows * width * width)


def unit_grads(normed_all, dy_all, w_up, w_down, flags, units, part):
    total, width = normed_all.shape
    n = w_up.shape[1]
    block = total // max(1, total // 736)
    if total % block:
        block = total
    steps = total // block
    dp = width // part

    def kernel(flag_ref, nb_ref, dy_ref, wu_ref, wd_ref, gu_ref, gd_ref, gdt):
        step = pl.program_id(0)
        nb = nb_ref[...]
        dy = dy_ref[...]

        def cols(a):
            picked = a[:, :part]
            for i in range(1, dp):
                picked = jnp.where(flag_ref[0] == i, a[:, i * part : (i + 1) * part], picked)
            return picked

        nb_cols, dy_cols = cols(nb), cols(dy)

        @pl.when(step == 0)
        def _():
            gu_ref[...] = jnp.zeros_like(gu_ref)
            gdt[...] = jnp.zeros_like(gdt)

        for at, k in spans(n, 512):
            act, slope = gelu_both(dot(nb, wu_ref[:, at : at + k]))
            inner = low16(dot_t(dy, wd_ref[at : at + k, :]) * slope)
            real = min(k, units - at)
            gu_ref[:, at : at + real] += t_dot(nb_cols, inner)[:, :real]
            gdt[:, at : at + k] += t_dot(dy_cols, low16(act))

        @pl.when(step == steps - 1)
        def _():
            gd_ref[...] = gdt[...].T[:units, :]

    args = [flags, normed_all, dy_all, w_up, w_down]
    return pl.pallas_call(
        kernel,
        grid=(steps,),
        in_specs=[
            SMEM,
            pl.BlockSpec((block, width), lambda i: (i, 0)),
            pl.BlockSpec((block, width), lambda i: (i, 0)),
            VMEM,
            VMEM,
        ],
        out_specs=(VMEM, VMEM),
        out_shape=(shape((part, units), F32), shape((units, part), F32)),
        scratch_shapes=[pltpu.VMEM((part, n), F32)],
        compiler_params=pltpu.CompilerParams(vmem_limit_bytes=60 * 2**20),
        cost_estimate=pl.CostEstimate(flops=int(6 * 1.4 * total * width * n), bytes_accessed=4 * total * width, transcendentals=0),
        name="unit_grads",
    )(*args)


def head_grads(flags, na_own, na_far, keep, got, mix_own, mix_far, ml_own, ml_far):
    rows, width = na_own.shape
    span3 = keep.shape[1] // 2
    span = span3 // 3
    part = width // 2

    def kernel(flag_ref, na0, na1, k0, k1, m0, m1, l0, l1, *rest):
        qkv_out, o_out, na, kk, mm, ml = rest[:4], rest[4:8], rest[8], rest[9], rest[10], rest[11]
        for a, b, c in ((na0, na1, na), (k0, k1, kk), (m0, m1, mm), (l0, l1, ml)):
            c[:rows] = a[...]
            c[rows:] = b[...]
        first = flag_ref[0] == 0
        lo, hi = na[:, :part], na[:, part:]
        by_row = (jnp.where(first, lo, hi), jnp.where(first, hi, lo))
        lo, hi = ml[:, :part], ml[:, part:]
        by_col = (jnp.where(first, lo, hi), jnp.where(first, hi, lo))
        for yr in (0, 1):
            for xr in (0, 1):
                out = qkv_out[yr * 2 + xr]
                out[...] = t_dot(by_row[yr], kk[:, xr * span3 : (xr + 1) * span3]).astype(out.dtype)
                out = o_out[yr * 2 + xr]
                out[...] = t_dot(mm[:, xr * span : (xr + 1) * span], by_col[yr]).astype(out.dtype)

    types = (F32, BF, BF, BF)
    outs = [shape((part, span3), t) for t in types] + [shape((span, part), t) for t in types]
    scratch = [
        pltpu.VMEM((2 * rows, width), BF),
        pltpu.VMEM((2 * rows, 2 * span3), BF),
        pltpu.VMEM((2 * rows, 2 * span), BF),
        pltpu.VMEM((2 * rows, width), BF),
    ]
    args = [flags, na_own, na_far, keep, got, mix_own, mix_far, ml_own, ml_far]
    flops = 8 * 2 * rows * width * width
    got = call(kernel, "head_grads", outs, [SMEM] + [VMEM] * 8, scratch, args, flops)
    return got[:4], got[4:]


def plane_scatter(own, beside, above, across):
    cut = half_cut(own.shape[0])
    rest = own.shape[0] - cut
    via_x = swap_x(jnp.concatenate((beside[:cut], across[:cut]), axis=0))
    via_y = swap_y(jnp.concatenate((above[cut:], across[cut:]), axis=0))
    up_top = swap_y(low16(up32(above[:cut]) + up32(via_x[cut:])))
    x_bottom = swap_x(low16(up32(beside[cut:]) + up32(via_y[rest:])))
    top = own[:cut] + up32(via_x[:cut]) + up32(up_top)
    bottom = own[cut:] + up32(via_y[:rest]) + up32(x_bottom)
    return jnp.concatenate((top, bottom), axis=0)


def gather_gains(shard, dp_idx, x_idx, core):
    if not two_rows():
        return lax.all_gather(shard, ("dp", "tensor"), axis=1, tiled=True)
    for index, swap in ((core, swap_core), (x_idx, swap_x), (dp_idx, swap_y)):
        other = swap(shard)
        shard = jnp.where(index == 0, jnp.concatenate((shard, other), axis=1), jnp.concatenate((other, shard), axis=1))
    return shard


def scatter_gains(sums, dp_idx, tensor_idx):
    if not two_rows():
        return lax.psum_scatter(sums, ("dp", "tensor"), scatter_dimension=1, tiled=True)
    for swap in (swap_core, swap_x, swap_y):
        sums = sums + swap(sums)
    part = sums.shape[1] // 8
    return lax.dynamic_slice_in_dim(sums, (dp_idx * 4 + tensor_idx) * part, part, 1)


def local(images, valid_len, query_weight, key_weight, value_weight, output_weight, up_weight, down_weight, norm_gains, cotangent):
    section = lax.axis_index("section")
    sections = lax.axis_size("section")
    dp_idx = lax.axis_index("dp")
    dp = lax.axis_size("dp")
    tensor_idx = lax.axis_index("tensor")
    x_idx, core = tensor_idx // 2, tensor_idx % 2
    per_dp, quarter, width = images.shape
    assert per_dp == 2 and lax.axis_size("tensor") == 4
    padded_quarter = (quarter + 7) // 8 * 8
    flags = jnp.stack((dp_idx, core)).astype(jnp.int32)
    core_flag = flags[1:]

    def pad_rows(a):
        return jnp.pad(a, ((0, padded_quarter - quarter), (0, 0)))

    def pick(a):
        own = lax.dynamic_index_in_dim(a, x_idx, 0, keepdims=False)
        give = lax.dynamic_index_in_dim(a, 1 - x_idx, 0, keepdims=False)
        got = up32(swap_x(pad_rows(low16(give))))
        return jnp.concatenate((pad_rows(own), got), axis=0)

    def unpick(rows):
        own, give = rows[:quarter], rows[padded_quarter:]
        got = up32(swap_x(low16(give))[:quarter])
        return jnp.where(x_idx == 0, jnp.stack((own, got)), jnp.stack((got, own)))

    first_rows = pick(images)
    rows = 2 * padded_quarter
    valid = lax.dynamic_index_in_dim(valid_len, x_idx, 0, keepdims=False)
    spot = jnp.arange(padded_quarter)
    live = [
        (spot < quarter) & ((2 * xx + cc) * quarter + spot < valid) for cc in (core, 1 - core) for xx in (x_idx, 1 - x_idx)
    ]
    bias = jnp.where(jnp.concatenate(live), 0.0, -1e30).astype(F32)[None, :]
    bias = jnp.broadcast_to(bias, (8, bias.shape[1]))
    gains = gather_gains(norm_gains[0], dp_idx, x_idx, core)
    gain_a, gain_b = gains[0:1], gains[1:2]

    def plane_pieces(w, after):
        if not two_rows():
            mine = lax.all_gather(w, "dp")
            other = swap_x(mine)
            mine_far, other_far = swap_core(mine), swap_core(other)
            split = lambda a: [a[i] for i in range(dp)]
            return [[split(mine), split(mine_far)], [split(other), split(other_far)]], other
        w = lax.optimization_barrier((w, after))[0] if after is not None else w
        cut = half_cut(w.shape[0])
        from_x = swap_x(w)
        from_y = swap_y(w)
        far = jnp.concatenate((swap_x(from_y[:cut]), swap_y(from_x[cut:])), axis=0)
        mine, other = [w, from_y], [from_x, far]
        pieces = [[mine, [swap_core(a) for a in mine]], [other, [swap_core(a) for a in other]]]
        return pieces, (from_x, from_y)

    span = query_weight.shape[2]
    units = up_weight.shape[2]
    wide = (units + 15) // 16 * 16

    def place_qkv(out, row, by_core, count):
        part = width // count
        for xr in (0, 1):
            for c in (0, 1):
                for i in range(count):
                    block = by_core(xr, c, i)
                    for k in range(3):
                        to = k * width + (2 * xr + c) * span
                        out[i * part : (i + 1) * part, to : to + span] = block[:, k * span : (k + 1) * span]

    def place_o(out, row, by_core, count):
        part = width // count
        for xr in (0, 1):
            for c in (0, 1):
                at = (2 * xr + c) * span
                for i in range(count):
                    out[at : at + span, i * part : (i + 1) * part] = by_core(xr, c, i)

    def place_up(out, row, by_core, count):
        part = width // count
        out[...] = jnp.zeros_like(out)
        for cr in (0, 1):
            for xr in (0, 1):
                at = (2 * cr + xr) * wide
                for i in range(count):
                    out[i * part : (i + 1) * part, at : at + units] = row(xr, cr, i)

    def place_down(out, row, by_core, count):
        part = width // count
        out[...] = jnp.zeros_like(out)
        for cr in (0, 1):
            for xr in (0, 1):
                at = (2 * cr + xr) * wide
                for i in range(count):
                    out[at : at + units, i * part : (i + 1) * part] = row(xr, cr, i)

    qkv_shard = jnp.concatenate((query_weight[0], key_weight[0], value_weight[0]), axis=1)
    qkv_pieces, token = plane_pieces(qkv_shard, first_rows)
    o_pieces, token = plane_pieces(output_weight[0], token)
    up_pieces, token = plane_pieces(up_weight[0], token)
    down_pieces, token = plane_pieces(down_weight[0], token)
    w_qkv = assemble("assemble_qkv", qkv_pieces, flags, place_qkv, (width, 3 * width))
    w_o = assemble("assemble_output", o_pieces, flags, place_o, (width, width))
    w_up = assemble("assemble_up", up_pieces, flags, place_up, (width, 4 * wide))
    w_down = assemble("assemble_down", down_pieces, flags, place_down, (4 * wide, width))

    x, got = first_rows, None
    for tick in range(sections):
        sel = (section == tick).astype(jnp.int32)[None]
        x, normed_a, kv = project_kv(sel, got, x, gain_a, w_qkv)
        kv_far = swap_core(kv)
        q = project_q(normed_a, w_qkv)
        if tick == 0:
            hidden, normed_b = layer_attention(q, kv, kv_far, bias, x, gain_b, w_o)
            out = layer_feed(hidden, normed_b, w_up, w_down)
        else:
            last = tick + 1 == sections
            got = layer_whole(last, q, kv, kv_far, bias, x, gain_b, w_o, w_up, w_down)
            out = got[0]
        if tick + 1 < sections:
            got = shift(out, 1)
    _, out, hidden, normed_b, slope, mix, lse = got
    acts = unpick(out)
    normed_b_all = row_gather(normed_b)

    dy, got = pick(cotangent), None
    for tick in range(sections):
        last = tick + 1 == sections
        sel = (section == sections - 1 - tick).astype(jnp.int32)[None]
        results = feed_back(last, sel, got, dy, slope, hidden, gain_b, w_up, w_down, w_o)
        if got is not None:
            dy, results = results[0], results[1:]
        hidden_grad, do = results[:2]
        dq, dkv, dkv_far = attention_back(q, kv, kv_far, do, mix, lse, bias)
        dkv_got = swap_core(dkv_far)
        back = qkv_back(last, dq, dkv, dkv_got, x, hidden_grad, gain_a, w_qkv, core_flag)
        if not last:
            got = shift(back[0], -1)
    dy_low, mix_low, gain_sum_b = results[2:]
    dx, _, keep, give, gain_sum_a = back
    grads = unpick(dx)

    dy_all = row_gather(dy_low)
    part = width // dp
    grad_up, grad_down = unit_grads(normed_b_all, dy_all, w_up[:, :wide], w_down[:wide], flags, units, part)

    def core_halves(a):
        lo = jnp.concatenate((a[:, :span], a[:, 2 * span : 3 * span]), axis=1)
        hi = jnp.concatenate((a[:, span : 2 * span], a[:, 3 * span :]), axis=1)
        return jnp.where(core == 0, lo, hi), jnp.where(core == 0, hi, lo)

    mix_keep, mix_give = core_halves(mix)
    na_far, ml_far = swap_core(normed_a), swap_core(mix_low)
    mix_got, got = swap_core(mix_give), swap_core(give)
    if two_rows():
        qkv_parts, o_parts = head_grads(flags, normed_a, na_far, keep, got, mix_keep, mix_got, mix_low, ml_far)
        grad_o = plane_scatter(*o_parts)
        grad_qkv = plane_scatter(*qkv_parts)
    else:
        both = lambda a, b: jnp.concatenate((a, b), axis=0)
        g = t_dot(both(normed_a, na_far), both(keep, got))
        g = g[:, : 3 * span] + up32(swap_x(low16(g[:, 3 * span :])))
        grad_qkv = up32(lax.psum_scatter(low16(g), "dp", scatter_dimension=0, tiled=True))
        g = t_dot(both(mix_keep, mix_got), both(mix_low, ml_far))
        g = g[:span] + up32(swap_x(low16(g[span:])))
        grad_o = up32(lax.psum_scatter(low16(g), "dp", scatter_dimension=1, tiled=True))
    gain_shard = scatter_gains(jnp.concatenate((gain_sum_a, gain_sum_b), axis=0), dp_idx, tensor_idx)

    return (
        acts[None],
        grads[None],
        grad_qkv[None, :, :span],
        grad_qkv[None, :, span : 2 * span],
        grad_qkv[None, :, 2 * span :],
        grad_o[None],
        grad_up[None],
        grad_down[None],
        gain_shard[None],
    )


def solution(mesh):
    return jax.shard_map(
        local,
        mesh=mesh,
        in_specs=(
            P("dp", "tensor", None),
            P("dp"),
            P("section", "dp", "tensor"),
            P("section", "dp", "tensor"),
            P("section", "dp", "tensor"),
            P("section", "tensor", "dp"),
            P("section", "dp", "tensor"),
            P("section", "tensor", "dp"),
            P("section", None, ("dp", "tensor")),
            P("dp", "tensor", None),
        ),
        out_specs=(
            P("section", "dp", "tensor", None),
            P("section", "dp", "tensor", None),
            P("section", "dp", "tensor"),
            P("section", "dp", "tensor"),
            P("section", "dp", "tensor"),
            P("section", "tensor", "dp"),
            P("section", "dp", "tensor"),
            P("section", "tensor", "dp"),
            P("section", None, ("dp", "tensor")),
        ),
        check_vma=False,
    )
```

```python
import jax
import jax.numpy as jnp
from jax import lax
from jax.experimental import pallas as pl
from jax.experimental.pallas import tpu as pltpu
from jax.sharding import PartitionSpec as P

HD = 72
EPS = 1e-06
SCALE = HD ** (-0.5)
LOG2E = 1.4426950408889634
BF = jnp.bfloat16
F32 = jnp.float32
WIN = 256
LANES = 128
COST = 0.1
ROOM = 28
K0 = 0.7978845608028654
K1 = 0.044715
VMEM = pl.BlockSpec(memory_space=pltpu.VMEM)
SMEM = pl.BlockSpec(memory_space=pltpu.SMEM)
ANY = pl.BlockSpec(memory_space=pl.ANY)


def swap_core(a):
    n = lax.axis_size("tensor")
    return lax.ppermute(a, "tensor", [(i, i ^ 1) for i in range(n)])


def swap_x(a):
    n = lax.axis_size("tensor")
    return lax.ppermute(a, "tensor", [(i, i ^ 2) for i in range(n)])


def swap_y(a):
    return lax.ppermute(a, "dp", [(0, 1), (1, 0)])


def swap_both(a):
    n = lax.axis_size("tensor")
    pairs = [(y * n + i, (1 - y) * n + (i ^ 2)) for y in (0, 1) for i in range(n)]
    return lax.ppermute(a, ("dp", "tensor"), pairs)


def shift(a, by):
    n = lax.axis_size("section")
    pairs = [(i, i + by) for i in range(n) if 0 <= i + by < n]
    return lax.ppermute(a, "section", pairs)


def two_rows():
    return lax.axis_size("dp") == 2


def half_cut(rows):
    return (rows // 2 + 15) // 16 * 16


def up32(a):
    return a.astype(F32)


def low16(a):
    return a.astype(BF)


def dot(a, b):
    return jnp.dot(a, b, preferred_element_type=F32)


def dot_t(a, b):
    return lax.dot_general(a, b, (((1,), (1,)), ((), ())), preferred_element_type=F32)


def t_dot(a, b):
    return lax.dot_general(a, b, (((0,), (0,)), ((), ())), preferred_element_type=F32)


def in_hbm(a):
    return pltpu.with_memory_space_constraint(a, pltpu.HBM)


def spans(total, size):
    return [(at, min(size, total - at)) for at in range(0, total, size)]


def norm_parts(values):
    centre = jnp.mean(values, axis=-1, keepdims=True)
    centred = values - centre
    spread = jnp.mean(centred * centred, axis=-1, keepdims=True)
    inverse = lax.rsqrt(spread + EPS)
    return centred * inverse, inverse


def norm_back(grad, unit, inverse, gain):
    e = grad * gain
    return inverse * (e - jnp.mean(e, axis=-1, keepdims=True) - unit * jnp.mean(e * unit, axis=-1, keepdims=True))


def span_copies(pieces, whole, sems, base):
    rows = pieces[0].shape[0]
    return [
        (pltpu.make_async_copy(piece, whole.at[i * rows : (i + 1) * rows], sems.at[base + i]), (i + 1) * rows)
        for i, piece in enumerate(pieces)
    ]


class Arrivals:
    def __init__(self, copies):
        self.left = list(copies)
        self.have = 0

    def start(self):
        for copy, _ in self.left:
            copy.start()

    def need(self, row):
        while self.left and self.have < row:
            copy, self.have = self.left.pop(0)
            copy.wait()

    def rest(self):
        self.need(1 << 30)


def gelu_one(u):
    return u * (0.5 + 0.5 * jnp.tanh(u * (K0 + (K0 * K1) * (u * u))))


def gelu_both(u):
    sq = u * u
    th = jnp.tanh(u * (K0 + (K0 * K1) * sq))
    half = 0.5 + 0.5 * th
    return u * half, half + (0.5 * u) * (1.0 - th * th) * (K0 + (3.0 * K1 * K0) * sq)


def head_window(h, width):
    tile = min(h * HD // LANES, width // LANES - WIN // LANES)
    off = h * HD - tile * LANES
    lane = lax.broadcasted_iota(jnp.int32, (1, WIN), 1)
    return slice(tile * LANES, tile * LANES + WIN), (lane >= off) & (lane < off + HD)


def shape(dims, dtype):
    return jax.ShapeDtypeStruct(dims, dtype)


def past(kernel, inputs, after):
    return lambda *refs: kernel(*refs[:inputs], *refs[inputs + len(after) :])


def call(kernel, name, outs, ins, scratch, args, flops, limit=60, after=()):
    moved = sum(a.size * a.dtype.itemsize for a in args) + sum(o.size * o.dtype.itemsize for o in outs)
    return pl.pallas_call(
        past(kernel, len(args), after),
        out_shape=tuple(outs),
        in_specs=[*ins, *[ANY] * len(after)],
        out_specs=tuple([VMEM] * len(outs)),
        scratch_shapes=scratch,
        compiler_params=pltpu.CompilerParams(vmem_limit_bytes=limit * 2**20),
        cost_estimate=pl.CostEstimate(flops=int(flops * COST), bytes_accessed=int(moved * COST), transcendentals=0),
        name=name,
    )(*args, *after)


def pack(flags, heads, up, down, pair, quarter):
    span, part = heads[0].shape
    units = up.shape[1]
    h = span // 2
    hu = (units + 31) // 32 * 16

    def kernel(flag_ref, *refs):
        pair_ref, out, out_x, mine_ref = refs[6:]
        got = pair_ref.shape[0]
        first = flag_ref[3] == 0
        one, two = pair_ref[:, 0, :], pair_ref[:, 1, :]
        mine_ref[...] = jnp.zeros_like(mine_ref)
        mine_ref[:got] = jnp.where(first, one, two)
        for i, ref in enumerate(refs[:4]):
            out[i * h : (i + 1) * h, :part] = ref[:h, :]
            out[i * h : (i + 1) * h, part:] = ref[h:, :]
        for i, ref in enumerate(refs[4:6]):
            base = 4 * h + i * hu
            rows = low16(up32(ref[...]).T)
            out[base : base + hu, :part] = rows[:hu]
            out[base : base + units - hu, part:] = rows[hu:]
            out[base + units - hu : base + hu, part:] = jnp.zeros((2 * hu - units, part), BF)
        if ride:
            out_x[:total] = out[...]
            out_x[total : total + quarter] = low16(jnp.concatenate((jnp.where(first, two, one), jnp.zeros((spare, width), F32)), axis=0))

    total = 4 * h + 2 * hu
    spare = quarter - pair.shape[0]
    width = pair.shape[2]
    ride = 2 * part == width
    outs = [shape((total, 2 * part), BF), shape((total + quarter if ride else 16, 2 * part), BF), shape((quarter, width), F32)]
    got = call(kernel, "pack", outs, [SMEM] + [VMEM] * 7, [], [flags, *heads, up, down, pair], 0, 30)
    return *got, (0, 4 * h, 4 * h + hu), hu


def put_together(name, pieces, flags, groups, h, after=()):
    count = len(pieces)
    parts = [(i, *p) for i, piece in enumerate(pieces) for p in piece]
    part = parts[0][1].shape[1] // 2
    width = part * count

    def kernel(flag_ref, *refs):
        out, held, sem = refs[len(parts) :]
        copies, at = [], [0] * count
        for j, (ref, (i, _, row, rows)) in enumerate(zip(refs, parts)):
            copies.append(pltpu.make_async_copy(ref.at[row : row + rows], held.at[i, at[i] : at[i] + rows], sem.at[j]))
            at[i] += rows
        for copy in copies:
            copy.start()
        wait_all(copies)
        first = flag_ref[0] == 0
        for i in range(count):
            for g in range(groups):
                rows = slice(g * h, (g + 1) * h)
                piece = jnp.where(first, held[i, rows], held[1 - i, rows]) if count == 2 else held[i, rows]
                out[g, :h, i * part : (i + 1) * part] = piece[:, :part]
                out[g, h:, i * part : (i + 1) * part] = piece[:, part:]

    scratch = [pltpu.VMEM((count, groups * h, 2 * part), BF), pltpu.SemaphoreType.DMA((len(parts),))]
    outs = [shape((groups, 2 * h, width), BF)]
    args = [flags, *[in_hbm(p[1]) for p in parts]]
    return call(kernel, name, outs, [SMEM] + [ANY] * len(parts), scratch, args, 0, 24, after)[0]


def head_copies(pieces, core, kinds, whole, sems, base):
    span, width = pieces[0].shape[1], pieces[0].shape[2]
    out = []
    for n, kind in enumerate(kinds):
        group = []
        for i, piece in enumerate(pieces):
            c = core if i < 2 else 1 - core
            at = pl.multiple_of(n * width + (2 * (i % 2) + c) * span, span)
            sem = sems.at[base + 4 * n + i]
            group.append(pltpu.make_async_copy(piece.at[kind], whole.at[pl.ds(at, span)], sem))
        out.append(group)
    return out


def wait_all(copies):
    for copy in copies:
        copy.wait()


def attend(q, kv, bias, mix, rest, lse_ref):
    rows, width = q.shape
    lane = lax.broadcasted_iota(jnp.int32, (1, LANES), 1)
    for h in range(width // HD):
        win, live = head_window(h, width)
        keys = jnp.where(live, kv[:, win], jnp.zeros((), BF))
        vals = kv[:, width + win.start : width + win.stop]
        s = dot_t(q[:, win], keys) * (SCALE * LOG2E) + bias
        top = jnp.max(s, axis=-1, keepdims=True)
        p = jnp.exp2(s - top)
        total = jnp.sum(p, axis=-1, keepdims=True)
        o = dot(low16(p), vals) * (1.0 / total)
        o_low = low16(o)
        mix[:, win] = jnp.where(live, o_low, mix[:, win])
        if rest is not None:
            rest[:, win] = jnp.where(live, low16(o - up32(o_low)), rest[:, win])
            lse_ref[...] = jnp.where(lane == h, top + jnp.log2(total), lse_ref[...])


def feed_up(normed, pieces, after=()):
    rows, width = normed.shape
    units = sum(piece.shape[0] for piece in pieces)
    n = len(pieces)

    def kernel(nb_ref, *refs):
        act, w, sem = refs[n:]
        arrivals = Arrivals(span_copies(refs[:n], w, sem, 0))
        arrivals.start()
        for at, k in spans(units, 512):
            arrivals.need(at + k)
            act[:, at : at + k] = low16(gelu_one(dot_t(nb_ref[...], w[at : at + k, :])))

    scratch = [pltpu.VMEM((units, width), BF), pltpu.SemaphoreType.DMA((n,))]
    outs = [shape((rows, units), BF)]
    return call(kernel, "feed_up", outs, [VMEM] + [ANY] * n, scratch, [normed, *pieces], 2 * rows * width * units, 30, after)[0]


def feed_down(base, act, pieces, out_type, after=()):
    rows, width = base.shape
    units = act.shape[1]
    n = len(pieces)

    def kernel(base_ref, act_ref, *refs):
        out, w, sem = refs[n:]
        arrivals = Arrivals(span_copies(refs[:n], w, sem, 0))
        arrivals.start()
        arrivals.rest()
        for at, k in spans(width, 256):
            out[:, at : at + k] = (base_ref[:, at : at + k] + dot(act_ref[...], w[:, at : at + k])).astype(out.dtype)

    scratch = [pltpu.VMEM((units, width), BF), pltpu.SemaphoreType.DMA((n,))]
    outs = [shape((rows, width), out_type)]
    args = [base, act, *pieces]
    return call(kernel, "feed_down", outs, [VMEM, VMEM] + [ANY] * n, scratch, args, 2 * rows * width * units, 30, after)[0]


def project(nall, w, q, kv):
    rows, width = q.shape
    for at, n in spans(width, 512):
        q[:, at : at + n] = low16(dot_t(nall[:rows], w[width + at : width + at + n, :]))
    for at, n in spans(2 * width, 512):
        kv[:, at : at + n] = low16(dot_t(nall[...], w[2 * width + at : 2 * width + at + n, :]))


def layer_first(flags, rows32, far, bias, gains, heads):
    rows, width = rows32.shape

    def kernel(flag_ref, bias_ref, gain_ref, x_ref, far_ref, *refs):
        heads_r, hid_ref, nb_ref, w, nall, q, kv, mix, sem = refs[:4], *refs[4:]
        groups = head_copies(heads_r, flag_ref[1], (3, 0, 1, 2), w, sem, 0)
        for group in groups:
            for copy in group:
                copy.start()
        gain_a, gain_b = gain_ref[0:1, :], gain_ref[1:2, :]
        nall[:rows] = low16(norm_parts(x_ref[...])[0] * gain_a)
        nall[rows:] = low16(norm_parts(up32(far_ref[...]))[0] * gain_a)
        for group in groups:
            wait_all(group)
        project(nall, w, q, kv)
        mix[...] = jnp.zeros_like(mix)
        attend(q, kv, bias_ref[0:1, :], mix, None, None)
        hidden = x_ref[...] + dot(mix[...], w[:width, :])
        hid_ref[...] = hidden
        nb_ref[...] = low16(norm_parts(hidden)[0] * gain_b)

    scratch = [
        pltpu.VMEM((4 * width, width), BF),
        pltpu.VMEM((2 * rows, width), BF),
        pltpu.VMEM((rows, width), BF),
        pltpu.VMEM((2 * rows, 2 * width), BF),
        pltpu.VMEM((rows, width), BF),
        pltpu.SemaphoreType.DMA((16,)),
    ]
    outs = [shape((rows, width), F32), shape((rows, width), BF)]
    ins = [SMEM] + [VMEM] * 4 + [ANY] * 4
    flops = 16 * rows * 2 * rows * WIN * 4 + 12 * rows * width * width
    return call(kernel, "layer_first", outs, ins, scratch, [flags, bias, gains, rows32, far, *heads], flops, 44)


def settle(flags, after, heads, ups, downs):
    kinds, span, width = heads[0].shape
    units = 4 * ups[0].shape[0]

    def kernel(flag_ref, *refs):
        wh, wu, wd, token, sem = refs[13:]
        copies = sum(head_copies(refs[:4], flag_ref[1], (3, 0, 1, 2), wh, sem, 0), [])
        copies += [copy for copy, _ in span_copies(refs[4:8], wu, sem, 16) + span_copies(refs[8:12], wd, sem, 20)]
        for copy in copies:
            copy.start()
        token[...] = jnp.zeros_like(token)
        wait_all(copies)

    pieces = [pltpu.with_memory_space_constraint(a, pltpu.HBM) for a in (*heads, *ups, *downs)]
    wh, wu, wd, token = pl.pallas_call(
        kernel,
        out_shape=(
            pltpu.VMEM((kinds * 4 * span, width), BF),
            pltpu.VMEM((units, width), BF),
            pltpu.VMEM((units, width), BF),
            shape((8, LANES), F32),
        ),
        in_specs=[SMEM] + [ANY] * 13,
        out_specs=(ANY, ANY, ANY, VMEM),
        scratch_shapes=[pltpu.SemaphoreType.DMA((24,))],
        compiler_params=pltpu.CompilerParams(vmem_limit_bytes=ROOM * 2**20),
        cost_estimate=pl.CostEstimate(flops=0, bytes_accessed=int(60 * COST * 2**20), transcendentals=0),
        name="settle",
    )(flags, *pieces, after)
    return [pltpu.with_memory_space_constraint(a, pltpu.VMEM) for a in (wh, wu, wd)], token


def feed(normed, hidden, w_up, w_down, act, slope_out, out):
    for at, n in spans(w_up.shape[0], 512):
        u = dot_t(normed, w_up[at : at + n, :])
        if slope_out is None:
            act[:, at : at + n] = low16(gelu_one(u))
        else:
            a, slope = gelu_both(u)
            act[:, at : at + n] = low16(a)
            slope_out[:, at : at + n] = low16(slope)
    for at, n in spans(w_down.shape[1], 256):
        out[:, at : at + n] = (hidden[:, at : at + n] + dot(act[...], w_down[:, at : at + n])).astype(out.dtype)


def layer_mid(flags, own, far, bias, gains, w_heads, w_up, w_down, after=()):
    rows, width = own.shape
    units = w_up.shape[0]

    def kernel(bias_ref, gain_ref, wh, wu, wd, own_ref, far_ref, out_ref, x_ref, q, kv, mix, hid_ref, nall, act):
        gain_a, gain_b = gain_ref[0:1, :], gain_ref[1:2, :]
        x_ref[...] = up32(own_ref[...])
        nall[:rows] = low16(norm_parts(x_ref[...])[0] * gain_a)
        nall[rows:] = low16(norm_parts(up32(far_ref[...]))[0] * gain_a)
        project(nall, wh, q, kv)
        mix[...] = jnp.zeros_like(mix)
        attend(q, kv, bias_ref[0:1, :], mix, None, None)
        hidden = x_ref[...] + dot(mix[...], wh[:width, :])
        hid_ref[...] = hidden
        feed(low16(norm_parts(hidden)[0] * gain_b), hid_ref, wu, wd, act, None, out_ref)

    scratch = [
        pltpu.VMEM((rows, width), F32),
        pltpu.VMEM((rows, width), BF),
        pltpu.VMEM((2 * rows, 2 * width), BF),
        pltpu.VMEM((rows, width), BF),
        pltpu.VMEM((rows, width), F32),
        pltpu.VMEM((2 * rows, width), BF),
        pltpu.VMEM((rows, units), BF),
    ]
    flops = 16 * rows * 2 * rows * WIN * 4 + 12 * rows * width * width + 4 * rows * width * units
    args = [bias, gains, w_heads, w_up, w_down, own, far]
    return call(kernel, "layer_mid", [shape((rows, width), BF)], [VMEM] * 7, scratch, args, flops, ROOM, after)[0]


def last_project(flags, sources, gains, w_heads):
    rows, width = sources[0].shape
    sections = len(sources) // 2

    def kernel(flag_ref, gain_ref, wh, *refs):
        src, refs = refs[: len(sources)], refs[len(sources) :]
        x_ref, na_ref, q, kv, nall, sem = refs

        def load(i, go):
            own, far = src[2 * i], src[2 * i + 1]
            near = pltpu.make_async_copy(own, x_ref if own.dtype == F32 else na_ref, sem.at[0])
            other = pltpu.make_async_copy(far, nall.at[rows:], sem.at[1])
            for copy in (near, other):
                if go:
                    copy.start()
                else:
                    copy.wait()
            if not go and own.dtype != F32:
                x_ref[...] = up32(na_ref[...])

        for go in (True, False):
            for i in range(sections):
                pl.when(flag_ref[2] == i)(lambda i=i, go=go: load(i, go))
        gain_a = gain_ref[0:1, :]
        normed = low16(norm_parts(x_ref[...])[0] * gain_a)
        na_ref[...] = normed
        nall[:rows] = normed
        nall[rows:] = low16(norm_parts(up32(nall[rows:]))[0] * gain_a)
        project(nall, wh, q, kv)

    row32, row16 = shape((rows, width), F32), shape((rows, width), BF)
    outs = [row32, row16, row16, shape((2 * rows, 2 * width), BF)]
    scratch = [pltpu.VMEM((2 * rows, width), BF), pltpu.SemaphoreType.DMA((2,))]
    ins = [SMEM, VMEM, VMEM] + [ANY] * len(sources)
    args = [flags, gains, w_heads, *[in_hbm(a) for a in sources]]
    return call(kernel, "last_project", outs, ins, scratch, args, 10 * rows * width * width, 12)


def last_attention(q, kv, bias, x, gains, w_heads, after=()):
    rows, width = q.shape

    def kernel(q_ref, kv_ref, bias_ref, x_ref, gain_ref, wh, mix, rest_ref, lse_ref, hid_ref, nb_ref):
        mix[...] = jnp.zeros_like(mix)
        lse_ref[...] = jnp.zeros_like(lse_ref)
        rest_ref[...] = jnp.zeros_like(rest_ref)
        attend(q_ref, kv_ref, bias_ref[0:1, :], mix, rest_ref, lse_ref)
        hidden = x_ref[...] + dot(mix[...], wh[:width, :])
        hid_ref[...] = hidden
        nb_ref[...] = low16(norm_parts(hidden)[0] * gain_ref[1:2, :])

    row32, row16 = shape((rows, width), F32), shape((rows, width), BF)
    outs = [row16, row16, shape((rows, LANES), F32), row32, row16]
    flops = 16 * rows * 2 * rows * WIN * 4 + 2 * rows * width * width
    return call(kernel, "last_attention", outs, [VMEM] * 6, [], [q, kv, bias, x, gains, w_heads], flops, 18, after)


def feed_turn(hidden, normed, dy_own, dy_got, gains, w_heads, w_up, w_down):
    rows, width = hidden.shape
    units = w_up.shape[0]

    half = dy_own.shape[0]

    def kernel(hid_ref, nb_ref, own_ref, got_ref, gain_ref, wh, wu, wd, out_ref, slope_ref, hg_ref, do_ref, dy_ref, act, nbg):
        dy_ref[:half] = own_ref[...]
        dy_ref[half:] = up32(got_ref[...])
        feed(nb_ref[...], hid_ref, wu, wd, act, slope_ref, out_ref)
        feed_grads(low16(dy_ref[...]), slope_ref, wu, wd, act, nbg)
        unit, inverse = norm_parts(hid_ref[...])
        hidden_grad = dy_ref[...] + norm_back(nbg[...], unit, inverse, gain_ref[1:2, :])
        hg_ref[...] = hidden_grad
        do_ref[...] = low16(dot_t(low16(hidden_grad), wh[:width, :]))

    row32 = shape((rows, width), F32)
    outs = [row32, shape((rows, units), BF), row32, shape((rows, width), BF), row32]
    scratch = [pltpu.VMEM((rows, units), BF), pltpu.VMEM((rows, width), F32)]
    flops = 8 * rows * width * units
    args = [hidden, normed, dy_own, dy_got, gains, w_heads, w_up, w_down]
    return call(kernel, "feed_turn", outs, [VMEM] * 8, scratch, args, flops, 22)


def feed_grads(low, slope_ref, w_up, w_down, inner, out):
    for at, n in spans(w_up.shape[0], 512):
        inner[:, at : at + n] = low16(dot_t(low, w_down[at : at + n, :]) * up32(slope_ref[:, at : at + n]))
    for at, n in spans(w_up.shape[1], 256):
        out[:, at : at + n] = dot(inner[...], w_up[:, at : at + n])


def feed_back(mode, flags, sources, slope, hidden, gains, w_heads, w_up, w_down, after=()):
    last = mode == "last"
    rows, width = hidden.shape
    units = w_up.shape[0]

    def kernel(flag_ref, gain_ref, hid_ref, slope_ref, wh, wu, wd, *refs):
        src, refs = refs[: len(sources)], refs[len(sources) :]
        hg_ref, do_ref, refs = refs[0], refs[1], refs[2:]
        if last:
            ml_ref, gs_ref, ig, nbg, dy_ref, low, sem = refs

            def load(a, go):
                copy = pltpu.make_async_copy(a, dy_ref if a.dtype == F32 else low, sem.at[0])
                if go:
                    copy.start()
                    return
                copy.wait()
                if a.dtype == F32:
                    low[...] = low16(dy_ref[...])
                else:
                    dy_ref[...] = up32(low[...])

            for go in (True, False):
                for i, a in enumerate(src):
                    pl.when(flag_ref[2] == len(src) - 1 - i)(lambda a=a, go=go: load(a, go))
        else:
            ig, nbg, dy_ref, low = refs
            dy_ref[...] = src[0][...].astype(F32)
            low[...] = low16(src[0][...])
        feed_grads(low[...], slope_ref, wu, wd, ig, nbg)
        unit, inverse = norm_parts(hid_ref[...])
        grad = nbg[...]
        if last:
            gs_ref[...] = jnp.sum(grad * unit, axis=0, keepdims=True)
        hidden_grad = dy_ref[...] + norm_back(grad, unit, inverse, gain_ref[1:2, :])
        hg_ref[...] = hidden_grad
        mix_low = low16(hidden_grad)
        if last:
            ml_ref[...] = mix_low
        do_ref[...] = low16(dot_t(mix_low, wh[:width, :]))

    sources = [in_hbm(a) if last else a for a in sources]
    args = [flags, gains, hidden, slope, w_heads, w_up, w_down, *sources]
    outs = [shape((rows, width), F32), shape((rows, width), BF)]
    if last:
        outs += [shape((rows, width), BF), shape((1, width), F32)]
    scratch = [
        pltpu.VMEM((rows, units), BF),
        pltpu.VMEM((rows, width), F32),
        pltpu.VMEM((rows, width), F32),
        pltpu.VMEM((rows, width), BF),
    ]
    if last:
        scratch.append(pltpu.SemaphoreType.DMA((1,)))
    ins = [SMEM] + [VMEM] * 6 + [ANY if last else VMEM] * len(sources)
    flops = 4 * rows * width * units + 2 * rows * width * width
    return call(kernel, "feed_back_" + mode, outs, ins, scratch, args, flops, 13, after)


def attention_back(q, kv_all, do, mix, mix_rest, lse, bias, after=()):
    rows, width = q.shape
    keys_n = 2 * rows

    def kernel(q_ref, kv, do_ref, o_ref, rest_ref, lse_ref, bias_ref, dq_ref, dkv_own, dkv_far, qt, dt, dkt, dvt):
        bias_row = bias_ref[0:1, :]
        qt[...] = q_ref[...].T
        dt[...] = do_ref[...].T
        dq_ref[...] = jnp.zeros_like(dq_ref)
        zero = jnp.zeros((), BF)
        parts = ([], [])
        for h in range(width // HD):
            win, live = head_window(h, width)
            keys = jnp.where(live, kv[:, win], zero)
            vals = jnp.where(live, kv[:, width + win.start : width + win.stop], zero)
            d_out = do_ref[:, win]
            whole = up32(o_ref[:, win]) + up32(rest_ref[:, win])
            row_dot = jnp.sum(jnp.where(live, up32(d_out) * whole, 0.0), axis=-1, keepdims=True)
            s = dot_t(q_ref[:, win], keys) * (SCALE * LOG2E) + bias_row
            p = jnp.exp2(s - lse_ref[:, h : h + 1])
            ds = low16(p * (dot_t(d_out, vals) - row_dot))
            dq = dot(ds, keys) * SCALE
            dq_ref[:, win] = jnp.where(live, low16(dq), dq_ref[:, win])
            row = h % 2 * HD
            pair = slice((h - h % 2) * HD, (h - h % 2 + 2) * HD)
            parts[0].append(low16(dot(qt[pair, :][row : row + HD], ds) * SCALE))
            parts[1].append(low16(dot(dt[pair, :][row : row + HD], low16(p))))
            if h % 2:
                dkt[pair, :] = jnp.concatenate(parts[0], axis=0)
                dvt[pair, :] = jnp.concatenate(parts[1], axis=0)
                parts = ([], [])
        dk = dkt[...].T
        dv = dvt[...].T
        dkv_own[:, :width] = dk[:rows]
        dkv_own[:, width:] = dv[:rows]
        dkv_far[:, :width] = dk[rows:]
        dkv_far[:, width:] = dv[rows:]

    outs = [shape((rows, width), BF), shape((rows, 2 * width), BF), shape((rows, 2 * width), BF)]
    scratch = [
        pltpu.VMEM((width, rows), BF),
        pltpu.VMEM((width, rows), BF),
        pltpu.VMEM((width, keys_n), BF),
        pltpu.VMEM((width, keys_n), BF),
    ]
    flops = 16 * rows * keys_n * WIN * 10
    return call(kernel, "attention_back", outs, [VMEM] * 7, scratch, [q, kv_all, do, mix, mix_rest, lse, bias], flops, 17, after)


def qkv_back(full, flags, dq, own, got, x, hidden_grad, gains, w_heads, after=()):
    rows, width = dq.shape
    span = width // 4

    def kernel(flag_ref, gain_ref, dq_ref, own_ref, got_ref, x_ref, hg_ref, w, *refs):
        if full:
            dx_ref, low_ref, keep_ref, give_ref, gs_ref, grads, nag = refs
        else:
            low_ref, grads, nag = refs
        grads[:, :width] = dq_ref[...]
        grads[:, width:] = low16(up32(own_ref[...]) + up32(got_ref[...]))
        if full:
            mine = flag_ref[1] == 0
            for i in range(3):
                for xr in (0, 1):
                    at = i * width + 2 * xr * span
                    lo = grads[:, at : at + span]
                    hi = grads[:, at + span : at + 2 * span]
                    to = xr * 3 * span + i * span
                    keep_ref[:, to : to + span] = jnp.where(mine, lo, hi)
                    give_ref[:, to : to + span] = jnp.where(mine, hi, lo)
        for at, n in spans(width, 256):
            nag[:, at : at + n] = dot(grads[...], w[width:, at : at + n])
        unit, inverse = norm_parts(x_ref[...])
        grad = nag[...]
        if full:
            gs_ref[...] = jnp.sum(grad * unit, axis=0, keepdims=True)
        dx = hg_ref[...] + norm_back(grad, unit, inverse, gain_ref[0:1, :])
        low_ref[...] = low16(dx)
        if full:
            dx_ref[...] = dx

    outs = [shape((rows, width), BF)]
    if full:
        outs = [shape((rows, width), F32)] + outs
        outs += [shape((rows, 6 * span), BF), shape((rows, 6 * span), BF), shape((1, width), F32)]
    scratch = [pltpu.VMEM((rows, 3 * width), BF), pltpu.VMEM((rows, width), F32)]
    args = [flags, gains, dq, own, got, x, hidden_grad, w_heads]
    return call(kernel, "qkv_back", outs, [SMEM] + [VMEM] * 7, scratch, args, 6 * rows * width * width, 11, after)


def halves_of(total):
    steps = max(1, total // 736)
    return steps, total // steps


def halves_specs(steps, block, cols):
    return [
        pl.BlockSpec((block, cols), lambda i: (jnp.minimum(i, steps - 1), 0)),
        pl.BlockSpec((block, cols), lambda i: (jnp.maximum(i, steps) - steps, 0)),
    ]


def unit_forward(normed_four, normed_far, w_up, after=()):
    total, width = normed_four.shape
    n = w_up.shape[0]
    half, block = halves_of(total)

    def kernel(a_ref, b_ref, wu_ref, act_ref, slope_ref):
        nb = jnp.where(pl.program_id(0) < half, a_ref[...], b_ref[...])
        for at, k in spans(n, 512):
            act, slope = gelu_both(dot_t(nb, wu_ref[at : at + k, :]))
            act_ref[:, at : at + k] = low16(act)
            slope_ref[:, at : at + k] = low16(slope)

    by_rows = pl.BlockSpec((block, n), lambda i: (i, 0))
    return pl.pallas_call(
        past(kernel, 3, after),
        grid=(2 * half,),
        in_specs=[*halves_specs(half, block, width), VMEM, *[ANY] * len(after)],
        out_specs=(by_rows, by_rows),
        out_shape=(shape((2 * total, n), BF), shape((2 * total, n), BF)),
        compiler_params=pltpu.CompilerParams(vmem_limit_bytes=26 * 2**20),
        cost_estimate=pl.CostEstimate(flops=int(5.6 * COST * total * width * n), bytes_accessed=int(12 * COST * total * width), transcendentals=0),
        name="unit_forward",
    )(normed_four, normed_far, w_up, *after)


def pick_cols(a, which, part):
    picked = a[:, :part]
    for i in range(1, a.shape[1] // part):
        picked = jnp.where(which == i, a[:, i * part : (i + 1) * part], picked)
    return picked


def up_grads(normed_four, normed_far, dy_four, dy_far, slope_all, w_down, flags, units, part, after=()):
    total, width = normed_four.shape
    n = w_down.shape[0]
    half, block = halves_of(total)

    def kernel(flag_ref, na_ref, nb_ref, da_ref, db_ref, slope_ref, wd_ref, gu_ref):
        step = pl.program_id(0)
        dy = jnp.where(step < half, da_ref[...], db_ref[...])
        turned = pick_cols(jnp.where(step < half, na_ref[...], nb_ref[...]), flag_ref[0], part).T

        @pl.when(step == 0)
        def _():
            gu_ref[...] = jnp.zeros_like(gu_ref)

        for at, k in spans(n, 512):
            inner = low16(dot_t(dy, wd_ref[at : at + k, :]) * up32(slope_ref[:, at : at + k]))
            real = min(k, units - at)
            gu_ref[:, at : at + real] += dot(turned, inner)[:, :real]

    by_rows = pl.BlockSpec((block, n), lambda i: (i, 0))
    return pl.pallas_call(
        past(kernel, 7, after),
        grid=(2 * half,),
        in_specs=[
            SMEM, *halves_specs(half, block, width), *halves_specs(half, block, width), by_rows, VMEM, *[ANY] * len(after)
        ],
        out_specs=VMEM,
        out_shape=shape((part, units), F32),
        compiler_params=pltpu.CompilerParams(vmem_limit_bytes=48 * 2**20),
        cost_estimate=pl.CostEstimate(flops=int(8.4 * COST * total * width * n), bytes_accessed=int(12 * COST * total * width), transcendentals=0),
        name="up_grads",
    )(flags, normed_four, normed_far, dy_four, dy_far, slope_all, w_down, *after)


def down_grads(dy_four, dy_far, act_all, flags, units, part, after=()):
    total, width = dy_four.shape
    n = act_all.shape[1]
    half, block = halves_of(total)

    def kernel(flag_ref, da_ref, db_ref, act_ref, gdt):
        step = pl.program_id(0)
        turned = pick_cols(jnp.where(step < half, da_ref[...], db_ref[...]), flag_ref[0], part).T

        @pl.when(step == 0)
        def _():
            gdt[...] = jnp.zeros_like(gdt)

        for at, k in spans(n, 512):
            real = min(k, units - at)
            gdt[:, at : at + real] += dot(turned, act_ref[:, at : at + k])[:, :real]

    return pl.pallas_call(
        past(kernel, 4, after),
        grid=(2 * half,),
        in_specs=[
            SMEM, *halves_specs(half, block, width), pl.BlockSpec((block, n), lambda i: (i, 0)), *[ANY] * len(after)
        ],
        out_specs=VMEM,
        out_shape=shape((part, units), F32),
        compiler_params=pltpu.CompilerParams(vmem_limit_bytes=44 * 2**20),
        cost_estimate=pl.CostEstimate(flops=int(4.2 * COST * total * width * n), bytes_accessed=int(8 * COST * total * width), transcendentals=0),
        name="down_grads",
    )(flags, dy_four, dy_far, act_all, *after)


def join(name, pieces, after=()):
    n = len(pieces)

    def kernel(*refs):
        out, at = refs[n], 0
        for ref in refs[:n]:
            out[at : at + ref.shape[0]] = ref[...]
            at += ref.shape[0]

    rows = sum(a.shape[0] for a in pieces)
    return call(kernel, name, [shape((rows, pieces[0].shape[1]), BF)], [VMEM] * n, [], list(pieces), 0, 16, after)[0]


def plane_blocks(name, flags, left, right, after=()):
    rows = left[0].shape[0]
    part = right[0].shape[1] // 2
    span = left[0].shape[1] // 2
    h = span // 2
    cut = half_cut(h)

    def kernel(flag_ref, l0, l1, r0, r1, *refs):
        outs, ls, rs = refs[:5], refs[5], refs[6]
        for a, b, c in ((l0, l1, ls), (r0, r1, rs)):
            c[:rows] = a[...]
            c[rows:] = b[...]
        first = flag_ref[0] == 0
        lo, hi = rs[:, :part], rs[:, part:]
        shares = (jnp.where(first, lo, hi), jnp.where(first, hi, lo))
        for yr in (0, 1):
            for xr in (0, 1):
                got = t_dot(ls[:, xr * span : (xr + 1) * span], shares[yr])
                if yr == 0 and xr == 0:
                    outs[0][...] = got
                    continue
                for side in (0, 1):
                    cols = slice(side * part, (side + 1) * part)
                    top, bottom = low16(got[side * h : side * h + cut]), low16(got[side * h + cut : (side + 1) * h])
                    if xr and yr:
                        outs[1][cut:, cols] = top
                        outs[2][h - cut :, cols] = bottom
                    elif xr:
                        outs[1][:cut, cols] = top
                        outs[3][:, cols] = bottom
                    else:
                        outs[2][: h - cut, cols] = bottom
                        outs[4][:, cols] = top

    outs = [shape((span, part), F32)]
    outs += [shape((n, 2 * part), BF) for n in (2 * cut, 2 * (h - cut), h - cut, cut)]
    scratch = [pltpu.VMEM((2 * rows, 2 * span), BF), pltpu.VMEM((2 * rows, 2 * part), BF)]
    args = [flags, *left, *right]
    flops = 16 * rows * span * part
    return call(kernel, name, outs, [SMEM] + [VMEM] * 4, scratch, args, flops, 40, after)


def scatter_middle(name, beside, above, via_x, via_y, after=()):
    rest, double = beside.shape
    cut = above.shape[0]

    def kernel(beside_ref, above_ref, vx, vy, to_y, to_x):
        to_y[...] = low16(up32(above_ref[...]) + up32(vx[cut:, :]))
        to_x[...] = low16(up32(beside_ref[...]) + up32(vy[rest:, :]))

    outs = [shape((cut, double), BF), shape((rest, double), BF)]
    to_y, to_x = call(kernel, name, outs, [VMEM] * 4, [], [beside, above, via_x, via_y], 0, 16, after)
    return swap_y(to_y), swap_x(to_x)


def scatter_end(name, own, via_x, via_y, over_y, over_x, count, after=()):
    span, part = own.shape
    h = span // 2
    cut = half_cut(h)
    rest = h - cut
    each = span // count

    def kernel(own_ref, vx, vy, oy, ox, *refs):
        outs, total = refs[:count], refs[count]
        for side in (0, 1):
            cols = slice(side * part, (side + 1) * part)
            base = side * h
            total[base : base + cut] = own_ref[base : base + cut, :] + up32(vx[:cut, cols]) + up32(oy[:, cols])
            total[base + cut : base + h] = own_ref[base + cut : base + h, :] + up32(vy[:rest, cols]) + up32(ox[:, cols])
        for i, out in enumerate(outs):
            out[...] = total[i * each : (i + 1) * each]

    outs = [shape((each, part), F32)] * count
    scratch = [pltpu.VMEM((span, part), F32)]
    return call(kernel, name, outs, [VMEM] * 5, scratch, [own, via_x, via_y, over_y, over_x], 0, 24, after)


def gather_gains(shard, moves, dp_idx, x_idx, core):
    if not two_rows():
        return lax.all_gather(shard, ("dp", "tensor"), axis=1, tiled=True)
    beside, above, across = moves

    def pair(index, a, b):
        return jnp.where(index == 0, jnp.concatenate((a, b), axis=1), jnp.concatenate((b, a), axis=1))

    four = jnp.concatenate((shard, beside, above, across), axis=1)
    other = swap_core(four)
    n = shard.shape[1]
    by_core = [pair(core, four[:, i * n : (i + 1) * n], other[:, i * n : (i + 1) * n]) for i in range(4)]
    return pair(dp_idx, pair(x_idx, *by_core[:2]), pair(x_idx, *by_core[2:]))


def ties(*arrays):
    return list(lax.optimization_barrier(arrays))


def tie(a, *others):
    return ties(a, *others)[0]


def local(images, valid_len, query_weight, key_weight, value_weight, output_weight, up_weight, down_weight, norm_gains, cotangent):
    section = lax.axis_index("section")
    sections = lax.axis_size("section")
    dp_idx = lax.axis_index("dp")
    dp = lax.axis_size("dp")
    tensor_idx = lax.axis_index("tensor")
    x_idx, core = tensor_idx // 2, tensor_idx % 2
    per_dp, quarter, width = images.shape
    assert per_dp == 2 and lax.axis_size("tensor") == 4
    padded_quarter = (quarter + 7) // 8 * 8
    flags = jnp.stack((dp_idx, core, section, x_idx)).astype(jnp.int32)

    def pad_rows(a):
        return jnp.pad(a, ((0, padded_quarter - quarter), (0, 0)))

    def mine(a):
        return pad_rows(lax.dynamic_index_in_dim(a, x_idx, 0, keepdims=False))

    def theirs(a):
        return pad_rows(low16(lax.dynamic_index_in_dim(a, 1 - x_idx, 0, keepdims=False)))

    def give_back(rows):
        return swap_x(low16(rows[padded_quarter:]))

    def both_images(rows, got, after=()):
        def kernel(flag_ref, own_ref, got_ref, out):
            first = flag_ref[3] == 0
            own, other = own_ref[:quarter], up32(got_ref[...])[:quarter]
            out[:, 0, :] = jnp.where(first, own, other)
            out[:, 1, :] = jnp.where(first, other, own)

        outs = [shape((quarter, 2, width), F32)]
        pair = call(kernel, "both_images", outs, [SMEM, VMEM, VMEM], [], [flags, rows, got], 0, 16, after)[0]
        return pair

    rows = 2 * padded_quarter
    valid = lax.dynamic_index_in_dim(valid_len, x_idx, 0, keepdims=False)
    spot = jnp.arange(padded_quarter)
    live = [
        (spot < quarter) & ((2 * xx + cc) * quarter + spot < valid) for cc in (core, 1 - core) for xx in (x_idx, 1 - x_idx)
    ]
    bias = jnp.where(jnp.concatenate(live), 0.0, -1e30).astype(F32)[None, :]
    bias = jnp.broadcast_to(bias, (8, bias.shape[1]))

    span = query_weight.shape[2]
    units = up_weight.shape[2]
    part = width // dp
    plane = two_rows()

    gain_moves = [move(norm_gains[0]) for move in (swap_x, swap_y, swap_both)] if plane else []
    turned = [jnp.transpose(w[0]) for w in (query_weight, key_weight, value_weight)]
    packed, packed_x, keep_rows, (at_heads, at_up, at_down), h_units = pack(
        flags, [*turned, output_weight[0]], up_weight[0], jnp.transpose(down_weight[0]), jnp.transpose(images, (1, 0, 2)),
        padded_quarter,
    )
    h_heads = span // 2
    if plane:
        from_x, from_y = swap_x(packed_x), swap_y(packed)
        img_got = from_x[-padded_quarter:]
        at = 2 * h_heads
        over_heads = [(swap_x(from_y[:at]), 0, at), (swap_y(from_x[at:at_up]), 0, at)]
        over_up = [(swap_x(from_y[at_up:at_down]), 0, h_units)]
        over_down = [(swap_y(from_x[at_down : at_down + h_units]), 0, h_units)]
        near = lambda row, rows: [[(packed, row, rows)], [(from_y, row, rows)]]
        far = lambda row, rows, over: [[(from_x, row, rows)], over]
    else:
        whole = lax.all_gather(packed, "dp")
        other = swap_x(whole)
        over_heads = over_up = over_down = None
        img_got = swap_x(theirs(images))
        near = lambda row, rows: [[(whole[i], row, rows)] for i in range(dp)]
        far = lambda row, rows, over: [[(other[i], row, rows)] for i in range(dp)]
    gains = gather_gains(norm_gains[0], gain_moves, dp_idx, x_idx, core)
    first_rows = jnp.concatenate((keep_rows, up32(img_got)), axis=0)
    first_far = swap_core(low16(first_rows))
    heads_near = put_together("heads_near", near(at_heads, 4 * h_heads), flags, 4, h_heads)
    up_near = put_together("up_near", near(at_up, h_units), flags, 1, h_units, [heads_near])[0]
    down_near = put_together("down_near", near(at_down, h_units), flags, 1, h_units, [heads_near])[0]
    heads_far = put_together("heads_far", far(at_heads, 4 * h_heads, over_heads), flags, 4, h_heads, [up_near, down_near, first_rows])
    heads = [heads_near, heads_far, swap_core(heads_near), swap_core(heads_far)]
    hidden, normed_b = layer_first(flags, first_rows, first_far, bias, gains, heads)
    up_near = [up_near, swap_core(up_near)]
    down_near = [down_near, swap_core(down_near)]
    act_near = feed_up(normed_b, up_near)
    half_out = feed_down(hidden, act_near, down_near, F32)
    up_far = put_together("up_far", far(at_up, h_units, over_up), flags, 1, h_units, [normed_b])[0]
    up_far = [up_far, swap_core(up_far)]
    down_far = put_together("down_far", far(at_down, h_units, over_down), flags, 1, h_units, [normed_b])[0]
    down_far = [down_far, swap_core(down_far)]
    act_far = feed_up(normed_b, up_far)
    out = feed_down(half_out, act_far, down_far, BF)

    def fetch(after):
        return settle(flags, after, heads, up_near + up_far, down_near + down_far)

    sources = [first_rows, first_far]
    for tick in range(1, sections):
        got = shift(out, 1)
        if tick == 1:
            weights, token = fetch(out)
            got, token = ties(got, token)
        sources += [got, swap_core(got)]
        if tick + 1 < sections:
            out = layer_mid(flags, *sources[-2:], bias, gains, *weights, [token] if tick == 1 else [])
            if tick == 1:
                cot_got = swap_x(theirs(cotangent))
    x, normed_a, q, kv = last_project(flags, sources, gains, weights[0])
    mix, mix_rest, lse, hidden, normed_b = last_attention(q, kv, bias, x, gains, weights[0])
    out, slope, hidden_grad, do, dy = feed_turn(hidden, normed_b, mine(cotangent), cot_got, gains, *weights)

    sources = [dy]
    acts_got = give_back(out)

    def core_halves(a):
        lo = jnp.concatenate((a[:, :span], a[:, 2 * span : 3 * span]), axis=1)
        hi = jnp.concatenate((a[:, span : 2 * span], a[:, 3 * span :]), axis=1)
        return jnp.where(core == 0, lo, hi), jnp.where(core == 0, hi, lo)

    at = half_cut(rows)

    at = half_cut(rows)
    for tick in range(sections):
        last = tick + 1 == sections
        if last:
            dy_low = low16(sources[0])
            for i, a in enumerate(sources[1:]):
                dy_low = jnp.where(section == sections - 2 - i, a, dy_low)
            if plane:
                dy_x0, dy_y1 = swap_x(dy_low[:at]), swap_y(dy_low[at:])
        if tick:
            mode = "last" if last else "mid"
            used, after = (sources, [act_all]) if last else (sources[-1:], [acts] if tick == 2 else [])
            results = feed_back(mode, flags, used, slope, hidden, gains, *weights, after)
            hidden_grad, do = results[:2]
        if last:
            mix_low, gain_sum_b = results[2:]
            mix_got, ml_far = swap_core(mix_give), swap_core(mix_low)
        after = []
        if plane and tick == 2:
            after = [nb_d0, nb_d1]
        if plane and last:
            dy_d0, dy_d1 = swap_y(dy_x0), swap_x(dy_y1)
            after = [dy_x0, dy_y1]
        dq, dkv, dkv_far = attention_back(q, kv, do, mix, mix_rest, lse, bias, after)
        dkv_got = swap_core(dkv_far)
        after = []
        if plane and last:
            o_parts = plane_blocks("output_grads", flags, (mix_keep, mix_got), (mix_low, ml_far), [dq])
            dy_rest = tie(dy_low, o_parts[0])
            dy_x1, dy_y0 = swap_x(dy_rest[at:]), swap_y(dy_rest[:at])
            after = [o_parts[0]]
        back = qkv_back(last, flags, dq, dkv, dkv_got, x, hidden_grad, gains, weights[0], after)
        if last:
            break
        got = shift(back[0], -1)
        if tick == 0:
            nb_x, nb_y = (swap_x(normed_b), swap_y(normed_b)) if plane else (normed_b, normed_b)
        elif tick == 1:
            if plane:
                nb_d0, nb_d1 = swap_x(nb_y[:at]), swap_y(nb_x[at:])
            acts = both_images(out, acts_got)
            mix_keep, mix_give = core_halves(mix)
            na_far = swap_core(normed_a)
        elif tick == 2:
            if plane:
                pieces = [normed_b, nb_x[:at], nb_x[at:], nb_y[:at], nb_y[at:], nb_d0, nb_d1]
                nb_four = join("join_normed", pieces, [back[0]])
                nb_far = swap_core(nb_four)
            else:
                nb_all = lax.all_gather(normed_b, ("dp", "tensor"), axis=0, tiled=True)
                nb_four, nb_far = jnp.split(nb_all, 2)
            act_all, slope_all = unit_forward(nb_four, nb_far, up_near[0], [mix_keep, mix_give, na_far])
            got, act_all = ties(got, act_all)
        sources.append(got)
    dx, _, keep, give, gain_sum_a = back

    got = swap_core(give)
    grads_got = give_back(dx)
    gain_sums = jnp.concatenate((gain_sum_a, gain_sum_b), axis=0)
    if plane:
        gain_moves = [move(gain_sums) for move in (swap_x, swap_y, swap_both)]
        o_via = swap_x(o_parts[1]), swap_y(o_parts[2])
        qkv_parts = plane_blocks("qkv_grads", flags, (keep, got), (normed_a, na_far))
        via = swap_x(qkv_parts[1]), swap_y(qkv_parts[2])
        dy_four = join("join_dy", [dy_low, dy_x0, dy_x1, dy_y0, dy_y1, dy_d0, dy_d1], [qkv_parts[0]])
        dy_far = swap_core(dy_four)
        grad_up = up_grads(nb_four, nb_far, dy_four, dy_far, slope_all, down_near[0], flags, units, part, [qkv_parts[0]])
        o_over = scatter_middle("output_middle", *o_parts[3:], *o_via, [grad_up])
        over = scatter_middle("qkv_middle", *qkv_parts[3:], *via, [grad_up])
        grad_down = down_grads(dy_four, dy_far, act_all, flags, units, part, [grad_up, *gain_moves])
        gain_sums = gain_sums + gain_moves[0] + gain_moves[1] + gain_moves[2]
        gain_sums = gain_sums + swap_core(gain_sums)
        (grad_o,) = scatter_end("output_end", o_parts[0], *o_via, *o_over, 1, [grad_down])
        grad_heads = scatter_end("qkv_end", qkv_parts[0], *via, *over, 3, [grad_down])
        gain_shard = lax.dynamic_slice_in_dim(gain_sums, (dp_idx * 4 + tensor_idx) * (width // 8), width // 8, 1)
    else:
        dy_all = lax.all_gather(dy_low, ("dp", "tensor"), axis=0, tiled=True)
        dy_four, dy_far = jnp.split(dy_all, 2)
        grad_up = up_grads(nb_four, nb_far, dy_four, dy_far, slope_all, down_near[0], flags, units, part)
        grad_down = down_grads(dy_four, dy_far, act_all, flags, units, part)
        both = lambda a, b: jnp.concatenate((a, b), axis=0)
        g = t_dot(both(keep, got), both(normed_a, na_far))
        g = g[: 3 * span] + up32(swap_x(low16(g[3 * span :])))
        g = up32(lax.psum_scatter(low16(g), "dp", scatter_dimension=1, tiled=True))
        grad_heads = [g[i * span : (i + 1) * span] for i in range(3)]
        g = t_dot(both(mix_keep, swap_core(mix_give)), both(mix_low, swap_core(mix_low)))
        g = g[:span] + up32(swap_x(low16(g[span:])))
        grad_o = up32(lax.psum_scatter(low16(g), "dp", scatter_dimension=1, tiled=True))
        gain_shard = lax.psum_scatter(gain_sums, ("dp", "tensor"), scatter_dimension=1, tiled=True)
    grads = both_images(dx, grads_got)

    return (
        jnp.transpose(acts, (1, 0, 2))[None],
        jnp.transpose(grads, (1, 0, 2))[None],
        *[jnp.transpose(g)[None] for g in grad_heads],
        grad_o[None],
        grad_up[None],
        jnp.transpose(grad_down)[None],
        gain_shard[None],
    )


def solution(mesh):
    return jax.shard_map(
        local,
        mesh=mesh,
        in_specs=(
            P("dp", "tensor", None),
            P("dp"),
            P("section", "dp", "tensor"),
            P("section", "dp", "tensor"),
            P("section", "dp", "tensor"),
            P("section", "tensor", "dp"),
            P("section", "dp", "tensor"),
            P("section", "tensor", "dp"),
            P("section", None, ("dp", "tensor")),
            P("dp", "tensor", None),
        ),
        out_specs=(
            P("section", "dp", "tensor", None),
            P("section", "dp", "tensor", None),
            P("section", "dp", "tensor"),
            P("section", "dp", "tensor"),
            P("section", "dp", "tensor"),
            P("section", "tensor", "dp"),
            P("section", "dp", "tensor"),
            P("section", "tensor", "dp"),
            P("section", None, ("dp", "tensor")),
        ),
        check_vma=False,
    )
```

```python
import jax
import jax.numpy as jnp
from jax import lax
from jax.experimental import pallas as pl
from jax.experimental.pallas import tpu as pltpu
from jax.sharding import PartitionSpec as P

HD = 72
EPS = 1e-06
SCALE = HD ** (-0.5)
LOG2E = 1.4426950408889634
BF = jnp.bfloat16
F32 = jnp.float32
WIN = 256
LANES = 128
COST = 0.1
ROOM = 28
K0 = 0.7978845608028654
K1 = 0.044715
VMEM = pl.BlockSpec(memory_space=pltpu.VMEM)
SMEM = pl.BlockSpec(memory_space=pltpu.SMEM)
ANY = pl.BlockSpec(memory_space=pl.ANY)


def swap_core(a):
    n = lax.axis_size("tensor")
    return lax.ppermute(a, "tensor", [(i, i ^ 1) for i in range(n)])


def swap_x(a):
    n = lax.axis_size("tensor")
    return lax.ppermute(a, "tensor", [(i, i ^ 2) for i in range(n)])


def swap_y(a):
    return lax.ppermute(a, "dp", [(0, 1), (1, 0)])


def swap_both(a):
    n = lax.axis_size("tensor")
    pairs = [(y * n + i, (1 - y) * n + (i ^ 2)) for y in (0, 1) for i in range(n)]
    return lax.ppermute(a, ("dp", "tensor"), pairs)


def shift(a, by):
    n = lax.axis_size("section")
    pairs = [(i, i + by) for i in range(n) if 0 <= i + by < n]
    return lax.ppermute(a, "section", pairs)


def two_rows():
    return lax.axis_size("dp") == 2


def half_cut(rows):
    return (rows // 2 + 15) // 16 * 16


def up32(a):
    return a.astype(F32)


def low16(a):
    return a.astype(BF)


def dot(a, b):
    return jnp.dot(a, b, preferred_element_type=F32)


def dot_t(a, b):
    return lax.dot_general(a, b, (((1,), (1,)), ((), ())), preferred_element_type=F32)


def t_dot(a, b):
    return lax.dot_general(a, b, (((0,), (0,)), ((), ())), preferred_element_type=F32)


def in_hbm(a):
    return pltpu.with_memory_space_constraint(a, pltpu.HBM)


def spans(total, size):
    return [(at, min(size, total - at)) for at in range(0, total, size)]


def norm_parts(values):
    centre = jnp.mean(values, axis=-1, keepdims=True)
    centred = values - centre
    spread = jnp.mean(centred * centred, axis=-1, keepdims=True)
    inverse = lax.rsqrt(spread + EPS)
    return centred * inverse, inverse


def norm_back(grad, unit, inverse, gain):
    e = grad * gain
    return inverse * (e - jnp.mean(e, axis=-1, keepdims=True) - unit * jnp.mean(e * unit, axis=-1, keepdims=True))


def span_copies(pieces, whole, sems, base):
    rows = pieces[0].shape[0]
    return [
        (pltpu.make_async_copy(piece, whole.at[i * rows : (i + 1) * rows], sems.at[base + i]), (i + 1) * rows)
        for i, piece in enumerate(pieces)
    ]


class Arrivals:
    def __init__(self, copies):
        self.left = list(copies)
        self.have = 0

    def start(self):
        for copy, _ in self.left:
            copy.start()

    def need(self, row):
        while self.left and self.have < row:
            copy, self.have = self.left.pop(0)
            copy.wait()

    def rest(self):
        self.need(1 << 30)


def gelu_one(u):
    return u * (0.5 + 0.5 * jnp.tanh(u * (K0 + (K0 * K1) * (u * u))))


def gelu_both(u):
    sq = u * u
    th = jnp.tanh(u * (K0 + (K0 * K1) * sq))
    half = 0.5 + 0.5 * th
    return u * half, half + (0.5 * u) * (1.0 - th * th) * (K0 + (3.0 * K1 * K0) * sq)


def head_window(h, width):
    tile = min(h * HD // LANES, width // LANES - WIN // LANES)
    off = h * HD - tile * LANES
    lane = lax.broadcasted_iota(jnp.int32, (1, WIN), 1)
    return slice(tile * LANES, tile * LANES + WIN), (lane >= off) & (lane < off + HD)


def shape(dims, dtype):
    return jax.ShapeDtypeStruct(dims, dtype)


def past(kernel, inputs, after):
    return lambda *refs: kernel(*refs[:inputs], *refs[inputs + len(after) :])


def call(kernel, name, outs, ins, scratch, args, flops, limit=60, after=(), cost=None):
    moved = sum(a.size * a.dtype.itemsize for a in args) + sum(o.size * o.dtype.itemsize for o in outs)
    return pl.pallas_call(
        past(kernel, len(args), after),
        out_shape=tuple(outs),
        in_specs=[*ins, *[ANY] * len(after)],
        out_specs=tuple([VMEM] * len(outs)),
        scratch_shapes=scratch,
        compiler_params=pltpu.CompilerParams(vmem_limit_bytes=limit * 2**20),
        cost_estimate=pl.CostEstimate(flops=int(flops * (cost or COST)), bytes_accessed=int(moved * (cost or COST)), transcendentals=0),
        name=name,
    )(*args, *after)


def pack(flags, heads, up, down, pair, quarter):
    span, part = heads[0].shape
    units = up.shape[1]
    h = span // 2
    hu = (units + 31) // 32 * 16

    def kernel(flag_ref, *refs):
        pair_ref, out, give_ref, mine_ref = refs[6:]
        got = pair_ref.shape[0]
        first = flag_ref[3] == 0
        one, two = pair_ref[:, 0, :], pair_ref[:, 1, :]
        mine_ref[...] = jnp.zeros_like(mine_ref)
        mine_ref[:got] = jnp.where(first, one, two)
        for i, ref in enumerate(refs[:4]):
            out[i * h : (i + 1) * h, :part] = ref[:h, :]
            out[i * h : (i + 1) * h, part:] = ref[h:, :]
        for i, ref in enumerate(refs[4:6]):
            base = 4 * h + i * hu
            rows = low16(up32(ref[...]).T)
            out[base : base + hu, :part] = rows[:hu]
            out[base : base + units - hu, part:] = rows[hu:]
            out[base + units - hu : base + hu, part:] = jnp.zeros((2 * hu - units, part), BF)
        give_ref[...] = jnp.zeros_like(give_ref)
        give_ref[:got] = low16(jnp.where(first, two, one))

    total = 4 * h + 2 * hu
    width = pair.shape[2]
    outs = [shape((total, 2 * part), BF), shape((quarter, width), BF), shape((quarter, width), F32)]
    got = call(kernel, "pack", outs, [SMEM] + [VMEM] * 7, [], [flags, *heads, up, down, pair], 0, 30)
    return *got, (0, 4 * h, 4 * h + hu), hu


def put_together(name, pieces, flags, groups, h, after=()):
    count = len(pieces)
    parts = [(i, *p) for i, piece in enumerate(pieces) for p in piece]
    part = parts[0][1].shape[1] // 2
    width = part * count

    def kernel(flag_ref, *refs):
        out, held, sem = refs[len(parts) :]
        copies, at = [], [0] * count
        for j, (ref, (i, _, row, rows)) in enumerate(zip(refs, parts)):
            copies.append(pltpu.make_async_copy(ref.at[row : row + rows], held.at[i, at[i] : at[i] + rows], sem.at[j]))
            at[i] += rows
        for copy in copies:
            copy.start()
        wait_all(copies)
        first = flag_ref[0] == 0
        for i in range(count):
            for g in range(groups):
                rows = slice(g * h, (g + 1) * h)
                piece = jnp.where(first, held[i, rows], held[1 - i, rows]) if count == 2 else held[i, rows]
                out[g, :h, i * part : (i + 1) * part] = piece[:, :part]
                out[g, h:, i * part : (i + 1) * part] = piece[:, part:]

    scratch = [pltpu.VMEM((count, groups * h, 2 * part), BF), pltpu.SemaphoreType.DMA((len(parts),))]
    outs = [shape((groups, 2 * h, width), BF)]
    args = [flags, *[in_hbm(p[1]) for p in parts]]
    return call(kernel, name, outs, [SMEM] + [ANY] * len(parts), scratch, args, 0, 24, after)[0]


def head_copies(pieces, core, kinds, whole, sems, base):
    span, width = pieces[0].shape[1], pieces[0].shape[2]
    out = []
    for n, kind in enumerate(kinds):
        group = []
        for i, piece in enumerate(pieces):
            c = core if i < 2 else 1 - core
            at = pl.multiple_of(n * width + (2 * (i % 2) + c) * span, span)
            sem = sems.at[base + 4 * n + i]
            group.append(pltpu.make_async_copy(piece.at[kind], whole.at[pl.ds(at, span)], sem))
        out.append(group)
    return out


def wait_all(copies):
    for copy in copies:
        copy.wait()


def attend(q, kv, bias, mix, rest, lse_ref):
    rows, width = q.shape
    lane = lax.broadcasted_iota(jnp.int32, (1, LANES), 1)
    for h in range(width // HD):
        win, live = head_window(h, width)
        keys = jnp.where(live, kv[:, win], jnp.zeros((), BF))
        vals = kv[:, width + win.start : width + win.stop]
        s = dot_t(q[:, win], keys) * (SCALE * LOG2E) + bias
        top = jnp.max(s, axis=-1, keepdims=True)
        p = jnp.exp2(s - top)
        total = jnp.sum(p, axis=-1, keepdims=True)
        o = dot(low16(p), vals) * (1.0 / total)
        o_low = low16(o)
        mix[:, win] = jnp.where(live, o_low, mix[:, win])
        if rest is not None:
            rest[:, win] = jnp.where(live, low16(o - up32(o_low)), rest[:, win])
            lse_ref[...] = jnp.where(lane == h, top + jnp.log2(total), lse_ref[...])


def feed_up(normed, pieces, after=()):
    rows, width = normed.shape
    units = sum(piece.shape[0] for piece in pieces)
    n = len(pieces)

    def kernel(nb_ref, *refs):
        act, w, sem = refs[n:]
        arrivals = Arrivals(span_copies(refs[:n], w, sem, 0))
        arrivals.start()
        for at, k in spans(units, 512):
            arrivals.need(at + k)
            act[:, at : at + k] = low16(gelu_one(dot_t(nb_ref[...], w[at : at + k, :])))

    scratch = [pltpu.VMEM((units, width), BF), pltpu.SemaphoreType.DMA((n,))]
    outs = [shape((rows, units), BF)]
    return call(kernel, "feed_up", outs, [VMEM] + [ANY] * n, scratch, [normed, *pieces], 2 * rows * width * units, 30, after)[0]


def feed_down(base, act, pieces, out_type, after=()):
    rows, width = base.shape
    units = act.shape[1]
    n = len(pieces)

    def kernel(base_ref, act_ref, *refs):
        out, w, sem = refs[n:]
        arrivals = Arrivals(span_copies(refs[:n], w, sem, 0))
        arrivals.start()
        arrivals.rest()
        for at, k in spans(width, 256):
            out[:, at : at + k] = (base_ref[:, at : at + k] + dot(act_ref[...], w[:, at : at + k])).astype(out.dtype)

    scratch = [pltpu.VMEM((units, width), BF), pltpu.SemaphoreType.DMA((n,))]
    outs = [shape((rows, width), out_type)]
    args = [base, act, *pieces]
    return call(kernel, "feed_down", outs, [VMEM, VMEM] + [ANY] * n, scratch, args, 2 * rows * width * units, 30, after)[0]


def project(nall, w, q, kv):
    rows, width = q.shape
    for at, n in spans(width, 512):
        q[:, at : at + n] = low16(dot_t(nall[:rows], w[width + at : width + at + n, :]))
    for at, n in spans(2 * width, 512):
        kv[:, at : at + n] = low16(dot_t(nall[...], w[2 * width + at : 2 * width + at + n, :]))


def layer_first(flags, rows32, far, bias, gains, heads):
    rows, width = rows32.shape

    def kernel(flag_ref, bias_ref, gain_ref, x_ref, far_ref, *refs):
        heads_r, hid_ref, nb_ref, w, nall, q, kv, mix, sem = refs[:4], *refs[4:]
        groups = head_copies(heads_r, flag_ref[1], (3, 0, 1, 2), w, sem, 0)
        for group in groups:
            for copy in group:
                copy.start()
        gain_a, gain_b = gain_ref[0:1, :], gain_ref[1:2, :]
        nall[:rows] = low16(norm_parts(x_ref[...])[0] * gain_a)
        nall[rows:] = low16(norm_parts(up32(far_ref[...]))[0] * gain_a)
        for group in groups:
            wait_all(group)
        project(nall, w, q, kv)
        mix[...] = jnp.zeros_like(mix)
        attend(q, kv, bias_ref[0:1, :], mix, None, None)
        hidden = x_ref[...] + dot(mix[...], w[:width, :])
        hid_ref[...] = hidden
        nb_ref[...] = low16(norm_parts(hidden)[0] * gain_b)

    scratch = [
        pltpu.VMEM((4 * width, width), BF),
        pltpu.VMEM((2 * rows, width), BF),
        pltpu.VMEM((rows, width), BF),
        pltpu.VMEM((2 * rows, 2 * width), BF),
        pltpu.VMEM((rows, width), BF),
        pltpu.SemaphoreType.DMA((16,)),
    ]
    outs = [shape((rows, width), F32), shape((rows, width), BF)]
    ins = [SMEM] + [VMEM] * 4 + [ANY] * 4
    flops = 16 * rows * 2 * rows * WIN * 4 + 12 * rows * width * width
    return call(kernel, "layer_first", outs, ins, scratch, [flags, bias, gains, rows32, far, *heads], flops, 44, (), 0.001)


def settle(flags, after, heads, ups, downs):
    kinds, span, width = heads[0].shape
    units = 4 * ups[0].shape[0]

    def kernel(flag_ref, *refs):
        wh, wu, wd, token, sem = refs[13:]
        copies = sum(head_copies(refs[:4], flag_ref[1], (3, 0, 1, 2), wh, sem, 0), [])
        copies += [copy for copy, _ in span_copies(refs[4:8], wu, sem, 16) + span_copies(refs[8:12], wd, sem, 20)]
        for copy in copies:
            copy.start()
        token[...] = jnp.zeros_like(token)
        wait_all(copies)

    pieces = [pltpu.with_memory_space_constraint(a, pltpu.HBM) for a in (*heads, *ups, *downs)]
    wh, wu, wd, token = pl.pallas_call(
        kernel,
        out_shape=(
            pltpu.VMEM((kinds * 4 * span, width), BF),
            pltpu.VMEM((units, width), BF),
            pltpu.VMEM((units, width), BF),
            shape((8, LANES), F32),
        ),
        in_specs=[SMEM] + [ANY] * 13,
        out_specs=(ANY, ANY, ANY, VMEM),
        scratch_shapes=[pltpu.SemaphoreType.DMA((24,))],
        compiler_params=pltpu.CompilerParams(vmem_limit_bytes=ROOM * 2**20),
        cost_estimate=pl.CostEstimate(flops=0, bytes_accessed=int(60 * COST * 2**20), transcendentals=0),
        name="settle",
    )(flags, *pieces, after)
    return [pltpu.with_memory_space_constraint(a, pltpu.VMEM) for a in (wh, wu, wd)], token


def feed(normed, hidden, w_up, w_down, act, slope_out, out):
    for at, n in spans(w_up.shape[0], 512):
        u = dot_t(normed, w_up[at : at + n, :])
        if slope_out is None:
            act[:, at : at + n] = low16(gelu_one(u))
        else:
            a, slope = gelu_both(u)
            act[:, at : at + n] = low16(a)
            slope_out[:, at : at + n] = low16(slope)
    for at, n in spans(w_down.shape[1], 256):
        out[:, at : at + n] = (hidden[:, at : at + n] + dot(act[...], w_down[:, at : at + n])).astype(out.dtype)


def layer_mid(flags, own, far, bias, gains, w_heads, w_up, w_down, after=()):
    rows, width = own.shape
    units = w_up.shape[0]

    def kernel(bias_ref, gain_ref, wh, wu, wd, own_ref, far_ref, out_ref, x_ref, q, kv, mix, hid_ref, nall, act):
        gain_a, gain_b = gain_ref[0:1, :], gain_ref[1:2, :]
        x_ref[...] = up32(own_ref[...])
        nall[:rows] = low16(norm_parts(x_ref[...])[0] * gain_a)
        nall[rows:] = low16(norm_parts(up32(far_ref[...]))[0] * gain_a)
        project(nall, wh, q, kv)
        mix[...] = jnp.zeros_like(mix)
        attend(q, kv, bias_ref[0:1, :], mix, None, None)
        hidden = x_ref[...] + dot(mix[...], wh[:width, :])
        hid_ref[...] = hidden
        feed(low16(norm_parts(hidden)[0] * gain_b), hid_ref, wu, wd, act, None, out_ref)

    scratch = [
        pltpu.VMEM((rows, width), F32),
        pltpu.VMEM((rows, width), BF),
        pltpu.VMEM((2 * rows, 2 * width), BF),
        pltpu.VMEM((rows, width), BF),
        pltpu.VMEM((rows, width), F32),
        pltpu.VMEM((2 * rows, width), BF),
        pltpu.VMEM((rows, units), BF),
    ]
    flops = 16 * rows * 2 * rows * WIN * 4 + 12 * rows * width * width + 4 * rows * width * units
    args = [bias, gains, w_heads, w_up, w_down, own, far]
    return call(kernel, "layer_mid", [shape((rows, width), BF)], [VMEM] * 7, scratch, args, flops, ROOM, after)[0]


def last_project(flags, sources, gains, w_heads):
    rows, width = sources[0].shape
    sections = len(sources) // 2

    def kernel(flag_ref, gain_ref, wh, *refs):
        src, refs = refs[: len(sources)], refs[len(sources) :]
        x_ref, na_ref, q, kv, nall, sem = refs

        def load(i, go):
            own, far = src[2 * i], src[2 * i + 1]
            near = pltpu.make_async_copy(own, x_ref if own.dtype == F32 else na_ref, sem.at[0])
            other = pltpu.make_async_copy(far, nall.at[rows:], sem.at[1])
            for copy in (near, other):
                if go:
                    copy.start()
                else:
                    copy.wait()
            if not go and own.dtype != F32:
                x_ref[...] = up32(na_ref[...])

        for go in (True, False):
            for i in range(sections):
                pl.when(flag_ref[2] == i)(lambda i=i, go=go: load(i, go))
        gain_a = gain_ref[0:1, :]
        normed = low16(norm_parts(x_ref[...])[0] * gain_a)
        na_ref[...] = normed
        nall[:rows] = normed
        nall[rows:] = low16(norm_parts(up32(nall[rows:]))[0] * gain_a)
        project(nall, wh, q, kv)

    row32, row16 = shape((rows, width), F32), shape((rows, width), BF)
    outs = [row32, row16, row16, shape((2 * rows, 2 * width), BF)]
    scratch = [pltpu.VMEM((2 * rows, width), BF), pltpu.SemaphoreType.DMA((2,))]
    ins = [SMEM, VMEM, VMEM] + [ANY] * len(sources)
    args = [flags, gains, w_heads, *[in_hbm(a) for a in sources]]
    return call(kernel, "last_project", outs, ins, scratch, args, 10 * rows * width * width, 12)


def last_attention(q, kv, bias, x, gains, w_heads, after=()):
    rows, width = q.shape

    def kernel(q_ref, kv_ref, bias_ref, x_ref, gain_ref, wh, mix, rest_ref, lse_ref, hid_ref, nb_ref):
        mix[...] = jnp.zeros_like(mix)
        lse_ref[...] = jnp.zeros_like(lse_ref)
        rest_ref[...] = jnp.zeros_like(rest_ref)
        attend(q_ref, kv_ref, bias_ref[0:1, :], mix, rest_ref, lse_ref)
        hidden = x_ref[...] + dot(mix[...], wh[:width, :])
        hid_ref[...] = hidden
        nb_ref[...] = low16(norm_parts(hidden)[0] * gain_ref[1:2, :])

    row32, row16 = shape((rows, width), F32), shape((rows, width), BF)
    outs = [row16, row16, shape((rows, LANES), F32), row32, row16]
    flops = 16 * rows * 2 * rows * WIN * 4 + 2 * rows * width * width
    return call(kernel, "last_attention", outs, [VMEM] * 6, [], [q, kv, bias, x, gains, w_heads], flops, 18, after)


def feed_turn(hidden, normed, dy_own, dy_got, gains, w_heads, w_up, w_down):
    rows, width = hidden.shape
    units = w_up.shape[0]

    half = dy_own.shape[0]

    def kernel(hid_ref, nb_ref, own_ref, got_ref, gain_ref, wh, wu, wd, out_ref, slope_ref, hg_ref, do_ref, dy_ref, act, nbg):
        dy_ref[:half] = own_ref[...]
        dy_ref[half:] = up32(got_ref[...])
        feed(nb_ref[...], hid_ref, wu, wd, act, slope_ref, out_ref)
        feed_grads(low16(dy_ref[...]), slope_ref, wu, wd, act, nbg)
        unit, inverse = norm_parts(hid_ref[...])
        hidden_grad = dy_ref[...] + norm_back(nbg[...], unit, inverse, gain_ref[1:2, :])
        hg_ref[...] = hidden_grad
        do_ref[...] = low16(dot_t(low16(hidden_grad), wh[:width, :]))

    row32 = shape((rows, width), F32)
    outs = [row32, shape((rows, units), BF), row32, shape((rows, width), BF), row32]
    scratch = [pltpu.VMEM((rows, units), BF), pltpu.VMEM((rows, width), F32)]
    flops = 8 * rows * width * units
    args = [hidden, normed, dy_own, dy_got, gains, w_heads, w_up, w_down]
    return call(kernel, "feed_turn", outs, [VMEM] * 8, scratch, args, flops, 22)


def feed_grads(low, slope_ref, w_up, w_down, inner, out, ups=()):
    for at, n in spans(w_up.shape[0], 512):
        inner[:, at : at + n] = low16(dot_t(low, w_down[at : at + n, :]) * up32(slope_ref[:, at : at + n]))
    wait_all(ups)
    for at, n in spans(w_up.shape[1], 256):
        out[:, at : at + n] = dot(inner[...], w_up[:, at : at + n])


def feed_back(mode, flags, sources, slope, hidden, gains, w_heads, w_ups, w_down, after=()):
    last = mode == "last"
    rows, width = hidden.shape
    units = w_down.shape[0]
    n_up = len(w_ups)

    def kernel(flag_ref, gain_ref, hid_ref, slope_ref, wh, wd, *refs):
        *refs, wu, up_sem = refs
        ups = [copy for copy, _ in span_copies(refs[:n_up], wu, up_sem, 0)]
        for copy in ups:
            copy.start()
        refs = refs[n_up:]
        src, refs = refs[: len(sources)], refs[len(sources) :]
        hg_ref, do_ref, refs = refs[0], refs[1], refs[2:]
        if last:
            ml_ref, gs_ref, ig, nbg, dy_ref, low, sem = refs

            def load(a, go):
                copy = pltpu.make_async_copy(a, dy_ref if a.dtype == F32 else low, sem.at[0])
                if go:
                    copy.start()
                    return
                copy.wait()
                if a.dtype == F32:
                    low[...] = low16(dy_ref[...])
                else:
                    dy_ref[...] = up32(low[...])

            for go in (True, False):
                for i, a in enumerate(src):
                    pl.when(flag_ref[2] == len(src) - 1 - i)(lambda a=a, go=go: load(a, go))
        else:
            ig, nbg, dy_ref, low = refs
            dy_ref[...] = src[0][...].astype(F32)
            low[...] = low16(src[0][...])
        feed_grads(low[...], slope_ref, wu, wd, ig, nbg, ups)
        unit, inverse = norm_parts(hid_ref[...])
        grad = nbg[...]
        if last:
            gs_ref[...] = jnp.sum(grad * unit, axis=0, keepdims=True)
        hidden_grad = dy_ref[...] + norm_back(grad, unit, inverse, gain_ref[1:2, :])
        hg_ref[...] = hidden_grad
        mix_low = low16(hidden_grad)
        if last:
            ml_ref[...] = mix_low
        do_ref[...] = low16(dot_t(mix_low, wh[:width, :]))

    sources = [in_hbm(a) if last else a for a in sources]
    args = [flags, gains, hidden, slope, w_heads, w_down, *[in_hbm(a) for a in w_ups], *sources]
    outs = [shape((rows, width), F32), shape((rows, width), BF)]
    if last:
        outs += [shape((rows, width), BF), shape((1, width), F32)]
    scratch = [
        pltpu.VMEM((rows, units), BF),
        pltpu.VMEM((rows, width), F32),
        pltpu.VMEM((rows, width), F32),
        pltpu.VMEM((rows, width), BF),
    ]
    if last:
        scratch.append(pltpu.SemaphoreType.DMA((1,)))
    scratch += [pltpu.VMEM((units, width), BF), pltpu.SemaphoreType.DMA((n_up,))]
    ins = [SMEM] + [VMEM] * 5 + [ANY] * n_up + [ANY if last else VMEM] * len(sources)
    flops = 4 * rows * width * units + 2 * rows * width * width
    return call(kernel, "feed_back_" + mode, outs, ins, scratch, args, flops, 24, after)


def attention_back(q, kv_all, do, mix, mix_rest, lse, bias, after=()):
    rows, width = q.shape
    keys_n = 2 * rows

    def kernel(q_ref, kv, do_ref, o_ref, rest_ref, lse_ref, bias_ref, dq_ref, dkv_own, dkv_far, qt, dt, dkt, dvt):
        bias_row = bias_ref[0:1, :]
        qt[...] = q_ref[...].T
        dt[...] = do_ref[...].T
        dq_ref[...] = jnp.zeros_like(dq_ref)
        zero = jnp.zeros((), BF)
        parts = ([], [])
        for h in range(width // HD):
            win, live = head_window(h, width)
            keys = jnp.where(live, kv[:, win], zero)
            vals = jnp.where(live, kv[:, width + win.start : width + win.stop], zero)
            d_out = do_ref[:, win]
            whole = up32(o_ref[:, win]) + up32(rest_ref[:, win])
            row_dot = jnp.sum(jnp.where(live, up32(d_out) * whole, 0.0), axis=-1, keepdims=True)
            s = dot_t(q_ref[:, win], keys) * (SCALE * LOG2E) + bias_row
            p = jnp.exp2(s - lse_ref[:, h : h + 1])
            ds = low16(p * (dot_t(d_out, vals) - row_dot))
            dq = dot(ds, keys) * SCALE
            dq_ref[:, win] = jnp.where(live, low16(dq), dq_ref[:, win])
            row = h % 2 * HD
            pair = slice((h - h % 2) * HD, (h - h % 2 + 2) * HD)
            parts[0].append(low16(dot(qt[pair, :][row : row + HD], ds) * SCALE))
            parts[1].append(low16(dot(dt[pair, :][row : row + HD], low16(p))))
            if h % 2:
                dkt[pair, :] = jnp.concatenate(parts[0], axis=0)
                dvt[pair, :] = jnp.concatenate(parts[1], axis=0)
                parts = ([], [])
        dk = dkt[...].T
        dv = dvt[...].T
        dkv_own[:, :width] = dk[:rows]
        dkv_own[:, width:] = dv[:rows]
        dkv_far[:, :width] = dk[rows:]
        dkv_far[:, width:] = dv[rows:]

    outs = [shape((rows, width), BF), shape((rows, 2 * width), BF), shape((rows, 2 * width), BF)]
    scratch = [
        pltpu.VMEM((width, rows), BF),
        pltpu.VMEM((width, rows), BF),
        pltpu.VMEM((width, keys_n), BF),
        pltpu.VMEM((width, keys_n), BF),
    ]
    flops = 16 * rows * keys_n * WIN * 10
    return call(kernel, "attention_back", outs, [VMEM] * 7, scratch, [q, kv_all, do, mix, mix_rest, lse, bias], flops, 17, after)


def qkv_back(full, flags, dq, own, got, x, hidden_grad, gains, w_heads, after=()):
    rows, width = dq.shape
    span = width // 4

    def kernel(flag_ref, gain_ref, dq_ref, own_ref, got_ref, x_ref, hg_ref, w, *refs):
        if full:
            dx_ref, low_ref, keep_ref, give_ref, gs_ref, grads, nag = refs
        else:
            low_ref, grads, nag = refs
        grads[:, :width] = dq_ref[...]
        grads[:, width:] = low16(up32(own_ref[...]) + up32(got_ref[...]))
        if full:
            mine = flag_ref[1] == 0
            for i in range(3):
                for xr in (0, 1):
                    at = i * width + 2 * xr * span
                    lo = grads[:, at : at + span]
                    hi = grads[:, at + span : at + 2 * span]
                    to = xr * 3 * span + i * span
                    keep_ref[:, to : to + span] = jnp.where(mine, lo, hi)
                    give_ref[:, to : to + span] = jnp.where(mine, hi, lo)
        for at, n in spans(width, 256):
            nag[:, at : at + n] = dot(grads[...], w[width:, at : at + n])
        unit, inverse = norm_parts(x_ref[...])
        grad = nag[...]
        if full:
            gs_ref[...] = jnp.sum(grad * unit, axis=0, keepdims=True)
        dx = hg_ref[...] + norm_back(grad, unit, inverse, gain_ref[0:1, :])
        low_ref[...] = low16(dx)
        if full:
            dx_ref[...] = dx

    outs = [shape((rows, width), BF)]
    if full:
        outs = [shape((rows, width), F32)] + outs
        outs += [shape((rows, 6 * span), BF), shape((rows, 6 * span), BF), shape((1, width), F32)]
    scratch = [pltpu.VMEM((rows, 3 * width), BF), pltpu.VMEM((rows, width), F32)]
    args = [flags, gains, dq, own, got, x, hidden_grad, w_heads]
    return call(kernel, "qkv_back", outs, [SMEM] + [VMEM] * 7, scratch, args, 6 * rows * width * width, 11, after)


def halves_of(total):
    steps = max(1, total // 736)
    return steps, total // steps


def halves_specs(steps, block, cols):
    return [
        pl.BlockSpec((block, cols), lambda i: (jnp.minimum(i, steps - 1), 0)),
        pl.BlockSpec((block, cols), lambda i: (jnp.maximum(i, steps) - steps, 0)),
    ]


def unit_forward(normed_four, normed_far, w_up, after=()):
    total, width = normed_four.shape
    n = w_up.shape[0]
    half, block = halves_of(total)

    def kernel(a_ref, b_ref, wu_ref, act_ref, slope_ref):
        def rows(nb_ref):
            for at, k in spans(n, 512):
                act, slope = gelu_both(dot_t(nb_ref[...], wu_ref[at : at + k, :]))
                act_ref[:, at : at + k] = low16(act)
                slope_ref[:, at : at + k] = low16(slope)

        pl.when(pl.program_id(0) < half)(lambda: rows(a_ref))
        pl.when(pl.program_id(0) >= half)(lambda: rows(b_ref))

    by_rows = pl.BlockSpec((block, n), lambda i: (i, 0))
    return pl.pallas_call(
        past(kernel, 3, after),
        grid=(2 * half,),
        in_specs=[*halves_specs(half, block, width), VMEM, *[ANY] * len(after)],
        out_specs=(by_rows, by_rows),
        out_shape=(pltpu.HBM((2 * total, n), BF), pltpu.HBM((2 * total, n), BF)),
        compiler_params=pltpu.CompilerParams(vmem_limit_bytes=18 * 2**20),
        cost_estimate=pl.CostEstimate(flops=int(5.6 * COST * total * width * n), bytes_accessed=int(12 * COST * total * width), transcendentals=0),
        name="unit_forward",
    )(normed_four, normed_far, w_up, *after)


def pick_cols(a, which, part):
    picked = a[:, :part]
    for i in range(1, a.shape[1] // part):
        picked = jnp.where(which == i, a[:, i * part : (i + 1) * part], picked)
    return picked


def unit_sums(name, flags, sides, saved, w_down, units, part, after=()):
    total, width = sides[0][0].shape
    n = saved.shape[1]
    steps = max(1, total // 736)
    block = total // steps
    all_steps = steps * len(sides)
    kinds = len(sides[0])
    flat = [a for side in sides for a in side]
    with_w = w_down is not None

    def kernel(flag_ref, *refs):
        if with_w:
            wd_ref, refs = refs[0], refs[1:]
        saved_hbm, refs = refs[0], refs[1:]
        rows_hbm, refs = refs[: len(flat)], refs[len(flat) :]
        out, held, sems = refs[0], refs[1 : 2 + kinds], refs[2 + kinds]

        def into(i):
            rows = slice(i % steps * block, (i % steps + 1) * block)
            sources = [rows_hbm[i // steps * kinds + j].at[rows] for j in range(kinds)]
            sources.append(saved_hbm.at[i * block : (i + 1) * block])
            return [pltpu.make_async_copy(a, b.at[i % 2], sems.at[j, i % 2]) for j, (a, b) in enumerate(zip(sources, held))]

        for copy in into(0):
            copy.start()
        for i in range(all_steps):
            if i + 1 < all_steps:
                for copy in into(i + 1):
                    copy.start()
            wait_all(into(i))
            turned = pick_cols(held[0][i % 2], flag_ref[0], part).T
            for at, k in spans(n, 512):
                right = held[kinds][i % 2, :, at : at + k]
                if with_w:
                    right = low16(dot_t(held[1][i % 2], wd_ref[at : at + k, :]) * up32(right))
                real = min(k, units - at)
                cols = slice(at, at + real)
                got = dot(turned, right)[:, :real]
                out[:, cols] = got if i == 0 else out[:, cols] + got

    scratch = [pltpu.VMEM((2, block, width), BF)] * kinds + [pltpu.VMEM((2, block, n), BF)]
    scratch.append(pltpu.SemaphoreType.DMA((kinds + 1, 2)))
    args = [flags, *([w_down] if with_w else []), in_hbm(saved), *flat]
    ins = [SMEM] + [VMEM] * with_w + [ANY] * (1 + len(flat))
    flops = (4 if with_w else 2) * total * len(sides) * width * n
    return call(kernel, name, [shape((part, units), F32)], ins, scratch, args, flops, 40, after, 0.2)[0]


def join(name, pieces, after=()):
    n = len(pieces)

    def kernel(*refs):
        out, at = refs[n], 0
        for ref in refs[:n]:
            out[at : at + ref.shape[0]] = ref[...]
            at += ref.shape[0]

    rows = sum(a.shape[0] for a in pieces)
    return call(kernel, name, [shape((rows, pieces[0].shape[1]), BF)], [VMEM] * n, [], list(pieces), 0, 16, after)[0]


def plane_blocks(name, flags, left, right, after=()):
    rows = left[0].shape[0]
    part = right[0].shape[1] // 2
    span = left[0].shape[1] // 2
    h = span // 2
    cut = half_cut(h)

    def kernel(flag_ref, l0, l1, r0, r1, *refs):
        outs, ls, rs, sem = refs[:5], *refs[5:]
        copies = [
            pltpu.make_async_copy(a, c.at[at : at + rows], sem.at[i])
            for i, (a, c, at) in enumerate(((l0, ls, 0), (l1, ls, rows), (r0, rs, 0), (r1, rs, rows)))
        ]
        for copy in copies:
            copy.start()
        wait_all(copies)
        first = flag_ref[0] == 0
        lo, hi = rs[:, :part], rs[:, part:]
        shares = (jnp.where(first, lo, hi), jnp.where(first, hi, lo))
        for yr in (0, 1):
            for xr in (0, 1):
                got = t_dot(ls[:, xr * span : (xr + 1) * span], shares[yr])
                if yr == 0 and xr == 0:
                    outs[0][...] = got
                    continue
                for side in (0, 1):
                    cols = slice(side * part, (side + 1) * part)
                    top, bottom = low16(got[side * h : side * h + cut]), low16(got[side * h + cut : (side + 1) * h])
                    if xr and yr:
                        outs[1][cut:, cols] = top
                        outs[2][h - cut :, cols] = bottom
                    elif xr:
                        outs[1][:cut, cols] = top
                        outs[3][:, cols] = bottom
                    else:
                        outs[2][: h - cut, cols] = bottom
                        outs[4][:, cols] = top

    outs = [shape((span, part), F32)]
    outs += [shape((n, 2 * part), BF) for n in (2 * cut, 2 * (h - cut), h - cut, cut)]
    scratch = [pltpu.VMEM((2 * rows, 2 * span), BF), pltpu.VMEM((2 * rows, 2 * part), BF), pltpu.SemaphoreType.DMA((4,))]
    args = [flags, *left, *right]
    flops = 16 * rows * span * part
    return call(kernel, name, outs, [SMEM] + [ANY] * 4, scratch, args, flops, 24, after)


def scatter_middle(name, beside, above, via_x, via_y, after=()):
    rest, double = beside.shape
    cut = above.shape[0]

    def kernel(beside_ref, above_ref, vx, vy, to_y, to_x):
        to_y[...] = low16(up32(above_ref[...]) + up32(vx[cut:, :]))
        to_x[...] = low16(up32(beside_ref[...]) + up32(vy[rest:, :]))

    outs = [shape((cut, double), BF), shape((rest, double), BF)]
    to_y, to_x = call(kernel, name, outs, [VMEM] * 4, [], [beside, above, via_x, via_y], 0, 16, after)
    return swap_y(to_y), swap_x(to_x)


def scatter_end(name, own, via_x, via_y, over_y, over_x, count, after=()):
    span, part = own.shape
    h = span // 2
    cut = half_cut(h)
    rest = h - cut
    each = span // count

    def kernel(own_ref, vx, vy, oy, ox, *refs):
        outs, total = refs[:count], refs[count]
        for side in (0, 1):
            cols = slice(side * part, (side + 1) * part)
            base = side * h
            total[base : base + cut] = own_ref[base : base + cut, :] + up32(vx[:cut, cols]) + up32(oy[:, cols])
            total[base + cut : base + h] = own_ref[base + cut : base + h, :] + up32(vy[:rest, cols]) + up32(ox[:, cols])
        for i, out in enumerate(outs):
            out[...] = total[i * each : (i + 1) * each]

    outs = [shape((each, part), F32)] * count
    scratch = [pltpu.VMEM((span, part), F32)]
    return call(kernel, name, outs, [VMEM] * 5, scratch, [own, via_x, via_y, over_y, over_x], 0, 24, after)


def gather_gains(shard, moves, dp_idx, x_idx, core):
    if not two_rows():
        return lax.all_gather(shard, ("dp", "tensor"), axis=1, tiled=True)
    beside, above, across = moves

    def pair(index, a, b):
        return jnp.where(index == 0, jnp.concatenate((a, b), axis=1), jnp.concatenate((b, a), axis=1))

    four = jnp.concatenate((shard, beside, above, across), axis=1)
    other = swap_core(four)
    n = shard.shape[1]
    by_core = [pair(core, four[:, i * n : (i + 1) * n], other[:, i * n : (i + 1) * n]) for i in range(4)]
    return pair(dp_idx, pair(x_idx, *by_core[:2]), pair(x_idx, *by_core[2:]))


def ties(*arrays):
    return list(lax.optimization_barrier(arrays))


def tie(a, *others):
    return ties(a, *others)[0]


def local(images, valid_len, query_weight, key_weight, value_weight, output_weight, up_weight, down_weight, norm_gains, cotangent):
    section = lax.axis_index("section")
    sections = lax.axis_size("section")
    dp_idx = lax.axis_index("dp")
    dp = lax.axis_size("dp")
    tensor_idx = lax.axis_index("tensor")
    x_idx, core = tensor_idx // 2, tensor_idx % 2
    per_dp, quarter, width = images.shape
    assert per_dp == 2 and lax.axis_size("tensor") == 4
    padded_quarter = (quarter + 7) // 8 * 8
    flags = jnp.stack((dp_idx, core, section, x_idx)).astype(jnp.int32)

    def pad_rows(a):
        return jnp.pad(a, ((0, padded_quarter - quarter), (0, 0)))

    def mine(a):
        return pad_rows(lax.dynamic_index_in_dim(a, x_idx, 0, keepdims=False))

    def theirs(a):
        return pad_rows(low16(lax.dynamic_index_in_dim(a, 1 - x_idx, 0, keepdims=False)))

    def give_back(rows):
        return swap_x(low16(rows[padded_quarter:]))

    def both_images(rows, got, after=()):
        def kernel(flag_ref, own_ref, got_ref, out):
            first = flag_ref[3] == 0
            own, other = own_ref[:quarter], up32(got_ref[...])[:quarter]
            out[:, 0, :] = jnp.where(first, own, other)
            out[:, 1, :] = jnp.where(first, other, own)

        outs = [shape((quarter, 2, width), F32)]
        pair = call(kernel, "both_images", outs, [SMEM, VMEM, VMEM], [], [flags, rows, got], 0, 16, after)[0]
        return pair

    rows = 2 * padded_quarter
    valid = lax.dynamic_index_in_dim(valid_len, x_idx, 0, keepdims=False)
    spot = jnp.arange(padded_quarter)
    live = [
        (spot < quarter) & ((2 * xx + cc) * quarter + spot < valid) for cc in (core, 1 - core) for xx in (x_idx, 1 - x_idx)
    ]
    bias = jnp.where(jnp.concatenate(live), 0.0, -1e30).astype(F32)[None, :]
    bias = jnp.broadcast_to(bias, (8, bias.shape[1]))

    span = query_weight.shape[2]
    units = up_weight.shape[2]
    part = width // dp
    plane = two_rows()

    gain_moves = [move(norm_gains[0]) for move in (swap_x, swap_y, swap_both)] if plane else []
    turned = [jnp.transpose(w[0]) for w in (query_weight, key_weight, value_weight)]
    packed, give_rows, keep_rows, (at_heads, at_up, at_down), h_units = pack(
        flags, [*turned, output_weight[0]], up_weight[0], jnp.transpose(down_weight[0]), jnp.transpose(images, (1, 0, 2)),
        padded_quarter,
    )
    h_heads = span // 2
    if plane:
        from_x, from_y = swap_x(packed), swap_y(packed)
        img_got = swap_x(give_rows)
        at = 2 * h_heads
        over_heads = [(swap_x(from_y[:at]), 0, at), (swap_y(from_x[at:at_up]), 0, at)]
        up_on, down_on = from_y[at_up:at_down], from_x[at_down:]
        over_up, over_down = [(swap_x(up_on), 0, h_units)], [(swap_y(down_on), 0, h_units)]
        cuts = [up_on, down_on]
        near = lambda row, rows: [[(packed, row, rows)], [(from_y, row, rows)]]
        far = lambda row, rows, over: [[(from_x, row, rows)], over]
    else:
        whole = lax.all_gather(packed, "dp")
        other = swap_x(whole)
        over_heads = over_up = over_down = None
        cuts = []
        img_got = swap_x(give_rows)
        near = lambda row, rows: [[(whole[i], row, rows)] for i in range(dp)]
        far = lambda row, rows, over: [[(other[i], row, rows)] for i in range(dp)]
    gains = gather_gains(norm_gains[0], gain_moves, dp_idx, x_idx, core)
    first_rows = jnp.concatenate((keep_rows, up32(img_got)), axis=0)
    first_far = swap_core(low16(first_rows))
    heads_near = put_together("heads_near", near(at_heads, 4 * h_heads), flags, 4, h_heads)
    up_near = put_together("up_near", near(at_up, h_units), flags, 1, h_units, [heads_near])[0]
    down_near = put_together("down_near", near(at_down, h_units), flags, 1, h_units, [heads_near])[0]
    heads_far = put_together("heads_far", far(at_heads, 4 * h_heads, over_heads), flags, 4, h_heads, [up_near, down_near, *cuts])
    heads = [heads_near, heads_far, swap_core(heads_near), swap_core(heads_far)]
    hidden, normed_b = layer_first(flags, first_rows, first_far, bias, gains, heads)
    up_near = [up_near, swap_core(up_near)]
    down_near = [down_near, swap_core(down_near)]
    act_near = feed_up(normed_b, up_near)
    half_out = feed_down(hidden, act_near, down_near, F32)
    up_far = put_together("up_far", far(at_up, h_units, over_up), flags, 1, h_units, [normed_b])[0]
    up_far = [up_far, swap_core(up_far)]
    down_far = put_together("down_far", far(at_down, h_units, over_down), flags, 1, h_units, [normed_b])[0]
    down_far = [down_far, swap_core(down_far)]
    act_far = feed_up(normed_b, up_far)
    out = feed_down(half_out, act_far, down_far, BF)

    def fetch(after):
        return settle(flags, after, heads, up_near + up_far, down_near + down_far)

    sources = [first_rows, first_far]
    for tick in range(1, sections):
        got = shift(out, 1)
        if tick == 1:
            weights, token = fetch(out)
            got, token = ties(got, token)
        sources += [got, swap_core(got)]
        if tick + 1 < sections:
            out = layer_mid(flags, *sources[-2:], bias, gains, *weights, [token] if tick == 1 else [])
            if tick == 1:
                cot_got = swap_x(theirs(cotangent))
    x, normed_a, q, kv = last_project(flags, sources, gains, weights[0])
    mix, mix_rest, lse, hidden, normed_b = last_attention(q, kv, bias, x, gains, weights[0])
    out, slope, hidden_grad, do, dy = feed_turn(hidden, normed_b, mine(cotangent), cot_got, gains, *weights)

    sources = [dy]
    acts_got = give_back(out)

    def core_halves(a):
        lo = jnp.concatenate((a[:, :span], a[:, 2 * span : 3 * span]), axis=1)
        hi = jnp.concatenate((a[:, span : 2 * span], a[:, 3 * span :]), axis=1)
        return jnp.where(core == 0, lo, hi), jnp.where(core == 0, hi, lo)

    at = half_cut(rows)

    at = half_cut(rows)
    for tick in range(sections):
        last = tick + 1 == sections
        if last:
            dy_low = low16(sources[0])
            for i, a in enumerate(sources[1:]):
                dy_low = jnp.where(section == sections - 2 - i, a, dy_low)
            if plane:
                dy_x0, dy_y1 = swap_x(dy_low[:at]), swap_y(dy_low[at:])
        if tick:
            mode = "last" if last else "mid"
            used, after = (sources, [act_all]) if last else (sources[-1:], [acts_got] if tick == 1 else [acts, nb_x1, nb_y0])
            results = feed_back(mode, flags, used, slope, hidden, gains, weights[0], up_near + up_far, weights[2], after)
            hidden_grad, do = results[:2]
        if last:
            mix_low, gain_sum_b = results[2:]
            mix_got, ml_far = swap_core(mix_give), swap_core(mix_low)
        after = []
        if plane and tick == 1:
            after = [nb_x0, nb_y1]
        if plane and tick == 2:
            after = [nb_d0, nb_d1]
        if plane and last:
            dy_d0, dy_d1 = swap_y(dy_x0), swap_x(dy_y1)
            after = [dy_x0, dy_y1]
        dq, dkv, dkv_far = attention_back(q, kv, do, mix, mix_rest, lse, bias, after)
        dkv_got = swap_core(dkv_far)
        after = []
        if plane and last:
            o_parts = plane_blocks("output_grads", flags, (mix_keep, mix_got), (mix_low, ml_far), [dq])
            o_via = swap_x(o_parts[1]), swap_y(o_parts[2])
            dy_rest = tie(dy_low, dq)
            dy_x1, dy_y0 = swap_x(dy_rest[at:]), swap_y(dy_rest[:at])
            after = [o_parts[0], dy_d0, dy_d1]
        if plane and tick == 2:
            nb_four = join("join_normed", [normed_b, nb_x0, nb_x1, nb_y0, nb_y1, nb_d0, nb_d1], [dq])
            after = [nb_four]
        back = qkv_back(last, flags, dq, dkv, dkv_got, x, hidden_grad, gains, weights[0], after)
        if last:
            break
        low = back[0]
        if plane and tick == 2:
            nb_four, low = ties(nb_four, low)
        got = shift(low, -1)
        if tick == 0:
            nb_x0 = nb_x1 = nb_y0 = nb_y1 = normed_b
            if plane:
                nb_x0, nb_y1 = swap_x(normed_b[:at]), swap_y(normed_b[at:])
        elif tick == 1:
            if plane:
                nb_x1, nb_y0 = swap_x(normed_b[at:]), swap_y(normed_b[:at])
                nb_d0, nb_d1 = swap_y(nb_x0), swap_x(nb_y1)
            acts = both_images(out, acts_got)
            mix_keep, mix_give = core_halves(mix)
            na_far = swap_core(normed_a)
        elif tick == 2:
            if plane:
                nb_far = swap_core(nb_four)
            else:
                nb_all = lax.all_gather(normed_b, ("dp", "tensor"), axis=0, tiled=True)
                nb_four, nb_far = jnp.split(nb_all, 2)
            act_all, slope_all = unit_forward(nb_four, nb_far, up_near[0], [mix_keep, mix_give, na_far])
            got, act_all = ties(got, act_all)
        sources.append(got)
    dx, _, keep, give, gain_sum_a = back

    got = swap_core(give)
    grads_got = give_back(dx)
    gain_sums = jnp.concatenate((gain_sum_a, gain_sum_b), axis=0)
    if plane:
        gain_moves = [move(gain_sums) for move in (swap_x, swap_y, swap_both)]
        qkv_parts = plane_blocks("qkv_grads", flags, (keep, got), (normed_a, na_far))
        via = swap_x(qkv_parts[1]), swap_y(qkv_parts[2])
        dy_four = join("join_dy", [dy_low, dy_x0, dy_x1, dy_y0, dy_y1, dy_d0, dy_d1], [qkv_parts[0]])
        dy_far = swap_core(dy_four)
        sides = [(nb_four, dy_four), (nb_far, dy_far)]
        grad_up = unit_sums("up_grads", flags, sides, slope_all, down_near[0], units, part, [qkv_parts[0]])
        over = scatter_middle("qkv_middle", *qkv_parts[3:], *via, [grad_up])
        o_over = scatter_middle("output_middle", *o_parts[3:], *o_via, [grad_up])
        grad_down = unit_sums("down_grads", flags, [(dy_four,), (dy_far,)], act_all, None, units, part, [grad_up, *gain_moves])
        gain_sums = gain_sums + gain_moves[0] + gain_moves[1] + gain_moves[2]
        gain_sums = gain_sums + swap_core(gain_sums)
        (grad_o,) = scatter_end("output_end", o_parts[0], *o_via, *o_over, 1, [grad_down])
        grad_heads = scatter_end("qkv_end", qkv_parts[0], *via, *over, 3, [grad_down])
        gain_shard = lax.dynamic_slice_in_dim(gain_sums, (dp_idx * 4 + tensor_idx) * (width // 8), width // 8, 1)
        grads_after = [grad_down]
    else:
        dy_all = lax.all_gather(dy_low, ("dp", "tensor"), axis=0, tiled=True)
        dy_four, dy_far = jnp.split(dy_all, 2)
        grad_up = unit_sums("up_grads", flags, [(nb_four, dy_four), (nb_far, dy_far)], slope_all, down_near[0], units, part)
        grad_down = unit_sums("down_grads", flags, [(dy_four,), (dy_far,)], act_all, None, units, part)
        grads_after = []
        both = lambda a, b: jnp.concatenate((a, b), axis=0)
        g = t_dot(both(keep, got), both(normed_a, na_far))
        g = g[: 3 * span] + up32(swap_x(low16(g[3 * span :])))
        g = up32(lax.psum_scatter(low16(g), "dp", scatter_dimension=1, tiled=True))
        grad_heads = [g[i * span : (i + 1) * span] for i in range(3)]
        g = t_dot(both(mix_keep, swap_core(mix_give)), both(mix_low, swap_core(mix_low)))
        g = g[:span] + up32(swap_x(low16(g[span:])))
        grad_o = up32(lax.psum_scatter(low16(g), "dp", scatter_dimension=1, tiled=True))
        gain_shard = lax.psum_scatter(gain_sums, ("dp", "tensor"), scatter_dimension=1, tiled=True)
    grads = both_images(dx, grads_got, grads_after)

    return (
        jnp.transpose(acts, (1, 0, 2))[None],
        jnp.transpose(grads, (1, 0, 2))[None],
        *[jnp.transpose(g)[None] for g in grad_heads],
        grad_o[None],
        grad_up[None],
        jnp.transpose(grad_down)[None],
        gain_shard[None],
    )


def solution(mesh):
    return jax.shard_map(
        local,
        mesh=mesh,
        in_specs=(
            P("dp", "tensor", None),
            P("dp"),
            P("section", "dp", "tensor"),
            P("section", "dp", "tensor"),
            P("section", "dp", "tensor"),
            P("section", "tensor", "dp"),
            P("section", "dp", "tensor"),
            P("section", "tensor", "dp"),
            P("section", None, ("dp", "tensor")),
            P("dp", "tensor", None),
        ),
        out_specs=(
            P("section", "dp", "tensor", None),
            P("section", "dp", "tensor", None),
            P("section", "dp", "tensor"),
            P("section", "dp", "tensor"),
            P("section", "dp", "tensor"),
            P("section", "tensor", "dp"),
            P("section", "dp", "tensor"),
            P("section", "tensor", "dp"),
            P("section", None, ("dp", "tensor")),
        ),
        check_vma=False,
    )
```

```python
import math

import jax
import jax.numpy as jnp
from jax import lax
from jax.experimental import pallas as pl
from jax.experimental.pallas import tpu as pltpu
from jax.sharding import PartitionSpec as P

HD = 72
EPS = 1e-06
SCALE = HD ** (-0.5)
LOG2E = 1.4426950408889634
BF = jnp.bfloat16
F32 = jnp.float32
WIN = 256
LANES = 128
COST = 0.1
ROOM = 28
K0 = 0.7978845608028654
K1 = 0.044715
VMEM = pl.BlockSpec(memory_space=pltpu.VMEM)
SMEM = pl.BlockSpec(memory_space=pltpu.SMEM)
ANY = pl.BlockSpec(memory_space=pl.ANY)


def swap_core(a):
    n = lax.axis_size("tensor")
    return lax.ppermute(a, "tensor", [(i, i ^ 1) for i in range(n)])


def swap_x(a):
    n = lax.axis_size("tensor")
    return lax.ppermute(a, "tensor", [(i, i ^ 2) for i in range(n)])


def swap_y(a):
    return lax.ppermute(a, "dp", [(0, 1), (1, 0)])


def swap_both(a):
    n = lax.axis_size("tensor")
    pairs = [(y * n + i, (1 - y) * n + (i ^ 2)) for y in (0, 1) for i in range(n)]
    return lax.ppermute(a, ("dp", "tensor"), pairs)


def shift(a, by):
    n = lax.axis_size("section")
    pairs = [(i, i + by) for i in range(n) if 0 <= i + by < n]
    return lax.ppermute(a, "section", pairs)


def two_rows():
    return lax.axis_size("dp") == 2


def half_cut(rows):
    return (rows // 2 + 15) // 16 * 16


def up32(a):
    return a.astype(F32)


def low16(a):
    return a.astype(BF)


def dot(a, b):
    return jnp.dot(a, b, preferred_element_type=F32)


def dot_t(a, b):
    return lax.dot_general(a, b, (((1,), (1,)), ((), ())), preferred_element_type=F32)


def t_dot(a, b):
    return lax.dot_general(a, b, (((0,), (0,)), ((), ())), preferred_element_type=F32)


def in_hbm(a):
    return pltpu.with_memory_space_constraint(a, pltpu.HBM)


def spans(total, size):
    return [(at, min(size, total - at)) for at in range(0, total, size)]


def norm_parts(values):
    centre = jnp.mean(values, axis=-1, keepdims=True)
    centred = values - centre
    spread = jnp.mean(centred * centred, axis=-1, keepdims=True)
    inverse = lax.rsqrt(spread + EPS)
    return centred * inverse, inverse


def norm_back(grad, unit, inverse, gain):
    e = grad * gain
    return inverse * (e - jnp.mean(e, axis=-1, keepdims=True) - unit * jnp.mean(e * unit, axis=-1, keepdims=True))


def span_copies(pieces, whole, sems, base):
    rows = pieces[0].shape[0]
    return [
        (pltpu.make_async_copy(piece, whole.at[i * rows : (i + 1) * rows], sems.at[base + i]), (i + 1) * rows)
        for i, piece in enumerate(pieces)
    ]


class Arrivals:
    def __init__(self, copies):
        self.left = list(copies)
        self.have = 0

    def start(self):
        for copy, _ in self.left:
            copy.start()

    def need(self, row):
        while self.left and self.have < row:
            copy, self.have = self.left.pop(0)
            copy.wait()

    def rest(self):
        self.need(1 << 30)


def gelu_one(u):
    return u * (0.5 + 0.5 * jnp.tanh(u * (K0 + (K0 * K1) * (u * u))))


def gelu_both(u):
    sq = u * u
    th = jnp.tanh(u * (K0 + (K0 * K1) * sq))
    half = 0.5 + 0.5 * th
    return u * half, half + (0.5 * u) * (1.0 - th * th) * (K0 + (3.0 * K1 * K0) * sq)


def head_window(h, width):
    tile = min(h * HD // LANES, width // LANES - WIN // LANES)
    off = h * HD - tile * LANES
    lane = lax.broadcasted_iota(jnp.int32, (1, WIN), 1)
    return slice(tile * LANES, tile * LANES + WIN), (lane >= off) & (lane < off + HD)


def shape(dims, dtype):
    return jax.ShapeDtypeStruct(dims, dtype)


def past(kernel, inputs, after):
    return lambda *refs: kernel(*refs[:inputs], *refs[inputs + len(after) :])


def call(kernel, name, outs, ins, scratch, args, flops, limit=60, after=(), cost=None):
    moved = sum(4 * math.prod(a.shape) for a in (*args, *outs))
    return pl.pallas_call(
        past(kernel, len(args), after),
        out_shape=tuple(outs),
        in_specs=[*ins, *[ANY] * len(after)],
        out_specs=tuple([VMEM] * len(outs)),
        scratch_shapes=scratch,
        compiler_params=pltpu.CompilerParams(vmem_limit_bytes=limit * 2**20),
        cost_estimate=pl.CostEstimate(flops=int(flops * (cost or COST)), bytes_accessed=int(moved * (cost or COST)), transcendentals=0),
        name=name,
    )(*args, *after)


def pack(flags, heads, up, down, pair, quarter):
    span, part = heads[0].shape
    units = up.shape[1]
    h = span // 2
    hu = (units + 31) // 32 * 16

    def kernel(flag_ref, *refs):
        pair_ref, out, give_ref, mine_ref, *held, sem = refs[6:]
        copies = [pltpu.make_async_copy(a, b, sem.at[i]) for i, (a, b) in enumerate(zip(refs[:6], held))]
        for copy in copies:
            copy.start()
        refs = held
        got = pair_ref.shape[0]
        first = flag_ref[3] == 0
        one, two = pair_ref[:, 0, :], pair_ref[:, 1, :]
        mine_ref[...] = jnp.zeros_like(mine_ref)
        mine_ref[:got] = jnp.where(first, one, two)
        give_ref[...] = jnp.zeros_like(give_ref)
        give_ref[:got] = low16(jnp.where(first, two, one))
        wait_all(copies)
        for i, ref in enumerate(refs[:4]):
            out[i * h : (i + 1) * h, :part] = ref[:h, :]
            out[i * h : (i + 1) * h, part:] = ref[h:, :]
        for i, ref in enumerate(refs[4:6]):
            base = 4 * h + i * hu
            rows = low16(up32(ref[...]).T)
            out[base : base + hu, :part] = rows[:hu]
            out[base : base + units - hu, part:] = rows[hu:]
            out[base + units - hu : base + hu, part:] = jnp.zeros((2 * hu - units, part), BF)

    total = 4 * h + 2 * hu
    width = pair.shape[2]
    outs = [shape((total, 2 * part), BF), shape((quarter, width), BF), shape((quarter, width), F32)]
    scratch = [pltpu.VMEM(a.shape, BF) for a in (*heads, up, down)] + [pltpu.SemaphoreType.DMA((6,))]
    args = [flags, *[in_hbm(a) for a in (*heads, up, down)], pair]
    got = call(kernel, "pack", outs, [SMEM] + [ANY] * 6 + [VMEM], scratch, args, 0, 34)
    return *got, (0, 4 * h, 4 * h + hu), hu


def put_together(name, pieces, flags, groups, h, after=()):
    count = len(pieces)
    parts = [(i, *p) for i, piece in enumerate(pieces) for p in piece]
    part = parts[0][1].shape[1] // 2
    width = part * count

    def kernel(flag_ref, *refs):
        out, held, sem = refs[len(parts) :]
        copies, at = [], [0] * count
        for j, (ref, (i, _, row, rows)) in enumerate(zip(refs, parts)):
            copies.append(pltpu.make_async_copy(ref.at[row : row + rows], held.at[i, at[i] : at[i] + rows], sem.at[j]))
            at[i] += rows
        for copy in copies:
            copy.start()
        wait_all(copies)
        first = flag_ref[0] == 0
        for i in range(count):
            for g in range(groups):
                rows = slice(g * h, (g + 1) * h)
                piece = jnp.where(first, held[i, rows], held[1 - i, rows]) if count == 2 else held[i, rows]
                out[g, :h, i * part : (i + 1) * part] = piece[:, :part]
                out[g, h:, i * part : (i + 1) * part] = piece[:, part:]

    scratch = [pltpu.VMEM((count, groups * h, 2 * part), BF), pltpu.SemaphoreType.DMA((len(parts),))]
    outs = [shape((groups, 2 * h, width), BF)]
    args = [flags, *[in_hbm(p[1]) for p in parts]]
    return call(kernel, name, outs, [SMEM] + [ANY] * len(parts), scratch, args, 0, 24, after)[0]


def head_copies(pieces, core, kinds, whole, sems, base):
    span, width = pieces[0].shape[1], pieces[0].shape[2]
    out = []
    for n, kind in enumerate(kinds):
        group = []
        for i, piece in enumerate(pieces):
            c = core if i < 2 else 1 - core
            at = pl.multiple_of(n * width + (2 * (i % 2) + c) * span, span)
            sem = sems.at[base + 4 * n + i]
            group.append(pltpu.make_async_copy(piece.at[kind], whole.at[pl.ds(at, span)], sem))
        out.append(group)
    return out


def wait_all(copies):
    for copy in copies:
        copy.wait()


def attend(q, kv, bias, mix, rest, lse_ref):
    rows, width = q.shape
    lane = lax.broadcasted_iota(jnp.int32, (1, LANES), 1)
    for h in range(width // HD):
        win, live = head_window(h, width)
        keys = jnp.where(live, kv[:, win], jnp.zeros((), BF))
        vals = kv[:, width + win.start : width + win.stop]
        s = dot_t(q[:, win], keys) * (SCALE * LOG2E) + bias
        top = jnp.max(s, axis=-1, keepdims=True)
        p = jnp.exp2(s - top)
        total = jnp.sum(p, axis=-1, keepdims=True)
        o = dot(low16(p), vals) * (1.0 / total)
        o_low = low16(o)
        mix[:, win] = jnp.where(live, o_low, mix[:, win])
        if rest is not None:
            rest[:, win] = jnp.where(live, low16(o - up32(o_low)), rest[:, win])
            lse_ref[...] = jnp.where(lane == h, top + jnp.log2(total), lse_ref[...])


def feed_up(normed, pieces, after=()):
    rows, width = normed.shape
    units = sum(piece.shape[0] for piece in pieces)
    n = len(pieces)

    def kernel(nb_ref, *refs):
        act, w, sem = refs[n:]
        arrivals = Arrivals(span_copies(refs[:n], w, sem, 0))
        arrivals.start()
        for at, k in spans(units, 512):
            arrivals.need(at + k)
            act[:, at : at + k] = low16(gelu_one(dot_t(nb_ref[...], w[at : at + k, :])))

    scratch = [pltpu.VMEM((units, width), BF), pltpu.SemaphoreType.DMA((n,))]
    outs = [shape((rows, units), BF)]
    return call(kernel, "feed_up", outs, [VMEM] + [ANY] * n, scratch, [normed, *pieces], 2 * rows * width * units, 30, after)[0]


def feed_down(base, act, pieces, out_type, after=()):
    rows, width = base.shape
    units = act.shape[1]
    n = len(pieces)

    def kernel(base_ref, act_ref, *refs):
        out, w, sem = refs[n:]
        arrivals = Arrivals(span_copies(refs[:n], w, sem, 0))
        arrivals.start()
        arrivals.rest()
        for at, k in spans(width, 256):
            out[:, at : at + k] = (base_ref[:, at : at + k] + dot(act_ref[...], w[:, at : at + k])).astype(out.dtype)

    scratch = [pltpu.VMEM((units, width), BF), pltpu.SemaphoreType.DMA((n,))]
    outs = [shape((rows, width), out_type)]
    args = [base, act, *pieces]
    return call(kernel, "feed_down", outs, [VMEM, VMEM] + [ANY] * n, scratch, args, 2 * rows * width * units, 30, after)[0]


def project(nall, w, q, kv):
    rows, width = q.shape
    for at, n in spans(width, 512):
        q[:, at : at + n] = low16(dot_t(nall[:rows], w[width + at : width + at + n, :]))
    for at, n in spans(2 * width, 512):
        kv[:, at : at + n] = low16(dot_t(nall[...], w[2 * width + at : 2 * width + at + n, :]))


def layer_first(flags, rows32, far, bias, gains, heads):
    rows, width = rows32.shape

    def kernel(flag_ref, bias_ref, gain_ref, x_ref, far_ref, *refs):
        heads_r, hid_ref, nb_ref, w, nall, q, kv, mix, sem = refs[:4], *refs[4:]
        groups = head_copies(heads_r, flag_ref[1], (3, 0, 1, 2), w, sem, 0)
        for group in groups:
            for copy in group:
                copy.start()
        gain_a, gain_b = gain_ref[0:1, :], gain_ref[1:2, :]
        nall[:rows] = low16(norm_parts(x_ref[...])[0] * gain_a)
        nall[rows:] = low16(norm_parts(up32(far_ref[...]))[0] * gain_a)
        for group in groups:
            wait_all(group)
        project(nall, w, q, kv)
        mix[...] = jnp.zeros_like(mix)
        attend(q, kv, bias_ref[0:1, :], mix, None, None)
        hidden = x_ref[...] + dot(mix[...], w[:width, :])
        hid_ref[...] = hidden
        nb_ref[...] = low16(norm_parts(hidden)[0] * gain_b)

    scratch = [
        pltpu.VMEM((4 * width, width), BF),
        pltpu.VMEM((2 * rows, width), BF),
        pltpu.VMEM((rows, width), BF),
        pltpu.VMEM((2 * rows, 2 * width), BF),
        pltpu.VMEM((rows, width), BF),
        pltpu.SemaphoreType.DMA((16,)),
    ]
    outs = [shape((rows, width), F32), shape((rows, width), BF)]
    ins = [SMEM] + [VMEM] * 4 + [ANY] * 4
    flops = 16 * rows * 2 * rows * WIN * 4 + 12 * rows * width * width
    return call(kernel, "layer_first", outs, ins, scratch, [flags, bias, gains, rows32, far, *heads], flops, 44, (), 0.001)


def settle(flags, after, heads, ups, downs):
    kinds, span, width = heads[0].shape
    units = 4 * ups[0].shape[0]

    def kernel(flag_ref, *refs):
        wh, wu, wd, token, sem = refs[13:]
        copies = sum(head_copies(refs[:4], flag_ref[1], (3, 0, 1, 2), wh, sem, 0), [])
        copies += [copy for copy, _ in span_copies(refs[4:8], wu, sem, 16) + span_copies(refs[8:12], wd, sem, 20)]
        for copy in copies:
            copy.start()
        token[...] = jnp.zeros_like(token)
        wait_all(copies)

    pieces = [pltpu.with_memory_space_constraint(a, pltpu.HBM) for a in (*heads, *ups, *downs)]
    wh, wu, wd, token = pl.pallas_call(
        kernel,
        out_shape=(
            pltpu.VMEM((kinds * 4 * span, width), BF),
            pltpu.VMEM((units, width), BF),
            pltpu.VMEM((units, width), BF),
            shape((8, LANES), F32),
        ),
        in_specs=[SMEM] + [ANY] * 13,
        out_specs=(ANY, ANY, ANY, VMEM),
        scratch_shapes=[pltpu.SemaphoreType.DMA((24,))],
        compiler_params=pltpu.CompilerParams(vmem_limit_bytes=ROOM * 2**20),
        cost_estimate=pl.CostEstimate(flops=0, bytes_accessed=int(60 * COST * 2**20), transcendentals=0),
        name="settle",
    )(flags, *pieces, after)
    return [pltpu.with_memory_space_constraint(a, pltpu.VMEM) for a in (wh, wu, wd)], token


def feed(normed, hidden, w_up, w_down, act, slope_out, out):
    for at, n in spans(w_up.shape[0], 512):
        u = dot_t(normed, w_up[at : at + n, :])
        if slope_out is None:
            act[:, at : at + n] = low16(gelu_one(u))
        else:
            a, slope = gelu_both(u)
            act[:, at : at + n] = low16(a)
            slope_out[:, at : at + n] = low16(slope)
    for at, n in spans(w_down.shape[1], 256):
        out[:, at : at + n] = (hidden[:, at : at + n] + dot(act[...], w_down[:, at : at + n])).astype(out.dtype)


def layer_mid(flags, own, far, bias, gains, w_heads, w_up, w_down, after=()):
    rows, width = own.shape
    units = w_up.shape[0]

    def kernel(bias_ref, gain_ref, wh, wu, wd, own_ref, far_ref, out_ref, x_ref, q, kv, mix, hid_ref, nall, act):
        gain_a, gain_b = gain_ref[0:1, :], gain_ref[1:2, :]
        x_ref[...] = up32(own_ref[...])
        nall[:rows] = low16(norm_parts(x_ref[...])[0] * gain_a)
        nall[rows:] = low16(norm_parts(up32(far_ref[...]))[0] * gain_a)
        project(nall, wh, q, kv)
        mix[...] = jnp.zeros_like(mix)
        attend(q, kv, bias_ref[0:1, :], mix, None, None)
        hidden = x_ref[...] + dot(mix[...], wh[:width, :])
        hid_ref[...] = hidden
        feed(low16(norm_parts(hidden)[0] * gain_b), hid_ref, wu, wd, act, None, out_ref)

    scratch = [
        pltpu.VMEM((rows, width), F32),
        pltpu.VMEM((rows, width), BF),
        pltpu.VMEM((2 * rows, 2 * width), BF),
        pltpu.VMEM((rows, width), BF),
        pltpu.VMEM((rows, width), F32),
        pltpu.VMEM((2 * rows, width), BF),
        pltpu.VMEM((rows, units), BF),
    ]
    flops = 16 * rows * 2 * rows * WIN * 4 + 12 * rows * width * width + 4 * rows * width * units
    args = [bias, gains, w_heads, w_up, w_down, own, far]
    return call(kernel, "layer_mid", [shape((rows, width), BF)], [VMEM] * 7, scratch, args, flops, ROOM, after)[0]


def last_project(flags, sources, gains, w_heads):
    rows, width = sources[0].shape
    sections = len(sources) // 2

    def kernel(flag_ref, gain_ref, wh, *refs):
        src, refs = refs[: len(sources)], refs[len(sources) :]
        x_ref, na_ref, q, kv, nall, sem = refs

        def load(i, go):
            own, far = src[2 * i], src[2 * i + 1]
            near = pltpu.make_async_copy(own, x_ref if own.dtype == F32 else na_ref, sem.at[0])
            other = pltpu.make_async_copy(far, nall.at[rows:], sem.at[1])
            for copy in (near, other):
                if go:
                    copy.start()
                else:
                    copy.wait()
            if not go and own.dtype != F32:
                x_ref[...] = up32(na_ref[...])

        for go in (True, False):
            for i in range(sections):
                pl.when(flag_ref[2] == i)(lambda i=i, go=go: load(i, go))
        gain_a = gain_ref[0:1, :]
        normed = low16(norm_parts(x_ref[...])[0] * gain_a)
        na_ref[...] = normed
        nall[:rows] = normed
        nall[rows:] = low16(norm_parts(up32(nall[rows:]))[0] * gain_a)
        project(nall, wh, q, kv)

    row32, row16 = shape((rows, width), F32), shape((rows, width), BF)
    outs = [row32, row16, row16, shape((2 * rows, 2 * width), BF)]
    scratch = [pltpu.VMEM((2 * rows, width), BF), pltpu.SemaphoreType.DMA((2,))]
    ins = [SMEM, VMEM, VMEM] + [ANY] * len(sources)
    args = [flags, gains, w_heads, *[in_hbm(a) for a in sources]]
    return call(kernel, "last_project", outs, ins, scratch, args, 10 * rows * width * width, 12)


def last_attention(q, kv, bias, x, gains, w_heads, after=()):
    rows, width = q.shape

    def kernel(q_ref, kv_ref, bias_ref, x_ref, gain_ref, wh, mix, rest_ref, lse_ref, hid_ref, nb_ref):
        mix[...] = jnp.zeros_like(mix)
        lse_ref[...] = jnp.zeros_like(lse_ref)
        rest_ref[...] = jnp.zeros_like(rest_ref)
        attend(q_ref, kv_ref, bias_ref[0:1, :], mix, rest_ref, lse_ref)
        hidden = x_ref[...] + dot(mix[...], wh[:width, :])
        hid_ref[...] = hidden
        nb_ref[...] = low16(norm_parts(hidden)[0] * gain_ref[1:2, :])

    row32, row16 = shape((rows, width), F32), shape((rows, width), BF)
    outs = [row16, row16, shape((rows, LANES), F32), row32, row16]
    flops = 16 * rows * 2 * rows * WIN * 4 + 2 * rows * width * width
    return call(kernel, "last_attention", outs, [VMEM] * 6, [], [q, kv, bias, x, gains, w_heads], flops, 18, after)


def feed_turn(hidden, normed, dy_own, dy_got, gains, w_heads, w_up, w_down):
    rows, width = hidden.shape
    units = w_up.shape[0]

    half = dy_own.shape[0]

    def kernel(hid_ref, nb_ref, own_ref, got_ref, gain_ref, wh, wu, wd, out_ref, slope_ref, hg_ref, do_ref, dy_ref, act, nbg):
        dy_ref[:half] = own_ref[...]
        dy_ref[half:] = up32(got_ref[...])
        feed(nb_ref[...], hid_ref, wu, wd, act, slope_ref, out_ref)
        feed_grads(low16(dy_ref[...]), slope_ref, wu, wd, act, nbg)
        unit, inverse = norm_parts(hid_ref[...])
        hidden_grad = dy_ref[...] + norm_back(nbg[...], unit, inverse, gain_ref[1:2, :])
        hg_ref[...] = hidden_grad
        do_ref[...] = low16(dot_t(low16(hidden_grad), wh[:width, :]))

    row32 = shape((rows, width), F32)
    outs = [row32, shape((rows, units), BF), row32, shape((rows, width), BF), row32]
    scratch = [pltpu.VMEM((rows, units), BF), pltpu.VMEM((rows, width), F32)]
    flops = 8 * rows * width * units
    args = [hidden, normed, dy_own, dy_got, gains, w_heads, w_up, w_down]
    return call(kernel, "feed_turn", outs, [VMEM] * 8, scratch, args, flops, 22)


def feed_grads(low, slope_ref, w_up, w_down, inner, out, ups=()):
    for at, n in spans(w_up.shape[0], 512):
        inner[:, at : at + n] = low16(dot_t(low, w_down[at : at + n, :]) * up32(slope_ref[:, at : at + n]))
    wait_all(ups)
    for at, n in spans(w_up.shape[1], 256):
        out[:, at : at + n] = dot(inner[...], w_up[:, at : at + n])


def feed_back(mode, flags, sources, slope, hidden, gains, w_heads, w_ups, w_down, after=()):
    last = mode == "last"
    rows, width = hidden.shape
    units = w_down.shape[0]
    n_up = len(w_ups)

    def kernel(flag_ref, gain_ref, hid_ref, slope_ref, wh, wd, *refs):
        *refs, wu, up_sem = refs
        ups = [copy for copy, _ in span_copies(refs[:n_up], wu, up_sem, 0)]
        for copy in ups:
            copy.start()
        refs = refs[n_up:]
        src, refs = refs[: len(sources)], refs[len(sources) :]
        hg_ref, do_ref, refs = refs[0], refs[1], refs[2:]
        if last:
            ml_ref, gs_ref, ig, nbg, dy_ref, low, sem = refs

            def load(a, go):
                copy = pltpu.make_async_copy(a, dy_ref if a.dtype == F32 else low, sem.at[0])
                if go:
                    copy.start()
                    return
                copy.wait()
                if a.dtype == F32:
                    low[...] = low16(dy_ref[...])
                else:
                    dy_ref[...] = up32(low[...])

            for go in (True, False):
                for i, a in enumerate(src):
                    pl.when(flag_ref[2] == len(src) - 1 - i)(lambda a=a, go=go: load(a, go))
        else:
            ig, nbg, dy_ref, low = refs
            dy_ref[...] = src[0][...].astype(F32)
            low[...] = low16(src[0][...])
        feed_grads(low[...], slope_ref, wu, wd, ig, nbg, ups)
        unit, inverse = norm_parts(hid_ref[...])
        grad = nbg[...]
        if last:
            gs_ref[...] = jnp.sum(grad * unit, axis=0, keepdims=True)
        hidden_grad = dy_ref[...] + norm_back(grad, unit, inverse, gain_ref[1:2, :])
        hg_ref[...] = hidden_grad
        mix_low = low16(hidden_grad)
        if last:
            ml_ref[...] = mix_low
        do_ref[...] = low16(dot_t(mix_low, wh[:width, :]))

    sources = [in_hbm(a) if last else a for a in sources]
    args = [flags, gains, hidden, slope, w_heads, w_down, *[in_hbm(a) for a in w_ups], *sources]
    outs = [shape((rows, width), F32), shape((rows, width), BF)]
    if last:
        outs += [shape((rows, width), BF), shape((1, width), F32)]
    scratch = [
        pltpu.VMEM((rows, units), BF),
        pltpu.VMEM((rows, width), F32),
        pltpu.VMEM((rows, width), F32),
        pltpu.VMEM((rows, width), BF),
    ]
    if last:
        scratch.append(pltpu.SemaphoreType.DMA((1,)))
    scratch += [pltpu.VMEM((units, width), BF), pltpu.SemaphoreType.DMA((n_up,))]
    ins = [SMEM] + [VMEM] * 5 + [ANY] * n_up + [ANY if last else VMEM] * len(sources)
    flops = 4 * rows * width * units + 2 * rows * width * width
    return call(kernel, "feed_back_" + mode, outs, ins, scratch, args, flops, 24, after)


def attention_back(q, kv_all, do, mix, mix_rest, lse, bias, after=()):
    rows, width = q.shape
    keys_n = 2 * rows

    def kernel(q_ref, kv, do_ref, o_ref, rest_ref, lse_ref, bias_ref, dq_ref, dkv_own, dkv_far, qt, dt, dkt, dvt):
        bias_row = bias_ref[0:1, :]
        qt[...] = q_ref[...].T
        dt[...] = do_ref[...].T
        dq_ref[...] = jnp.zeros_like(dq_ref)
        zero = jnp.zeros((), BF)
        parts = ([], [])
        for h in range(width // HD):
            win, live = head_window(h, width)
            keys = jnp.where(live, kv[:, win], zero)
            vals = jnp.where(live, kv[:, width + win.start : width + win.stop], zero)
            d_out = do_ref[:, win]
            whole = up32(o_ref[:, win]) + up32(rest_ref[:, win])
            row_dot = jnp.sum(jnp.where(live, up32(d_out) * whole, 0.0), axis=-1, keepdims=True)
            s = dot_t(q_ref[:, win], keys) * (SCALE * LOG2E) + bias_row
            p = jnp.exp2(s - lse_ref[:, h : h + 1])
            ds = low16(p * (dot_t(d_out, vals) - row_dot))
            dq = dot(ds, keys) * SCALE
            dq_ref[:, win] = jnp.where(live, low16(dq), dq_ref[:, win])
            row = h % 2 * HD
            pair = slice((h - h % 2) * HD, (h - h % 2 + 2) * HD)
            parts[0].append(low16(dot(qt[pair, :][row : row + HD], ds) * SCALE))
            parts[1].append(low16(dot(dt[pair, :][row : row + HD], low16(p))))
            if h % 2:
                dkt[pair, :] = jnp.concatenate(parts[0], axis=0)
                dvt[pair, :] = jnp.concatenate(parts[1], axis=0)
                parts = ([], [])
        dk = dkt[...].T
        dv = dvt[...].T
        dkv_own[:, :width] = dk[:rows]
        dkv_own[:, width:] = dv[:rows]
        dkv_far[:, :width] = dk[rows:]
        dkv_far[:, width:] = dv[rows:]

    outs = [shape((rows, width), BF), shape((rows, 2 * width), BF), shape((rows, 2 * width), BF)]
    scratch = [
        pltpu.VMEM((width, rows), BF),
        pltpu.VMEM((width, rows), BF),
        pltpu.VMEM((width, keys_n), BF),
        pltpu.VMEM((width, keys_n), BF),
    ]
    flops = 16 * rows * keys_n * WIN * 10
    return call(kernel, "attention_back", outs, [VMEM] * 7, scratch, [q, kv_all, do, mix, mix_rest, lse, bias], flops, 17, after)


def qkv_back(full, flags, dq, own, got, x, hidden_grad, gains, w_heads, after=()):
    rows, width = dq.shape
    span = width // 4

    def kernel(flag_ref, gain_ref, dq_ref, own_ref, got_ref, x_ref, hg_ref, w, *refs):
        if full:
            dx_ref, low_ref, keep_ref, give_ref, gs_ref, grads, nag = refs
        else:
            low_ref, grads, nag = refs
        grads[:, :width] = dq_ref[...]
        grads[:, width:] = low16(up32(own_ref[...]) + up32(got_ref[...]))
        if full:
            mine = flag_ref[1] == 0
            for i in range(3):
                for xr in (0, 1):
                    at = i * width + 2 * xr * span
                    lo = grads[:, at : at + span]
                    hi = grads[:, at + span : at + 2 * span]
                    to = xr * 3 * span + i * span
                    keep_ref[:, to : to + span] = jnp.where(mine, lo, hi)
                    give_ref[:, to : to + span] = jnp.where(mine, hi, lo)
        for at, n in spans(width, 256):
            nag[:, at : at + n] = dot(grads[...], w[width:, at : at + n])
        unit, inverse = norm_parts(x_ref[...])
        grad = nag[...]
        if full:
            gs_ref[...] = jnp.sum(grad * unit, axis=0, keepdims=True)
        dx = hg_ref[...] + norm_back(grad, unit, inverse, gain_ref[0:1, :])
        low_ref[...] = low16(dx)
        if full:
            dx_ref[...] = dx

    outs = [shape((rows, width), BF)]
    if full:
        outs = [shape((rows, width), F32)] + outs
        outs += [shape((rows, 6 * span), BF), shape((rows, 6 * span), BF), shape((1, width), F32)]
    scratch = [pltpu.VMEM((rows, 3 * width), BF), pltpu.VMEM((rows, width), F32)]
    args = [flags, gains, dq, own, got, x, hidden_grad, w_heads]
    return call(kernel, "qkv_back", outs, [SMEM] + [VMEM] * 7, scratch, args, 6 * rows * width * width, 11, after)


def halves_of(total):
    steps = max(1, total // 736)
    return steps, total // steps


def halves_specs(steps, block, cols):
    return [
        pl.BlockSpec((block, cols), lambda i: (jnp.minimum(i, steps - 1), 0)),
        pl.BlockSpec((block, cols), lambda i: (jnp.maximum(i, steps) - steps, 0)),
    ]


def unit_forward(normed_four, normed_far, w_up, after=()):
    total, width = normed_four.shape
    n = w_up.shape[0]
    half, block = halves_of(total)

    def kernel(a_ref, b_ref, wu_ref, act_ref, slope_ref):
        def rows(nb_ref):
            for at, k in spans(n, 512):
                act, slope = gelu_both(dot_t(nb_ref[...], wu_ref[at : at + k, :]))
                act_ref[:, at : at + k] = low16(act)
                slope_ref[:, at : at + k] = low16(slope)

        pl.when(pl.program_id(0) < half)(lambda: rows(a_ref))
        pl.when(pl.program_id(0) >= half)(lambda: rows(b_ref))

    by_rows = pl.BlockSpec((block, n), lambda i: (i, 0))
    return pl.pallas_call(
        past(kernel, 3, after),
        grid=(2 * half,),
        in_specs=[*halves_specs(half, block, width), VMEM, *[ANY] * len(after)],
        out_specs=(by_rows, by_rows),
        out_shape=(pltpu.HBM((2 * total, n), BF), pltpu.HBM((2 * total, n), BF)),
        compiler_params=pltpu.CompilerParams(vmem_limit_bytes=18 * 2**20),
        cost_estimate=pl.CostEstimate(flops=int(5.6 * COST * total * width * n), bytes_accessed=int(12 * COST * total * width), transcendentals=0),
        name="unit_forward",
    )(normed_four, normed_far, w_up, *after)


def pick_cols(a, which, part):
    picked = a[:, :part]
    for i in range(1, a.shape[1] // part):
        picked = jnp.where(which == i, a[:, i * part : (i + 1) * part], picked)
    return picked


def unit_sums(name, flags, sides, saved, w_down, units, part, after=()):
    total, width = sides[0][0].shape
    n = saved.shape[1]
    steps = max(1, total // 736)
    block = total // steps
    all_steps = steps * len(sides)
    kinds = len(sides[0])
    flat = [a for side in sides for a in side]
    with_w = w_down is not None

    def kernel(flag_ref, *refs):
        if with_w:
            wd_ref, refs = refs[0], refs[1:]
        saved_hbm, refs = refs[0], refs[1:]
        rows_hbm, refs = refs[: len(flat)], refs[len(flat) :]
        out, held, sems = refs[0], refs[1 : 2 + kinds], refs[2 + kinds]

        def into(i):
            rows = slice(i % steps * block, (i % steps + 1) * block)
            sources = [rows_hbm[i // steps * kinds + j].at[rows] for j in range(kinds)]
            sources.append(saved_hbm.at[i * block : (i + 1) * block])
            return [pltpu.make_async_copy(a, b.at[i % 2], sems.at[j, i % 2]) for j, (a, b) in enumerate(zip(sources, held))]

        for copy in into(0):
            copy.start()
        for i in range(all_steps):
            if i + 1 < all_steps:
                for copy in into(i + 1):
                    copy.start()
            wait_all(into(i))
            turned = pick_cols(held[0][i % 2], flag_ref[0], part).T
            for at, k in spans(n, 512):
                right = held[kinds][i % 2, :, at : at + k]
                if with_w:
                    right = low16(dot_t(held[1][i % 2], wd_ref[at : at + k, :]) * up32(right))
                real = min(k, units - at)
                cols = slice(at, at + real)
                got = dot(turned, right)[:, :real]
                out[:, cols] = got if i == 0 else out[:, cols] + got

    scratch = [pltpu.VMEM((2, block, width), BF)] * kinds + [pltpu.VMEM((2, block, n), BF)]
    scratch.append(pltpu.SemaphoreType.DMA((kinds + 1, 2)))
    args = [flags, *([w_down] if with_w else []), in_hbm(saved), *[in_hbm(a) for a in flat]]
    ins = [SMEM] + [VMEM] * with_w + [ANY] * (1 + len(flat))
    flops = (4 if with_w else 2) * total * len(sides) * width * n
    return call(kernel, name, [shape((part, units), F32)], ins, scratch, args, flops, 40, after, 0.2)[0]


def join(name, pieces, after=()):
    n = len(pieces)

    def kernel(*refs):
        out, at = refs[n], 0
        for ref in refs[:n]:
            out[at : at + ref.shape[0]] = ref[...]
            at += ref.shape[0]

    rows = sum(a.shape[0] for a in pieces)
    return call(kernel, name, [pltpu.HBM((rows, pieces[0].shape[1]), BF)], [VMEM] * n, [], list(pieces), 0, 16, after)[0]


def plane_blocks(name, flags, left, right, after=()):
    rows = left[0].shape[0]
    part = right[0].shape[1] // 2
    span = left[0].shape[1] // 2
    h = span // 2
    cut = half_cut(h)

    def kernel(flag_ref, l0, l1, r0, r1, *refs):
        outs, ls, rs, sem = refs[:5], *refs[5:]
        copies = [
            pltpu.make_async_copy(a, c.at[at : at + rows], sem.at[i])
            for i, (a, c, at) in enumerate(((l0, ls, 0), (l1, ls, rows), (r0, rs, 0), (r1, rs, rows)))
        ]
        for copy in copies:
            copy.start()
        wait_all(copies)
        first = flag_ref[0] == 0
        lo, hi = rs[:, :part], rs[:, part:]
        shares = (jnp.where(first, lo, hi), jnp.where(first, hi, lo))
        for yr in (0, 1):
            for xr in (0, 1):
                got = t_dot(ls[:, xr * span : (xr + 1) * span], shares[yr])
                if yr == 0 and xr == 0:
                    outs[0][...] = got
                    continue
                for side in (0, 1):
                    cols = slice(side * part, (side + 1) * part)
                    top, bottom = low16(got[side * h : side * h + cut]), low16(got[side * h + cut : (side + 1) * h])
                    if xr and yr:
                        outs[1][cut:, cols] = top
                        outs[2][h - cut :, cols] = bottom
                    elif xr:
                        outs[1][:cut, cols] = top
                        outs[3][:, cols] = bottom
                    else:
                        outs[2][: h - cut, cols] = bottom
                        outs[4][:, cols] = top

    outs = [shape((span, part), F32)]
    outs += [shape((n, 2 * part), BF) for n in (2 * cut, 2 * (h - cut), h - cut, cut)]
    scratch = [pltpu.VMEM((2 * rows, 2 * span), BF), pltpu.VMEM((2 * rows, 2 * part), BF), pltpu.SemaphoreType.DMA((4,))]
    args = [flags, *left, *right]
    flops = 16 * rows * span * part
    return call(kernel, name, outs, [SMEM] + [ANY] * 4, scratch, args, flops, 24, after)


def scatter_middle(name, beside, above, via_x, via_y, after=()):
    rest, double = beside.shape
    cut = above.shape[0]

    def kernel(beside_ref, above_ref, vx, vy, to_y, to_x):
        to_y[...] = low16(up32(above_ref[...]) + up32(vx[cut:, :]))
        to_x[...] = low16(up32(beside_ref[...]) + up32(vy[rest:, :]))

    outs = [shape((cut, double), BF), shape((rest, double), BF)]
    to_y, to_x = call(kernel, name, outs, [VMEM] * 4, [], [beside, above, via_x, via_y], 0, 16, after)
    return swap_y(to_y), swap_x(to_x)


def scatter_end(name, own, via_x, via_y, over_y, over_x, count, after=()):
    span, part = own.shape
    h = span // 2
    cut = half_cut(h)
    rest = h - cut
    each = span // count

    def kernel(own_ref, vx, vy, oy, ox, *refs):
        outs, total = refs[:count], refs[count]
        for side in (0, 1):
            cols = slice(side * part, (side + 1) * part)
            base = side * h
            total[base : base + cut] = own_ref[base : base + cut, :] + up32(vx[:cut, cols]) + up32(oy[:, cols])
            total[base + cut : base + h] = own_ref[base + cut : base + h, :] + up32(vy[:rest, cols]) + up32(ox[:, cols])
        for i, out in enumerate(outs):
            out[...] = total[i * each : (i + 1) * each]

    outs = [shape((each, part), F32)] * count
    scratch = [pltpu.VMEM((span, part), F32)]
    return call(kernel, name, outs, [VMEM] * 5, scratch, [own, via_x, via_y, over_y, over_x], 0, 24, after)


def gather_gains(shard, moves, dp_idx, x_idx, core):
    if not two_rows():
        return lax.all_gather(shard, ("dp", "tensor"), axis=1, tiled=True)
    beside, above, across = moves

    def pair(index, a, b):
        return jnp.where(index == 0, jnp.concatenate((a, b), axis=1), jnp.concatenate((b, a), axis=1))

    four = jnp.concatenate((shard, beside, above, across), axis=1)
    other = swap_core(four)
    n = shard.shape[1]
    by_core = [pair(core, four[:, i * n : (i + 1) * n], other[:, i * n : (i + 1) * n]) for i in range(4)]
    return pair(dp_idx, pair(x_idx, *by_core[:2]), pair(x_idx, *by_core[2:]))


def ties(*arrays):
    return list(lax.optimization_barrier(arrays))


def tie(a, *others):
    return ties(a, *others)[0]


def local(images, valid_len, query_weight, key_weight, value_weight, output_weight, up_weight, down_weight, norm_gains, cotangent):
    section = lax.axis_index("section")
    sections = lax.axis_size("section")
    dp_idx = lax.axis_index("dp")
    dp = lax.axis_size("dp")
    tensor_idx = lax.axis_index("tensor")
    x_idx, core = tensor_idx // 2, tensor_idx % 2
    per_dp, quarter, width = images.shape
    assert per_dp == 2 and lax.axis_size("tensor") == 4
    padded_quarter = (quarter + 7) // 8 * 8
    flags = jnp.stack((dp_idx, core, section, x_idx)).astype(jnp.int32)

    def pad_rows(a):
        return jnp.pad(a, ((0, padded_quarter - quarter), (0, 0)))

    def mine(a):
        return pad_rows(lax.dynamic_index_in_dim(a, x_idx, 0, keepdims=False))

    def theirs(a):
        return pad_rows(low16(lax.dynamic_index_in_dim(a, 1 - x_idx, 0, keepdims=False)))

    def give_back(rows):
        return swap_x(low16(rows[padded_quarter:]))

    def both_images(rows, got, after=()):
        def kernel(flag_ref, own_ref, got_ref, out):
            first = flag_ref[3] == 0
            own, other = own_ref[:quarter], up32(got_ref[...])[:quarter]
            out[:, 0, :] = jnp.where(first, own, other)
            out[:, 1, :] = jnp.where(first, other, own)

        outs = [shape((quarter, 2, width), F32)]
        pair = call(kernel, "both_images", outs, [SMEM, VMEM, VMEM], [], [flags, rows, got], 0, 16, after)[0]
        return pair

    rows = 2 * padded_quarter
    valid = lax.dynamic_index_in_dim(valid_len, x_idx, 0, keepdims=False)
    spot = jnp.arange(padded_quarter)
    live = [
        (spot < quarter) & ((2 * xx + cc) * quarter + spot < valid) for cc in (core, 1 - core) for xx in (x_idx, 1 - x_idx)
    ]
    bias = jnp.where(jnp.concatenate(live), 0.0, -1e30).astype(F32)[None, :]
    bias = jnp.broadcast_to(bias, (8, bias.shape[1]))

    span = query_weight.shape[2]
    units = up_weight.shape[2]
    part = width // dp
    plane = two_rows()

    gain_moves = [move(norm_gains[0]) for move in (swap_x, swap_y, swap_both)] if plane else []
    turned = [jnp.transpose(w[0]) for w in (query_weight, key_weight, value_weight)]
    packed, give_rows, keep_rows, (at_heads, at_up, at_down), h_units = pack(
        flags, [*turned, output_weight[0]], up_weight[0], jnp.transpose(down_weight[0]), jnp.transpose(images, (1, 0, 2)),
        padded_quarter,
    )
    h_heads = span // 2
    if plane:
        from_x, from_y = swap_x(packed), swap_y(packed)
        img_got = swap_x(give_rows)
        at = 2 * h_heads
        over_heads = [(swap_x(from_y[:at]), 0, at), (swap_y(from_x[at:at_up]), 0, at)]
        up_on, down_on = from_y[at_up:at_down], from_x[at_down:]
        over_up, over_down = [(swap_x(up_on), 0, h_units)], [(swap_y(down_on), 0, h_units)]
        cuts = [up_on, down_on]
        near = lambda row, rows: [[(packed, row, rows)], [(from_y, row, rows)]]
        far = lambda row, rows, over: [[(from_x, row, rows)], over]
    else:
        whole = lax.all_gather(packed, "dp")
        other = swap_x(whole)
        over_heads = over_up = over_down = None
        cuts = []
        img_got = swap_x(give_rows)
        near = lambda row, rows: [[(whole[i], row, rows)] for i in range(dp)]
        far = lambda row, rows, over: [[(other[i], row, rows)] for i in range(dp)]
    gains = gather_gains(norm_gains[0], gain_moves, dp_idx, x_idx, core)
    first_rows = jnp.concatenate((keep_rows, up32(img_got)), axis=0)
    first_far = swap_core(low16(first_rows))
    heads_near = put_together("heads_near", near(at_heads, 4 * h_heads), flags, 4, h_heads)
    up_near = put_together("up_near", near(at_up, h_units), flags, 1, h_units, [heads_near])[0]
    down_near = put_together("down_near", near(at_down, h_units), flags, 1, h_units, [heads_near])[0]
    heads_far = put_together("heads_far", far(at_heads, 4 * h_heads, over_heads), flags, 4, h_heads, [up_near, down_near, *cuts])
    heads = [heads_near, heads_far, swap_core(heads_near), swap_core(heads_far)]
    hidden, normed_b = layer_first(flags, first_rows, first_far, bias, gains, heads)
    up_near = [up_near, swap_core(up_near)]
    down_near = [down_near, swap_core(down_near)]
    act_near = feed_up(normed_b, up_near)
    half_out = feed_down(hidden, act_near, down_near, F32)
    up_far = put_together("up_far", far(at_up, h_units, over_up), flags, 1, h_units, [normed_b])[0]
    up_far = [up_far, swap_core(up_far)]
    down_far = put_together("down_far", far(at_down, h_units, over_down), flags, 1, h_units, [normed_b])[0]
    down_far = [down_far, swap_core(down_far)]
    act_far = feed_up(normed_b, up_far)
    out = feed_down(half_out, act_far, down_far, BF)

    def fetch(after):
        return settle(flags, after, heads, up_near + up_far, down_near + down_far)

    sources = [first_rows, first_far]
    for tick in range(1, sections):
        got = shift(out, 1)
        if tick == 1:
            weights, token = fetch(out)
            got, token = ties(got, token)
        sources += [got, swap_core(got)]
        if tick + 1 < sections:
            out = layer_mid(flags, *sources[-2:], bias, gains, *weights, [token] if tick == 1 else [])
            if tick == 1:
                cot_got = swap_x(theirs(cotangent))
    x, normed_a, q, kv = last_project(flags, sources, gains, weights[0])
    mix, mix_rest, lse, hidden, normed_b = last_attention(q, kv, bias, x, gains, weights[0])
    out, slope, hidden_grad, do, dy = feed_turn(hidden, normed_b, mine(cotangent), cot_got, gains, *weights)

    sources = [dy]
    acts_got = give_back(out)

    def core_halves(a):
        lo = jnp.concatenate((a[:, :span], a[:, 2 * span : 3 * span]), axis=1)
        hi = jnp.concatenate((a[:, span : 2 * span], a[:, 3 * span :]), axis=1)
        return jnp.where(core == 0, lo, hi), jnp.where(core == 0, hi, lo)

    at = half_cut(rows)

    at = half_cut(rows)
    for tick in range(sections):
        last = tick + 1 == sections
        if last:
            dy_low = low16(sources[0])
            for i, a in enumerate(sources[1:]):
                dy_low = jnp.where(section == sections - 2 - i, a, dy_low)
            if plane:
                dy_x0, dy_y1 = swap_x(dy_low[:at]), swap_y(dy_low[at:])
        if tick:
            mode = "last" if last else "mid"
            used, after = (sources, [act_all]) if last else (sources[-1:], [acts_got] if tick == 1 else [acts, nb_x1, nb_y0])
            results = feed_back(mode, flags, used, slope, hidden, gains, weights[0], up_near + up_far, weights[2], after)
            hidden_grad, do = results[:2]
        if last:
            mix_low, gain_sum_b = results[2:]
            mix_got, ml_far = swap_core(mix_give), swap_core(mix_low)
        after = []
        if plane and tick == 1:
            after = [nb_x0, nb_y1]
        if plane and tick == 2:
            after = [nb_d0, nb_d1]
        if plane and last:
            dy_d0, dy_d1 = swap_y(dy_x0), swap_x(dy_y1)
            after = [dy_x0, dy_y1]
        dq, dkv, dkv_far = attention_back(q, kv, do, mix, mix_rest, lse, bias, after)
        dkv_got = swap_core(dkv_far)
        after = []
        if plane and last:
            o_parts = plane_blocks("output_grads", flags, (mix_keep, mix_got), (mix_low, ml_far), [dq])
            o_via = swap_x(o_parts[1]), swap_y(o_parts[2])
            dy_rest = tie(dy_low, dq)
            dy_x1, dy_y0 = swap_x(dy_rest[at:]), swap_y(dy_rest[:at])
            after = [o_parts[0], dy_d0, dy_d1]
        if plane and tick == 2:
            nb_four = join("join_normed", [normed_b, nb_x0, nb_x1, nb_y0, nb_y1, nb_d0, nb_d1], [dq])
            after = [nb_four]
        back = qkv_back(last, flags, dq, dkv, dkv_got, x, hidden_grad, gains, weights[0], after)
        if last:
            break
        low = back[0]
        if plane and tick == 2:
            nb_four, low = ties(nb_four, low)
        got = shift(low, -1)
        if tick == 0:
            nb_x0 = nb_x1 = nb_y0 = nb_y1 = normed_b
            if plane:
                nb_x0, nb_y1 = swap_x(normed_b[:at]), swap_y(normed_b[at:])
        elif tick == 1:
            if plane:
                nb_x1, nb_y0 = swap_x(normed_b[at:]), swap_y(normed_b[:at])
                nb_d0, nb_d1 = swap_y(nb_x0), swap_x(nb_y1)
            acts = both_images(out, acts_got)
            mix_keep, mix_give = core_halves(mix)
            na_far = swap_core(normed_a)
        elif tick == 2:
            if plane:
                nb_far = swap_core(nb_four)
            else:
                nb_all = lax.all_gather(normed_b, ("dp", "tensor"), axis=0, tiled=True)
                nb_four, nb_far = jnp.split(nb_all, 2)
            act_all, slope_all = unit_forward(nb_four, nb_far, up_near[0], [mix_keep, mix_give, na_far])
            got, act_all = ties(got, act_all)
        sources.append(got)
    dx, _, keep, give, gain_sum_a = back

    got = swap_core(give)
    grads_got = give_back(dx)
    gain_sums = jnp.concatenate((gain_sum_a, gain_sum_b), axis=0)
    if plane:
        gain_moves = [move(gain_sums) for move in (swap_x, swap_y, swap_both)]
        qkv_parts = plane_blocks("qkv_grads", flags, (keep, got), (normed_a, na_far))
        via = swap_x(qkv_parts[1]), swap_y(qkv_parts[2])
        dy_four = join("join_dy", [dy_low, dy_x0, dy_x1, dy_y0, dy_y1, dy_d0, dy_d1], [qkv_parts[0]])
        dy_far = swap_core(dy_four)
        sides = [(nb_four, dy_four), (nb_far, dy_far)]
        grad_up = unit_sums("up_grads", flags, sides, slope_all, down_near[0], units, part, [qkv_parts[0]])
        over = scatter_middle("qkv_middle", *qkv_parts[3:], *via, [grad_up])
        o_over = scatter_middle("output_middle", *o_parts[3:], *o_via, [grad_up])
        grad_down = unit_sums("down_grads", flags, [(dy_four,), (dy_far,)], act_all, None, units, part, [grad_up, *gain_moves])
        gain_sums = gain_sums + gain_moves[0] + gain_moves[1] + gain_moves[2]
        gain_sums = gain_sums + swap_core(gain_sums)
        (grad_o,) = scatter_end("output_end", o_parts[0], *o_via, *o_over, 1, [grad_down])
        grad_heads = scatter_end("qkv_end", qkv_parts[0], *via, *over, 3, [grad_down])
        gain_shard = lax.dynamic_slice_in_dim(gain_sums, (dp_idx * 4 + tensor_idx) * (width // 8), width // 8, 1)
        grads_after = [grad_down]
    else:
        dy_all = lax.all_gather(dy_low, ("dp", "tensor"), axis=0, tiled=True)
        dy_four, dy_far = jnp.split(dy_all, 2)
        grad_up = unit_sums("up_grads", flags, [(nb_four, dy_four), (nb_far, dy_far)], slope_all, down_near[0], units, part)
        grad_down = unit_sums("down_grads", flags, [(dy_four,), (dy_far,)], act_all, None, units, part)
        grads_after = []
        both = lambda a, b: jnp.concatenate((a, b), axis=0)
        g = t_dot(both(keep, got), both(normed_a, na_far))
        g = g[: 3 * span] + up32(swap_x(low16(g[3 * span :])))
        g = up32(lax.psum_scatter(low16(g), "dp", scatter_dimension=1, tiled=True))
        grad_heads = [g[i * span : (i + 1) * span] for i in range(3)]
        g = t_dot(both(mix_keep, swap_core(mix_give)), both(mix_low, swap_core(mix_low)))
        g = g[:span] + up32(swap_x(low16(g[span:])))
        grad_o = up32(lax.psum_scatter(low16(g), "dp", scatter_dimension=1, tiled=True))
        gain_shard = lax.psum_scatter(gain_sums, ("dp", "tensor"), scatter_dimension=1, tiled=True)
    grads = both_images(dx, grads_got, grads_after)

    return (
        jnp.transpose(acts, (1, 0, 2))[None],
        jnp.transpose(grads, (1, 0, 2))[None],
        *[jnp.transpose(g)[None] for g in grad_heads],
        grad_o[None],
        grad_up[None],
        jnp.transpose(grad_down)[None],
        gain_shard[None],
    )


def solution(mesh):
    return jax.shard_map(
        local,
        mesh=mesh,
        in_specs=(
            P("dp", "tensor", None),
            P("dp"),
            P("section", "dp", "tensor"),
            P("section", "dp", "tensor"),
            P("section", "dp", "tensor"),
            P("section", "tensor", "dp"),
            P("section", "dp", "tensor"),
            P("section", "tensor", "dp"),
            P("section", None, ("dp", "tensor")),
            P("dp", "tensor", None),
        ),
        out_specs=(
            P("section", "dp", "tensor", None),
            P("section", "dp", "tensor", None),
            P("section", "dp", "tensor"),
            P("section", "dp", "tensor"),
            P("section", "dp", "tensor"),
            P("section", "tensor", "dp"),
            P("section", "dp", "tensor"),
            P("section", "tensor", "dp"),
            P("section", None, ("dp", "tensor")),
        ),
        check_vma=False,
    )
```

```python
import math

import jax
import jax.numpy as jnp
from jax import lax
from jax.experimental import pallas as pl
from jax.experimental.pallas import tpu as pltpu
from jax.sharding import PartitionSpec as P

HD = 72
EPS = 1e-06
SCALE = HD ** (-0.5)
LOG2E = 1.4426950408889634
BF = jnp.bfloat16
F32 = jnp.float32
WIN = 256
LANES = 128
COST = 0.1
ROOM = 28
K0 = 0.7978845608028654
K1 = 0.044715
VMEM = pl.BlockSpec(memory_space=pltpu.VMEM)
SMEM = pl.BlockSpec(memory_space=pltpu.SMEM)
ANY = pl.BlockSpec(memory_space=pl.ANY)


def swap_core(a):
    n = lax.axis_size("tensor")
    return lax.ppermute(a, "tensor", [(i, i ^ 1) for i in range(n)])


def swap_x(a):
    n = lax.axis_size("tensor")
    return lax.ppermute(a, "tensor", [(i, i ^ 2) for i in range(n)])


def swap_y(a):
    return lax.ppermute(a, "dp", [(0, 1), (1, 0)])


def swap_both(a):
    n = lax.axis_size("tensor")
    pairs = [(y * n + i, (1 - y) * n + (i ^ 2)) for y in (0, 1) for i in range(n)]
    return lax.ppermute(a, ("dp", "tensor"), pairs)


def shift(a, by):
    n = lax.axis_size("section")
    pairs = [(i, i + by) for i in range(n) if 0 <= i + by < n]
    return lax.ppermute(a, "section", pairs)


def two_rows():
    return lax.axis_size("dp") == 2


def half_cut(rows):
    return (rows // 2 + 15) // 16 * 16


def up32(a):
    return a.astype(F32)


def low16(a):
    return a.astype(BF)


def dot(a, b):
    return jnp.dot(a, b, preferred_element_type=F32)


def dot_t(a, b):
    return lax.dot_general(a, b, (((1,), (1,)), ((), ())), preferred_element_type=F32)


def t_dot(a, b):
    return lax.dot_general(a, b, (((0,), (0,)), ((), ())), preferred_element_type=F32)


def in_hbm(a):
    return pltpu.with_memory_space_constraint(a, pltpu.HBM)


def spans(total, size):
    return [(at, min(size, total - at)) for at in range(0, total, size)]


def norm_parts(values):
    centre = jnp.mean(values, axis=-1, keepdims=True)
    centred = values - centre
    spread = jnp.mean(centred * centred, axis=-1, keepdims=True)
    inverse = lax.rsqrt(spread + EPS)
    return centred * inverse, inverse


def norm_back(grad, unit, inverse, gain):
    e = grad * gain
    return inverse * (e - jnp.mean(e, axis=-1, keepdims=True) - unit * jnp.mean(e * unit, axis=-1, keepdims=True))


def span_copies(pieces, whole, sems, base):
    rows = pieces[0].shape[0]
    return [
        (pltpu.make_async_copy(piece, whole.at[i * rows : (i + 1) * rows], sems.at[base + i]), (i + 1) * rows)
        for i, piece in enumerate(pieces)
    ]


class Arrivals:
    def __init__(self, copies):
        self.left = list(copies)
        self.have = 0

    def start(self):
        for copy, _ in self.left:
            copy.start()

    def need(self, row):
        while self.left and self.have < row:
            copy, self.have = self.left.pop(0)
            copy.wait()

    def rest(self):
        self.need(1 << 30)


def gelu_one(u):
    return u * (0.5 + 0.5 * jnp.tanh(u * (K0 + (K0 * K1) * (u * u))))


def gelu_both(u):
    sq = u * u
    th = jnp.tanh(u * (K0 + (K0 * K1) * sq))
    half = 0.5 + 0.5 * th
    return u * half, half + (0.5 * u) * (1.0 - th * th) * (K0 + (3.0 * K1 * K0) * sq)


def head_window(h, width):
    tile = min(h * HD // LANES, width // LANES - WIN // LANES)
    off = h * HD - tile * LANES
    lane = lax.broadcasted_iota(jnp.int32, (1, WIN), 1)
    return slice(tile * LANES, tile * LANES + WIN), (lane >= off) & (lane < off + HD)


def shape(dims, dtype):
    return jax.ShapeDtypeStruct(dims, dtype)


def past(kernel, inputs, after):
    return lambda *refs: kernel(*refs[:inputs], *refs[inputs + len(after) :])


def call(kernel, name, outs, ins, scratch, args, flops, limit=60, after=(), cost=None):
    moved = sum(4 * math.prod(a.shape) for a in (*args, *outs))
    return pl.pallas_call(
        past(kernel, len(args), after),
        out_shape=tuple(outs),
        in_specs=[*ins, *[ANY] * len(after)],
        out_specs=tuple([VMEM] * len(outs)),
        scratch_shapes=scratch,
        compiler_params=pltpu.CompilerParams(vmem_limit_bytes=limit * 2**20),
        cost_estimate=pl.CostEstimate(flops=int(flops * (cost or COST)), bytes_accessed=int(moved * (cost or COST)), transcendentals=0),
        name=name,
    )(*args, *after)


def pack(flags, heads, up, down, pair, quarter):
    span, part = heads[0].shape
    units = up.shape[1]
    h = span // 2
    hu = (units + 31) // 32 * 16

    def kernel(flag_ref, *refs):
        pair_ref, out, give_ref, mine_ref, *held, sem = refs[6:]
        copies = [pltpu.make_async_copy(a, b, sem.at[i]) for i, (a, b) in enumerate(zip(refs[:6], held))]
        for copy in copies:
            copy.start()
        refs = held
        got = pair_ref.shape[0]
        first = flag_ref[3] == 0
        one, two = pair_ref[:, 0, :], pair_ref[:, 1, :]
        mine_ref[...] = jnp.zeros_like(mine_ref)
        mine_ref[:got] = jnp.where(first, one, two)
        give_ref[...] = jnp.zeros_like(give_ref)
        give_ref[:got] = low16(jnp.where(first, two, one))
        wait_all(copies)
        for i, ref in enumerate(refs[:4]):
            out[i * h : (i + 1) * h, :part] = ref[:h, :]
            out[i * h : (i + 1) * h, part:] = ref[h:, :]
        for i, ref in enumerate(refs[4:6]):
            base = 4 * h + i * hu
            rows = low16(up32(ref[...]).T)
            out[base : base + hu, :part] = rows[:hu]
            out[base : base + units - hu, part:] = rows[hu:]
            out[base + units - hu : base + hu, part:] = jnp.zeros((2 * hu - units, part), BF)

    total = 4 * h + 2 * hu
    width = pair.shape[2]
    outs = [shape((total, 2 * part), BF), shape((quarter, width), BF), shape((quarter, width), F32)]
    scratch = [pltpu.VMEM(a.shape, BF) for a in (*heads, up, down)] + [pltpu.SemaphoreType.DMA((6,))]
    args = [flags, *[in_hbm(a) for a in (*heads, up, down)], pair]
    got = call(kernel, "pack", outs, [SMEM] + [ANY] * 6 + [VMEM], scratch, args, 0, 34)
    return *got, (0, 4 * h, 4 * h + hu), hu


def put_together(name, pieces, flags, groups, h, after=()):
    count = len(pieces)
    parts = [(i, *p) for i, piece in enumerate(pieces) for p in piece]
    part = parts[0][1].shape[1] // 2
    width = part * count

    def kernel(flag_ref, *refs):
        out, held, sem = refs[len(parts) :]
        copies, at = [], [0] * count
        for j, (ref, (i, _, row, rows)) in enumerate(zip(refs, parts)):
            copies.append(pltpu.make_async_copy(ref.at[row : row + rows], held.at[i, at[i] : at[i] + rows], sem.at[j]))
            at[i] += rows
        for copy in copies:
            copy.start()
        wait_all(copies)
        first = flag_ref[0] == 0
        for i in range(count):
            for g in range(groups):
                rows = slice(g * h, (g + 1) * h)
                piece = jnp.where(first, held[i, rows], held[1 - i, rows]) if count == 2 else held[i, rows]
                out[g, :h, i * part : (i + 1) * part] = piece[:, :part]
                out[g, h:, i * part : (i + 1) * part] = piece[:, part:]

    scratch = [pltpu.VMEM((count, groups * h, 2 * part), BF), pltpu.SemaphoreType.DMA((len(parts),))]
    outs = [shape((groups, 2 * h, width), BF)]
    args = [flags, *[in_hbm(p[1]) for p in parts]]
    return call(kernel, name, outs, [SMEM] + [ANY] * len(parts), scratch, args, 0, 24, after)[0]


def head_copies(pieces, core, kinds, whole, sems, base):
    span, width = pieces[0].shape[1], pieces[0].shape[2]
    out = []
    for n, kind in enumerate(kinds):
        group = []
        for i, piece in enumerate(pieces):
            c = core if i < 2 else 1 - core
            at = pl.multiple_of(n * width + (2 * (i % 2) + c) * span, span)
            sem = sems.at[base + 4 * n + i]
            group.append(pltpu.make_async_copy(piece.at[kind], whole.at[pl.ds(at, span)], sem))
        out.append(group)
    return out


def wait_all(copies):
    for copy in copies:
        copy.wait()


def attend(q, kv, bias, mix, rest, lse_ref):
    rows, width = q.shape
    lane = lax.broadcasted_iota(jnp.int32, (1, LANES), 1)
    for h in range(width // HD):
        win, live = head_window(h, width)
        keys = jnp.where(live, kv[:, win], jnp.zeros((), BF))
        vals = kv[:, width + win.start : width + win.stop]
        s = dot_t(q[:, win], keys) * (SCALE * LOG2E) + bias
        top = jnp.max(s, axis=-1, keepdims=True)
        p = jnp.exp2(s - top)
        total = jnp.sum(p, axis=-1, keepdims=True)
        o = dot(low16(p), vals) * (1.0 / total)
        o_low = low16(o)
        mix[:, win] = jnp.where(live, o_low, mix[:, win])
        if rest is not None:
            rest[:, win] = jnp.where(live, low16(o - up32(o_low)), rest[:, win])
            lse_ref[...] = jnp.where(lane == h, top + jnp.log2(total), lse_ref[...])


def feed_up(normed, pieces, after=()):
    rows, width = normed.shape
    units = sum(piece.shape[0] for piece in pieces)
    n = len(pieces)

    def kernel(nb_ref, *refs):
        act, w, sem = refs[n:]
        arrivals = Arrivals(span_copies(refs[:n], w, sem, 0))
        arrivals.start()
        for at, k in spans(units, 512):
            arrivals.need(at + k)
            act[:, at : at + k] = low16(gelu_one(dot_t(nb_ref[...], w[at : at + k, :])))

    scratch = [pltpu.VMEM((units, width), BF), pltpu.SemaphoreType.DMA((n,))]
    outs = [shape((rows, units), BF)]
    return call(kernel, "feed_up", outs, [VMEM] + [ANY] * n, scratch, [normed, *pieces], 2 * rows * width * units, 30, after)[0]


def feed_down(base, act, pieces, out_type, after=()):
    rows, width = base.shape
    units = act.shape[1]
    n = len(pieces)

    def kernel(base_ref, act_ref, *refs):
        out, w, sem = refs[n:]
        arrivals = Arrivals(span_copies(refs[:n], w, sem, 0))
        arrivals.start()
        arrivals.rest()
        for at, k in spans(width, 256):
            out[:, at : at + k] = (base_ref[:, at : at + k] + dot(act_ref[...], w[:, at : at + k])).astype(out.dtype)

    scratch = [pltpu.VMEM((units, width), BF), pltpu.SemaphoreType.DMA((n,))]
    outs = [shape((rows, width), out_type)]
    args = [base, act, *pieces]
    return call(kernel, "feed_down", outs, [VMEM, VMEM] + [ANY] * n, scratch, args, 2 * rows * width * units, 30, after)[0]


def project(nall, w, q, kv):
    rows, width = q.shape
    for at, n in spans(width, 512):
        q[:, at : at + n] = low16(dot_t(nall[:rows], w[width + at : width + at + n, :]))
    for at, n in spans(2 * width, 512):
        kv[:, at : at + n] = low16(dot_t(nall[...], w[2 * width + at : 2 * width + at + n, :]))


def layer_first(flags, rows32, far, bias, gains, heads):
    rows, width = rows32.shape

    def kernel(flag_ref, bias_ref, gain_ref, x_ref, far_ref, *refs):
        heads_r, hid_ref, nb_ref, w, nall, q, kv, mix, sem = refs[:4], *refs[4:]
        groups = head_copies(heads_r, flag_ref[1], (3, 0, 1, 2), w, sem, 0)
        for group in groups:
            for copy in group:
                copy.start()
        gain_a, gain_b = gain_ref[0:1, :], gain_ref[1:2, :]
        nall[:rows] = low16(norm_parts(x_ref[...])[0] * gain_a)
        nall[rows:] = low16(norm_parts(up32(far_ref[...]))[0] * gain_a)
        for group in groups:
            wait_all(group)
        project(nall, w, q, kv)
        mix[...] = jnp.zeros_like(mix)
        attend(q, kv, bias_ref[0:1, :], mix, None, None)
        hidden = x_ref[...] + dot(mix[...], w[:width, :])
        hid_ref[...] = hidden
        nb_ref[...] = low16(norm_parts(hidden)[0] * gain_b)

    scratch = [
        pltpu.VMEM((4 * width, width), BF),
        pltpu.VMEM((2 * rows, width), BF),
        pltpu.VMEM((rows, width), BF),
        pltpu.VMEM((2 * rows, 2 * width), BF),
        pltpu.VMEM((rows, width), BF),
        pltpu.SemaphoreType.DMA((16,)),
    ]
    outs = [shape((rows, width), F32), shape((rows, width), BF)]
    ins = [SMEM] + [VMEM] * 4 + [ANY] * 4
    flops = 16 * rows * 2 * rows * WIN * 4 + 12 * rows * width * width
    return call(kernel, "layer_first", outs, ins, scratch, [flags, bias, gains, rows32, far, *heads], flops, 44, (), 0.001)


def settle(flags, after, heads, ups, downs):
    kinds, span, width = heads[0].shape
    units = 4 * ups[0].shape[0]

    def kernel(flag_ref, *refs):
        wh, wu, wd, token, sem = refs[13:]
        copies = sum(head_copies(refs[:4], flag_ref[1], (3, 0, 1, 2), wh, sem, 0), [])
        copies += [copy for copy, _ in span_copies(refs[4:8], wu, sem, 16) + span_copies(refs[8:12], wd, sem, 20)]
        for copy in copies:
            copy.start()
        token[...] = jnp.zeros_like(token)
        wait_all(copies)

    pieces = [pltpu.with_memory_space_constraint(a, pltpu.HBM) for a in (*heads, *ups, *downs)]
    wh, wu, wd, token = pl.pallas_call(
        kernel,
        out_shape=(
            pltpu.VMEM((kinds * 4 * span, width), BF),
            pltpu.VMEM((units, width), BF),
            pltpu.VMEM((units, width), BF),
            shape((8, LANES), F32),
        ),
        in_specs=[SMEM] + [ANY] * 13,
        out_specs=(ANY, ANY, ANY, VMEM),
        scratch_shapes=[pltpu.SemaphoreType.DMA((24,))],
        compiler_params=pltpu.CompilerParams(vmem_limit_bytes=ROOM * 2**20),
        cost_estimate=pl.CostEstimate(flops=0, bytes_accessed=int(60 * COST * 2**20), transcendentals=0),
        name="settle",
    )(flags, *pieces, after)
    return [pltpu.with_memory_space_constraint(a, pltpu.VMEM) for a in (wh, wu, wd)], token


def feed(normed, hidden, w_up, w_down, act, slope_out, out):
    for at, n in spans(w_up.shape[0], 512):
        u = dot_t(normed, w_up[at : at + n, :])
        if slope_out is None:
            act[:, at : at + n] = low16(gelu_one(u))
        else:
            a, slope = gelu_both(u)
            act[:, at : at + n] = low16(a)
            slope_out[:, at : at + n] = low16(slope)
    for at, n in spans(w_down.shape[1], 256):
        out[:, at : at + n] = (hidden[:, at : at + n] + dot(act[...], w_down[:, at : at + n])).astype(out.dtype)


def layer_mid(flags, own, far, bias, gains, w_heads, w_up, w_down, after=()):
    rows, width = own.shape
    units = w_up.shape[0]

    def kernel(bias_ref, gain_ref, wh, wu, wd, own_ref, far_ref, out_ref, x_ref, q, kv, mix, hid_ref, nall, act):
        gain_a, gain_b = gain_ref[0:1, :], gain_ref[1:2, :]
        x_ref[...] = up32(own_ref[...])
        nall[:rows] = low16(norm_parts(x_ref[...])[0] * gain_a)
        nall[rows:] = low16(norm_parts(up32(far_ref[...]))[0] * gain_a)
        project(nall, wh, q, kv)
        mix[...] = jnp.zeros_like(mix)
        attend(q, kv, bias_ref[0:1, :], mix, None, None)
        hidden = x_ref[...] + dot(mix[...], wh[:width, :])
        hid_ref[...] = hidden
        feed(low16(norm_parts(hidden)[0] * gain_b), hid_ref, wu, wd, act, None, out_ref)

    scratch = [
        pltpu.VMEM((rows, width), F32),
        pltpu.VMEM((rows, width), BF),
        pltpu.VMEM((2 * rows, 2 * width), BF),
        pltpu.VMEM((rows, width), BF),
        pltpu.VMEM((rows, width), F32),
        pltpu.VMEM((2 * rows, width), BF),
        pltpu.VMEM((rows, units), BF),
    ]
    flops = 16 * rows * 2 * rows * WIN * 4 + 12 * rows * width * width + 4 * rows * width * units
    args = [bias, gains, w_heads, w_up, w_down, own, far]
    return call(kernel, "layer_mid", [shape((rows, width), BF)], [VMEM] * 7, scratch, args, flops, ROOM, after)[0]


def last_project(flags, sources, gains, w_heads):
    rows, width = sources[0].shape
    sections = len(sources) // 2

    def kernel(flag_ref, gain_ref, wh, *refs):
        src, refs = refs[: len(sources)], refs[len(sources) :]
        x_ref, na_ref, q, kv, nall, sem = refs

        def load(i, go):
            own, far = src[2 * i], src[2 * i + 1]
            near = pltpu.make_async_copy(own, x_ref if own.dtype == F32 else na_ref, sem.at[0])
            other = pltpu.make_async_copy(far, nall.at[rows:], sem.at[1])
            for copy in (near, other):
                if go:
                    copy.start()
                else:
                    copy.wait()
            if not go and own.dtype != F32:
                x_ref[...] = up32(na_ref[...])

        for go in (True, False):
            for i in range(sections):
                pl.when(flag_ref[2] == i)(lambda i=i, go=go: load(i, go))
        gain_a = gain_ref[0:1, :]
        normed = low16(norm_parts(x_ref[...])[0] * gain_a)
        na_ref[...] = normed
        nall[:rows] = normed
        nall[rows:] = low16(norm_parts(up32(nall[rows:]))[0] * gain_a)
        project(nall, wh, q, kv)

    row32, row16 = shape((rows, width), F32), shape((rows, width), BF)
    outs = [row32, row16, row16, shape((2 * rows, 2 * width), BF)]
    scratch = [pltpu.VMEM((2 * rows, width), BF), pltpu.SemaphoreType.DMA((2,))]
    ins = [SMEM, VMEM, VMEM] + [ANY] * len(sources)
    args = [flags, gains, w_heads, *[in_hbm(a) for a in sources]]
    return call(kernel, "last_project", outs, ins, scratch, args, 10 * rows * width * width, 12)


def last_attention(q, kv, bias, x, gains, w_heads, after=()):
    rows, width = q.shape

    def kernel(q_ref, kv_ref, bias_ref, x_ref, gain_ref, wh, mix, rest_ref, lse_ref, hid_ref, nb_ref):
        mix[...] = jnp.zeros_like(mix)
        lse_ref[...] = jnp.zeros_like(lse_ref)
        rest_ref[...] = jnp.zeros_like(rest_ref)
        attend(q_ref, kv_ref, bias_ref[0:1, :], mix, rest_ref, lse_ref)
        hidden = x_ref[...] + dot(mix[...], wh[:width, :])
        hid_ref[...] = hidden
        nb_ref[...] = low16(norm_parts(hidden)[0] * gain_ref[1:2, :])

    row32, row16 = shape((rows, width), F32), shape((rows, width), BF)
    outs = [row16, row16, shape((rows, LANES), F32), row32, row16]
    flops = 16 * rows * 2 * rows * WIN * 4 + 2 * rows * width * width
    return call(kernel, "last_attention", outs, [VMEM] * 6, [], [q, kv, bias, x, gains, w_heads], flops, 18, after)


def feed_turn(hidden, normed, dy_own, dy_got, gains, w_heads, w_up, w_down):
    rows, width = hidden.shape
    units = w_up.shape[0]

    half = dy_own.shape[0]

    def kernel(hid_ref, nb_ref, own_ref, got_ref, gain_ref, wh, wu, wd, out_ref, slope_ref, hg_ref, do_ref, dy_ref, act, nbg):
        dy_ref[:half] = own_ref[...]
        dy_ref[half:] = up32(got_ref[...])
        feed(nb_ref[...], hid_ref, wu, wd, act, slope_ref, out_ref)
        feed_grads(low16(dy_ref[...]), slope_ref, wu, wd, act, nbg)
        unit, inverse = norm_parts(hid_ref[...])
        hidden_grad = dy_ref[...] + norm_back(nbg[...], unit, inverse, gain_ref[1:2, :])
        hg_ref[...] = hidden_grad
        do_ref[...] = low16(dot_t(low16(hidden_grad), wh[:width, :]))

    row32 = shape((rows, width), F32)
    outs = [row32, shape((rows, units), BF), row32, shape((rows, width), BF), row32]
    scratch = [pltpu.VMEM((rows, units), BF), pltpu.VMEM((rows, width), F32)]
    flops = 8 * rows * width * units
    args = [hidden, normed, dy_own, dy_got, gains, w_heads, w_up, w_down]
    return call(kernel, "feed_turn", outs, [VMEM] * 8, scratch, args, flops, 22)


def feed_grads(low, slope_ref, w_up, w_down, inner, out, ups=()):
    for at, n in spans(w_up.shape[0], 512):
        inner[:, at : at + n] = low16(dot_t(low, w_down[at : at + n, :]) * up32(slope_ref[:, at : at + n]))
    wait_all(ups)
    for at, n in spans(w_up.shape[1], 256):
        out[:, at : at + n] = dot(inner[...], w_up[:, at : at + n])


def feed_back(mode, flags, sources, slope, hidden, gains, w_heads, w_ups, w_down, after=()):
    last = mode == "last"
    rows, width = hidden.shape
    units = w_down.shape[0]
    n_up = len(w_ups)

    def kernel(flag_ref, gain_ref, hid_ref, slope_ref, wh, wd, *refs):
        *refs, wu, up_sem = refs
        ups = [copy for copy, _ in span_copies(refs[:n_up], wu, up_sem, 0)]
        for copy in ups:
            copy.start()
        refs = refs[n_up:]
        src, refs = refs[: len(sources)], refs[len(sources) :]
        hg_ref, do_ref, refs = refs[0], refs[1], refs[2:]
        if last:
            ml_ref, gs_ref, ig, nbg, dy_ref, low, sem = refs

            def load(a, go):
                copy = pltpu.make_async_copy(a, dy_ref if a.dtype == F32 else low, sem.at[0])
                if go:
                    copy.start()
                    return
                copy.wait()
                if a.dtype == F32:
                    low[...] = low16(dy_ref[...])
                else:
                    dy_ref[...] = up32(low[...])

            for go in (True, False):
                for i, a in enumerate(src):
                    pl.when(flag_ref[2] == len(src) - 1 - i)(lambda a=a, go=go: load(a, go))
        else:
            ig, nbg, dy_ref, low = refs
            dy_ref[...] = src[0][...].astype(F32)
            low[...] = low16(src[0][...])
        feed_grads(low[...], slope_ref, wu, wd, ig, nbg, ups)
        unit, inverse = norm_parts(hid_ref[...])
        grad = nbg[...]
        if last:
            gs_ref[...] = jnp.sum(grad * unit, axis=0, keepdims=True)
        hidden_grad = dy_ref[...] + norm_back(grad, unit, inverse, gain_ref[1:2, :])
        hg_ref[...] = hidden_grad
        mix_low = low16(hidden_grad)
        if last:
            ml_ref[...] = mix_low
        do_ref[...] = low16(dot_t(mix_low, wh[:width, :]))

    sources = [in_hbm(a) if last else a for a in sources]
    args = [flags, gains, hidden, slope, w_heads, w_down, *[in_hbm(a) for a in w_ups], *sources]
    outs = [shape((rows, width), F32), shape((rows, width), BF)]
    if last:
        outs += [shape((rows, width), BF), shape((1, width), F32)]
    scratch = [
        pltpu.VMEM((rows, units), BF),
        pltpu.VMEM((rows, width), F32),
        pltpu.VMEM((rows, width), F32),
        pltpu.VMEM((rows, width), BF),
    ]
    if last:
        scratch.append(pltpu.SemaphoreType.DMA((1,)))
    scratch += [pltpu.VMEM((units, width), BF), pltpu.SemaphoreType.DMA((n_up,))]
    ins = [SMEM] + [VMEM] * 5 + [ANY] * n_up + [ANY if last else VMEM] * len(sources)
    flops = 4 * rows * width * units + 2 * rows * width * width
    return call(kernel, "feed_back_" + mode, outs, ins, scratch, args, flops, 24, after)


def attention_back(q, kv_all, do, mix, mix_rest, lse, bias, after=()):
    rows, width = q.shape
    keys_n = 2 * rows

    def kernel(q_ref, kv, do_ref, o_ref, rest_ref, lse_ref, bias_ref, dq_ref, dkv_own, dkv_far, qt, dt, dkt, dvt):
        bias_row = bias_ref[0:1, :]
        qt[...] = q_ref[...].T
        dt[...] = do_ref[...].T
        dq_ref[...] = jnp.zeros_like(dq_ref)
        zero = jnp.zeros((), BF)
        parts = ([], [])
        for h in range(width // HD):
            win, live = head_window(h, width)
            keys = jnp.where(live, kv[:, win], zero)
            vals = jnp.where(live, kv[:, width + win.start : width + win.stop], zero)
            d_out = do_ref[:, win]
            whole = up32(o_ref[:, win]) + up32(rest_ref[:, win])
            row_dot = jnp.sum(jnp.where(live, up32(d_out) * whole, 0.0), axis=-1, keepdims=True)
            s = dot_t(q_ref[:, win], keys) * (SCALE * LOG2E) + bias_row
            p = jnp.exp2(s - lse_ref[:, h : h + 1])
            ds = low16(p * (dot_t(d_out, vals) - row_dot))
            dq = dot(ds, keys) * SCALE
            dq_ref[:, win] = jnp.where(live, low16(dq), dq_ref[:, win])
            row = h % 2 * HD
            pair = slice((h - h % 2) * HD, (h - h % 2 + 2) * HD)
            parts[0].append(low16(dot(qt[pair, :][row : row + HD], ds) * SCALE))
            parts[1].append(low16(dot(dt[pair, :][row : row + HD], low16(p))))
            if h % 2:
                dkt[pair, :] = jnp.concatenate(parts[0], axis=0)
                dvt[pair, :] = jnp.concatenate(parts[1], axis=0)
                parts = ([], [])
        dk = dkt[...].T
        dv = dvt[...].T
        dkv_own[:, :width] = dk[:rows]
        dkv_own[:, width:] = dv[:rows]
        dkv_far[:, :width] = dk[rows:]
        dkv_far[:, width:] = dv[rows:]

    outs = [shape((rows, width), BF), shape((rows, 2 * width), BF), shape((rows, 2 * width), BF)]
    scratch = [
        pltpu.VMEM((width, rows), BF),
        pltpu.VMEM((width, rows), BF),
        pltpu.VMEM((width, keys_n), BF),
        pltpu.VMEM((width, keys_n), BF),
    ]
    flops = 16 * rows * keys_n * WIN * 10
    return call(kernel, "attention_back", outs, [VMEM] * 7, scratch, [q, kv_all, do, mix, mix_rest, lse, bias], flops, 17, after)


def qkv_back(full, flags, dq, own, got, x, hidden_grad, gains, w_heads, after=()):
    rows, width = dq.shape
    span = width // 4

    def kernel(flag_ref, gain_ref, dq_ref, own_ref, got_ref, x_ref, hg_ref, w, *refs):
        if full:
            dx_ref, low_ref, keep_ref, give_ref, gs_ref, grads, nag = refs
        else:
            low_ref, grads, nag = refs
        grads[:, :width] = dq_ref[...]
        grads[:, width:] = low16(up32(own_ref[...]) + up32(got_ref[...]))
        if full:
            mine = flag_ref[1] == 0
            for i in range(3):
                for xr in (0, 1):
                    at = i * width + 2 * xr * span
                    lo = grads[:, at : at + span]
                    hi = grads[:, at + span : at + 2 * span]
                    to = xr * 3 * span + i * span
                    keep_ref[:, to : to + span] = jnp.where(mine, lo, hi)
                    give_ref[:, to : to + span] = jnp.where(mine, hi, lo)
        for at, n in spans(width, 256):
            nag[:, at : at + n] = dot(grads[...], w[width:, at : at + n])
        unit, inverse = norm_parts(x_ref[...])
        grad = nag[...]
        if full:
            gs_ref[...] = jnp.sum(grad * unit, axis=0, keepdims=True)
        dx = hg_ref[...] + norm_back(grad, unit, inverse, gain_ref[0:1, :])
        low_ref[...] = low16(dx)
        if full:
            dx_ref[...] = dx

    outs = [shape((rows, width), BF)]
    if full:
        outs = [shape((rows, width), F32)] + outs
        outs += [shape((rows, 6 * span), BF), shape((rows, 6 * span), BF), shape((1, width), F32)]
    scratch = [pltpu.VMEM((rows, 3 * width), BF), pltpu.VMEM((rows, width), F32)]
    args = [flags, gains, dq, own, got, x, hidden_grad, w_heads]
    return call(kernel, "qkv_back", outs, [SMEM] + [VMEM] * 7, scratch, args, 6 * rows * width * width, 11, after)


def halves_of(total):
    steps = max(1, total // 736)
    return steps, total // steps


def halves_specs(steps, block, cols):
    return [
        pl.BlockSpec((block, cols), lambda i: (jnp.minimum(i, steps - 1), 0)),
        pl.BlockSpec((block, cols), lambda i: (jnp.maximum(i, steps) - steps, 0)),
    ]


def unit_forward(normed_four, normed_far, w_up, after=()):
    total, width = normed_four.shape
    n = w_up.shape[0]
    half, block = halves_of(total)

    def kernel(a_ref, b_ref, wu_ref, act_ref, slope_ref, token):
        token[...] = jnp.zeros_like(token)

        def rows(nb_ref):
            for at, k in spans(n, 512):
                act, slope = gelu_both(dot_t(nb_ref[...], wu_ref[at : at + k, :]))
                act_ref[:, at : at + k] = low16(act)
                slope_ref[:, at : at + k] = low16(slope)

        pl.when(pl.program_id(0) < half)(lambda: rows(a_ref))
        pl.when(pl.program_id(0) >= half)(lambda: rows(b_ref))

    by_rows = pl.BlockSpec((block, n), lambda i: (i, 0))
    return pl.pallas_call(
        past(kernel, 3, after),
        grid=(2 * half,),
        in_specs=[*halves_specs(half, block, width), VMEM, *[ANY] * len(after)],
        out_specs=(by_rows, by_rows, pl.BlockSpec((8, LANES), lambda i: (0, 0))),
        out_shape=(pltpu.HBM((2 * total, n), BF), pltpu.HBM((2 * total, n), BF), shape((8, LANES), F32)),
        compiler_params=pltpu.CompilerParams(vmem_limit_bytes=18 * 2**20),
        cost_estimate=pl.CostEstimate(flops=int(5.6 * COST * total * width * n), bytes_accessed=int(12 * COST * total * width), transcendentals=0),
        name="unit_forward",
    )(normed_four, normed_far, w_up, *after)


def pick_cols(a, which, part):
    picked = a[:, :part]
    for i in range(1, a.shape[1] // part):
        picked = jnp.where(which == i, a[:, i * part : (i + 1) * part], picked)
    return picked


def unit_sums(name, flags, sides, saved, w_down, units, part, after=()):
    total, width = sides[0][0].shape
    n = saved.shape[1]
    steps = max(1, total // 736)
    block = total // steps
    all_steps = steps * len(sides)
    kinds = len(sides[0])
    flat = [a for side in sides for a in side]
    with_w = w_down is not None

    def kernel(flag_ref, *refs):
        if with_w:
            wd_ref, refs = refs[0], refs[1:]
        saved_hbm, refs = refs[0], refs[1:]
        rows_hbm, refs = refs[: len(flat)], refs[len(flat) :]
        out, token, held, sems = refs[0], refs[1], refs[2 : 3 + kinds], refs[3 + kinds]
        token[...] = jnp.zeros_like(token)

        def into(i):
            rows = slice(i % steps * block, (i % steps + 1) * block)
            sources = [rows_hbm[i // steps * kinds + j].at[rows] for j in range(kinds)]
            sources.append(saved_hbm.at[i * block : (i + 1) * block])
            return [pltpu.make_async_copy(a, b.at[i % 2], sems.at[j, i % 2]) for j, (a, b) in enumerate(zip(sources, held))]

        for copy in into(0):
            copy.start()
        for i in range(all_steps):
            if i + 1 < all_steps:
                for copy in into(i + 1):
                    copy.start()
            wait_all(into(i))
            turned = pick_cols(held[0][i % 2], flag_ref[0], part).T
            for at, k in spans(n, 512):
                right = held[kinds][i % 2, :, at : at + k]
                if with_w:
                    right = low16(dot_t(held[1][i % 2], wd_ref[at : at + k, :]) * up32(right))
                real = min(k, units - at)
                cols = slice(at, at + real)
                got = dot(turned, right)[:, :real]
                out[:, cols] = got if i == 0 else out[:, cols] + got

    scratch = [pltpu.VMEM((2, block, width), BF)] * kinds + [pltpu.VMEM((2, block, n), BF)]
    scratch.append(pltpu.SemaphoreType.DMA((kinds + 1, 2)))
    args = [flags, *([w_down] if with_w else []), in_hbm(saved), *[in_hbm(a) for a in flat]]
    ins = [SMEM] + [VMEM] * with_w + [ANY] * (1 + len(flat))
    flops = (4 if with_w else 2) * total * len(sides) * width * n
    outs = [shape((part, units), F32), shape((8, LANES), F32)]
    return call(kernel, name, outs, ins, scratch, args, flops, 40, after, 0.2)


def join(name, pieces, after=()):
    n = len(pieces)

    def kernel(*refs):
        out, at = refs[n], 0
        for ref in refs[:n]:
            out[at : at + ref.shape[0]] = ref[...]
            at += ref.shape[0]

    rows = sum(a.shape[0] for a in pieces)
    return call(kernel, name, [pltpu.HBM((rows, pieces[0].shape[1]), BF)], [VMEM] * n, [], list(pieces), 0, 16, after)[0]


def plane_blocks(name, flags, left, right, after=()):
    rows = left[0].shape[0]
    part = right[0].shape[1] // 2
    span = left[0].shape[1] // 2
    h = span // 2
    cut = half_cut(h)

    def kernel(flag_ref, l0, l1, r0, r1, *refs):
        outs, ls, rs, sem = refs[:5], *refs[5:]
        copies = [
            pltpu.make_async_copy(a, c.at[at : at + rows], sem.at[i])
            for i, (a, c, at) in enumerate(((l0, ls, 0), (l1, ls, rows), (r0, rs, 0), (r1, rs, rows)))
        ]
        for copy in copies:
            copy.start()
        wait_all(copies)
        first = flag_ref[0] == 0
        lo, hi = rs[:, :part], rs[:, part:]
        shares = (jnp.where(first, lo, hi), jnp.where(first, hi, lo))
        for yr in (0, 1):
            for xr in (0, 1):
                got = t_dot(ls[:, xr * span : (xr + 1) * span], shares[yr])
                if yr == 0 and xr == 0:
                    outs[0][...] = got
                    continue
                for side in (0, 1):
                    cols = slice(side * part, (side + 1) * part)
                    top, bottom = low16(got[side * h : side * h + cut]), low16(got[side * h + cut : (side + 1) * h])
                    if xr and yr:
                        outs[1][cut:, cols] = top
                        outs[2][h - cut :, cols] = bottom
                    elif xr:
                        outs[1][:cut, cols] = top
                        outs[3][:, cols] = bottom
                    else:
                        outs[2][: h - cut, cols] = bottom
                        outs[4][:, cols] = top

    outs = [shape((span, part), F32)]
    outs += [shape((n, 2 * part), BF) for n in (2 * cut, 2 * (h - cut), h - cut, cut)]
    scratch = [pltpu.VMEM((2 * rows, 2 * span), BF), pltpu.VMEM((2 * rows, 2 * part), BF), pltpu.SemaphoreType.DMA((4,))]
    args = [flags, *left, *right]
    flops = 16 * rows * span * part
    return call(kernel, name, outs, [SMEM] + [ANY] * 4, scratch, args, flops, 24, after)


def scatter_middle(name, beside, above, via_x, via_y, after=()):
    rest, double = beside.shape
    cut = above.shape[0]

    def kernel(beside_ref, above_ref, vx, vy, to_y, to_x):
        to_y[...] = low16(up32(above_ref[...]) + up32(vx[cut:, :]))
        to_x[...] = low16(up32(beside_ref[...]) + up32(vy[rest:, :]))

    outs = [shape((cut, double), BF), shape((rest, double), BF)]
    to_y, to_x = call(kernel, name, outs, [VMEM] * 4, [], [beside, above, via_x, via_y], 0, 16, after)
    return swap_y(to_y), swap_x(to_x)


def scatter_end(name, own, via_x, via_y, over_y, over_x, count, after=()):
    span, part = own.shape
    h = span // 2
    cut = half_cut(h)
    rest = h - cut
    each = span // count

    def kernel(own_ref, vx, vy, oy, ox, *refs):
        outs, total = refs[:count], refs[count]
        for side in (0, 1):
            cols = slice(side * part, (side + 1) * part)
            base = side * h
            total[base : base + cut] = own_ref[base : base + cut, :] + up32(vx[:cut, cols]) + up32(oy[:, cols])
            total[base + cut : base + h] = own_ref[base + cut : base + h, :] + up32(vy[:rest, cols]) + up32(ox[:, cols])
        for i, out in enumerate(outs):
            out[...] = total[i * each : (i + 1) * each]

    outs = [shape((each, part), F32)] * count
    scratch = [pltpu.VMEM((span, part), F32)]
    return call(kernel, name, outs, [VMEM] * 5, scratch, [own, via_x, via_y, over_y, over_x], 0, 24, after)


def gather_gains(shard, moves, dp_idx, x_idx, core):
    if not two_rows():
        return lax.all_gather(shard, ("dp", "tensor"), axis=1, tiled=True)
    beside, above, across = moves

    def pair(index, a, b):
        return jnp.where(index == 0, jnp.concatenate((a, b), axis=1), jnp.concatenate((b, a), axis=1))

    four = jnp.concatenate((shard, beside, above, across), axis=1)
    other = swap_core(four)
    n = shard.shape[1]
    by_core = [pair(core, four[:, i * n : (i + 1) * n], other[:, i * n : (i + 1) * n]) for i in range(4)]
    return pair(dp_idx, pair(x_idx, *by_core[:2]), pair(x_idx, *by_core[2:]))


def ties(*arrays):
    return list(lax.optimization_barrier(arrays))


def tie(a, *others):
    return ties(a, *others)[0]


def local(images, valid_len, query_weight, key_weight, value_weight, output_weight, up_weight, down_weight, norm_gains, cotangent):
    section = lax.axis_index("section")
    sections = lax.axis_size("section")
    dp_idx = lax.axis_index("dp")
    dp = lax.axis_size("dp")
    tensor_idx = lax.axis_index("tensor")
    x_idx, core = tensor_idx // 2, tensor_idx % 2
    per_dp, quarter, width = images.shape
    assert per_dp == 2 and lax.axis_size("tensor") == 4
    padded_quarter = (quarter + 7) // 8 * 8
    flags = jnp.stack((dp_idx, core, section, x_idx)).astype(jnp.int32)

    def pad_rows(a):
        return jnp.pad(a, ((0, padded_quarter - quarter), (0, 0)))

    def mine(a):
        return pad_rows(lax.dynamic_index_in_dim(a, x_idx, 0, keepdims=False))

    def theirs(a):
        return pad_rows(low16(lax.dynamic_index_in_dim(a, 1 - x_idx, 0, keepdims=False)))

    def give_back(rows):
        return swap_x(low16(rows[padded_quarter:]))

    def both_images(rows, got, after=()):
        def kernel(flag_ref, own_ref, got_ref, out, token):
            token[...] = jnp.zeros_like(token)
            first = flag_ref[3] == 0
            own, other = own_ref[:quarter], up32(got_ref[...])[:quarter]
            out[:, 0, :] = jnp.where(first, own, other)
            out[:, 1, :] = jnp.where(first, other, own)

        outs = [shape((quarter, 2, width), F32), shape((8, LANES), F32)]
        return call(kernel, "both_images", outs, [SMEM, VMEM, VMEM], [], [flags, rows, got], 0, 16, after)

    rows = 2 * padded_quarter
    valid = lax.dynamic_index_in_dim(valid_len, x_idx, 0, keepdims=False)
    spot = jnp.arange(padded_quarter)
    live = [
        (spot < quarter) & ((2 * xx + cc) * quarter + spot < valid) for cc in (core, 1 - core) for xx in (x_idx, 1 - x_idx)
    ]
    bias = jnp.where(jnp.concatenate(live), 0.0, -1e30).astype(F32)[None, :]
    bias = jnp.broadcast_to(bias, (8, bias.shape[1]))

    span = query_weight.shape[2]
    units = up_weight.shape[2]
    part = width // dp
    plane = two_rows()

    gain_moves = [move(norm_gains[0]) for move in (swap_x, swap_y, swap_both)] if plane else []
    turned = [jnp.transpose(w[0]) for w in (query_weight, key_weight, value_weight)]
    packed, give_rows, keep_rows, (at_heads, at_up, at_down), h_units = pack(
        flags, [*turned, output_weight[0]], up_weight[0], jnp.transpose(down_weight[0]), jnp.transpose(images, (1, 0, 2)),
        padded_quarter,
    )
    h_heads = span // 2
    if plane:
        from_x, from_y = swap_x(packed), swap_y(packed)
        img_got = swap_x(give_rows)
        at = 2 * h_heads
        over_heads = [(swap_x(from_y[:at]), 0, at), (swap_y(from_x[at:at_up]), 0, at)]
        up_on, down_on = from_y[at_up:at_down], from_x[at_down:]
        over_up, over_down = [(swap_x(up_on), 0, h_units)], [(swap_y(down_on), 0, h_units)]
        cuts = [up_on, down_on]
        near = lambda row, rows: [[(packed, row, rows)], [(from_y, row, rows)]]
        far = lambda row, rows, over: [[(from_x, row, rows)], over]
    else:
        whole = lax.all_gather(packed, "dp")
        other = swap_x(whole)
        over_heads = over_up = over_down = None
        cuts = []
        img_got = swap_x(give_rows)
        near = lambda row, rows: [[(whole[i], row, rows)] for i in range(dp)]
        far = lambda row, rows, over: [[(other[i], row, rows)] for i in range(dp)]
    gains = gather_gains(norm_gains[0], gain_moves, dp_idx, x_idx, core)
    first_rows = jnp.concatenate((keep_rows, up32(img_got)), axis=0)
    first_far = swap_core(low16(first_rows))
    heads_near = put_together("heads_near", near(at_heads, 4 * h_heads), flags, 4, h_heads)
    up_near = put_together("up_near", near(at_up, h_units), flags, 1, h_units, [heads_near])[0]
    down_near = put_together("down_near", near(at_down, h_units), flags, 1, h_units, [heads_near])[0]
    heads_far = put_together("heads_far", far(at_heads, 4 * h_heads, over_heads), flags, 4, h_heads, [up_near, down_near, *cuts])
    heads = [heads_near, heads_far, swap_core(heads_near), swap_core(heads_far)]
    hidden, normed_b = layer_first(flags, first_rows, first_far, bias, gains, heads)
    up_near = [up_near, swap_core(up_near)]
    down_near = [down_near, swap_core(down_near)]
    act_near = feed_up(normed_b, up_near)
    half_out = feed_down(hidden, act_near, down_near, F32)
    up_far = put_together("up_far", far(at_up, h_units, over_up), flags, 1, h_units, [normed_b])[0]
    up_far = [up_far, swap_core(up_far)]
    down_far = put_together("down_far", far(at_down, h_units, over_down), flags, 1, h_units, [normed_b])[0]
    down_far = [down_far, swap_core(down_far)]
    act_far = feed_up(normed_b, up_far)
    out = feed_down(half_out, act_far, down_far, BF)

    def fetch(after):
        return settle(flags, after, heads, up_near + up_far, down_near + down_far)

    sources = [first_rows, first_far]
    for tick in range(1, sections):
        got = shift(out, 1)
        if tick == 1:
            weights, token = fetch(out)
            got, token = ties(got, token)
        sources += [got, swap_core(got)]
        if tick + 1 < sections:
            out = layer_mid(flags, *sources[-2:], bias, gains, *weights, [token] if tick == 1 else [])
            if tick == 1:
                cot_got = swap_x(theirs(cotangent))
    x, normed_a, q, kv = last_project(flags, sources, gains, weights[0])
    mix, mix_rest, lse, hidden, normed_b = last_attention(q, kv, bias, x, gains, weights[0])
    out, slope, hidden_grad, do, dy = feed_turn(hidden, normed_b, mine(cotangent), cot_got, gains, *weights)

    sources = [dy]
    acts_got = give_back(out)

    def core_halves(a):
        lo = jnp.concatenate((a[:, :span], a[:, 2 * span : 3 * span]), axis=1)
        hi = jnp.concatenate((a[:, span : 2 * span], a[:, 3 * span :]), axis=1)
        return jnp.where(core == 0, lo, hi), jnp.where(core == 0, hi, lo)

    at = half_cut(rows)

    at = half_cut(rows)
    for tick in range(sections):
        last = tick + 1 == sections
        if last:
            dy_low = low16(sources[0])
            for i, a in enumerate(sources[1:]):
                dy_low = jnp.where(section == sections - 2 - i, a, dy_low)
            if plane:
                dy_x0, dy_y1 = swap_x(dy_low[:at]), swap_y(dy_low[at:])
        if tick:
            mode = "last" if last else "mid"
            used, after = (sources, [unit_done]) if last else (sources[-1:], [acts_got] if tick == 1 else [acts_done, nb_x1, nb_y0])
            results = feed_back(mode, flags, used, slope, hidden, gains, weights[0], up_near + up_far, weights[2], after)
            hidden_grad, do = results[:2]
        if last:
            mix_low, gain_sum_b = results[2:]
            mix_got, ml_far = swap_core(mix_give), swap_core(mix_low)
        after = []
        if plane and tick == 1:
            after = [nb_x0, nb_y1]
        if plane and tick == 2:
            after = [nb_d0, nb_d1]
        if plane and last:
            dy_d0, dy_d1 = swap_y(dy_x0), swap_x(dy_y1)
            after = [dy_x0, dy_y1]
        dq, dkv, dkv_far = attention_back(q, kv, do, mix, mix_rest, lse, bias, after)
        dkv_got = swap_core(dkv_far)
        after = []
        if plane and last:
            o_parts = plane_blocks("output_grads", flags, (mix_keep, mix_got), (mix_low, ml_far), [dq])
            o_via = swap_x(o_parts[1]), swap_y(o_parts[2])
            dy_rest = tie(dy_low, dq)
            dy_x1, dy_y0 = swap_x(dy_rest[at:]), swap_y(dy_rest[:at])
            after = [o_parts[4], dy_d0, dy_d1]
        if plane and tick == 2:
            nb_four = join("join_normed", [normed_b, nb_x0, nb_x1, nb_y0, nb_y1, nb_d0, nb_d1], [dq])
            after = [nb_four]
        back = qkv_back(last, flags, dq, dkv, dkv_got, x, hidden_grad, gains, weights[0], after)
        if last:
            break
        low = back[0]
        if plane and tick == 2:
            nb_four, low = ties(nb_four, low)
        got = shift(low, -1)
        if tick == 0:
            nb_x0 = nb_x1 = nb_y0 = nb_y1 = normed_b
            if plane:
                nb_x0, nb_y1 = swap_x(normed_b[:at]), swap_y(normed_b[at:])
        elif tick == 1:
            if plane:
                nb_x1, nb_y0 = swap_x(normed_b[at:]), swap_y(normed_b[:at])
                nb_d0, nb_d1 = swap_y(nb_x0), swap_x(nb_y1)
            acts, acts_done = both_images(out, acts_got)
            mix_keep, mix_give = core_halves(mix)
            na_far = swap_core(normed_a)
        elif tick == 2:
            if plane:
                nb_far = swap_core(nb_four)
            else:
                nb_all = lax.all_gather(normed_b, ("dp", "tensor"), axis=0, tiled=True)
                nb_four, nb_far = jnp.split(nb_all, 2)
            act_all, slope_all, unit_done = unit_forward(nb_four, nb_far, up_near[0], [mix_keep, mix_give, na_far])
            got, unit_done = ties(got, unit_done)
        sources.append(got)
    dx, _, keep, give, gain_sum_a = back

    got = swap_core(give)
    grads_got = give_back(dx)
    gain_sums = jnp.concatenate((gain_sum_a, gain_sum_b), axis=0)
    if plane:
        gain_moves = [move(gain_sums) for move in (swap_x, swap_y, swap_both)]
        qkv_parts = plane_blocks("qkv_grads", flags, (keep, got), (normed_a, na_far))
        via = swap_x(qkv_parts[1]), swap_y(qkv_parts[2])
        dy_four = join("join_dy", [dy_low, dy_x0, dy_x1, dy_y0, dy_y1, dy_d0, dy_d1], [qkv_parts[0]])
        dy_far = swap_core(dy_four)
        sides = [(nb_four, dy_four), (nb_far, dy_far)]
        grad_up, up_done = unit_sums("up_grads", flags, sides, slope_all, down_near[0], units, part, [qkv_parts[0]])
        over = scatter_middle("qkv_middle", *qkv_parts[3:], *via, [up_done])
        o_over = scatter_middle("output_middle", *o_parts[3:], *o_via, [up_done])
        grad_down, down_done = unit_sums("down_grads", flags, [(dy_four,), (dy_far,)], act_all, None, units, part, [up_done, *gain_moves])
        gain_sums = gain_sums + gain_moves[0] + gain_moves[1] + gain_moves[2]
        gain_sums = gain_sums + swap_core(gain_sums)
        (grad_o,) = scatter_end("output_end", o_parts[0], *o_via, *o_over, 1, [down_done])
        grad_heads = scatter_end("qkv_end", qkv_parts[0], *via, *over, 3, [down_done])
        gain_shard = lax.dynamic_slice_in_dim(gain_sums, (dp_idx * 4 + tensor_idx) * (width // 8), width // 8, 1)
        grads_after = [down_done]
    else:
        dy_all = lax.all_gather(dy_low, ("dp", "tensor"), axis=0, tiled=True)
        dy_four, dy_far = jnp.split(dy_all, 2)
        grad_up, _ = unit_sums("up_grads", flags, [(nb_four, dy_four), (nb_far, dy_far)], slope_all, down_near[0], units, part)
        grad_down, _ = unit_sums("down_grads", flags, [(dy_four,), (dy_far,)], act_all, None, units, part)
        grads_after = []
        both = lambda a, b: jnp.concatenate((a, b), axis=0)
        g = t_dot(both(keep, got), both(normed_a, na_far))
        g = g[: 3 * span] + up32(swap_x(low16(g[3 * span :])))
        g = up32(lax.psum_scatter(low16(g), "dp", scatter_dimension=1, tiled=True))
        grad_heads = [g[i * span : (i + 1) * span] for i in range(3)]
        g = t_dot(both(mix_keep, swap_core(mix_give)), both(mix_low, swap_core(mix_low)))
        g = g[:span] + up32(swap_x(low16(g[span:])))
        grad_o = up32(lax.psum_scatter(low16(g), "dp", scatter_dimension=1, tiled=True))
        gain_shard = lax.psum_scatter(gain_sums, ("dp", "tensor"), scatter_dimension=1, tiled=True)
    grads, _ = both_images(dx, grads_got, grads_after)

    return (
        jnp.transpose(acts, (1, 0, 2))[None],
        jnp.transpose(grads, (1, 0, 2))[None],
        *[jnp.transpose(g)[None] for g in grad_heads],
        grad_o[None],
        grad_up[None],
        jnp.transpose(grad_down)[None],
        gain_shard[None],
    )


def solution(mesh):
    return jax.shard_map(
        local,
        mesh=mesh,
        in_specs=(
            P("dp", "tensor", None),
            P("dp"),
            P("section", "dp", "tensor"),
            P("section", "dp", "tensor"),
            P("section", "dp", "tensor"),
            P("section", "tensor", "dp"),
            P("section", "dp", "tensor"),
            P("section", "tensor", "dp"),
            P("section", None, ("dp", "tensor")),
            P("dp", "tensor", None),
        ),
        out_specs=(
            P("section", "dp", "tensor", None),
            P("section", "dp", "tensor", None),
            P("section", "dp", "tensor"),
            P("section", "dp", "tensor"),
            P("section", "dp", "tensor"),
            P("section", "tensor", "dp"),
            P("section", "dp", "tensor"),
            P("section", "tensor", "dp"),
            P("section", None, ("dp", "tensor")),
        ),
        check_vma=False,
    )
```

```python
import math

import jax
import jax.numpy as jnp
from jax import lax
from jax.experimental import pallas as pl
from jax.experimental.pallas import tpu as pltpu
from jax.sharding import PartitionSpec as P

HD = 72
EPS = 1e-06
SCALE = HD ** (-0.5)
LOG2E = 1.4426950408889634
BF = jnp.bfloat16
F32 = jnp.float32
WIN = 256
LANES = 128
COST = 0.1
ROOM = 28
K0 = 0.7978845608028654
K1 = 0.044715
VMEM = pl.BlockSpec(memory_space=pltpu.VMEM)
SMEM = pl.BlockSpec(memory_space=pltpu.SMEM)
ANY = pl.BlockSpec(memory_space=pl.ANY)


def swap_core(a):
    n = lax.axis_size("tensor")
    return lax.ppermute(a, "tensor", [(i, i ^ 1) for i in range(n)])


def swap_x(a):
    n = lax.axis_size("tensor")
    return lax.ppermute(a, "tensor", [(i, i ^ 2) for i in range(n)])


def swap_y(a):
    return lax.ppermute(a, "dp", [(0, 1), (1, 0)])


def swap_both(a):
    n = lax.axis_size("tensor")
    pairs = [(y * n + i, (1 - y) * n + (i ^ 2)) for y in (0, 1) for i in range(n)]
    return lax.ppermute(a, ("dp", "tensor"), pairs)


def shift(a, by):
    n = lax.axis_size("section")
    pairs = [(i, i + by) for i in range(n) if 0 <= i + by < n]
    return lax.ppermute(a, "section", pairs)


def two_rows():
    return lax.axis_size("dp") == 2


def half_cut(rows):
    return (rows // 2 + 15) // 16 * 16


def up32(a):
    return a.astype(F32)


def low16(a):
    return a.astype(BF)


def dot(a, b):
    return jnp.dot(a, b, preferred_element_type=F32)


def dot_t(a, b):
    return lax.dot_general(a, b, (((1,), (1,)), ((), ())), preferred_element_type=F32)


def t_dot(a, b):
    return lax.dot_general(a, b, (((0,), (0,)), ((), ())), preferred_element_type=F32)


def in_hbm(a):
    return pltpu.with_memory_space_constraint(a, pltpu.HBM)


def spans(total, size):
    return [(at, min(size, total - at)) for at in range(0, total, size)]


def norm_parts(values):
    centre = jnp.mean(values, axis=-1, keepdims=True)
    centred = values - centre
    spread = jnp.mean(centred * centred, axis=-1, keepdims=True)
    inverse = lax.rsqrt(spread + EPS)
    return centred * inverse, inverse


def norm_back(grad, unit, inverse, gain):
    e = grad * gain
    return inverse * (e - jnp.mean(e, axis=-1, keepdims=True) - unit * jnp.mean(e * unit, axis=-1, keepdims=True))


def span_copies(pieces, whole, sems, base):
    rows = pieces[0].shape[0]
    return [
        (pltpu.make_async_copy(piece, whole.at[i * rows : (i + 1) * rows], sems.at[base + i]), (i + 1) * rows)
        for i, piece in enumerate(pieces)
    ]


class Arrivals:
    def __init__(self, copies):
        self.left = list(copies)
        self.have = 0

    def start(self):
        for copy, _ in self.left:
            copy.start()

    def need(self, row):
        while self.left and self.have < row:
            copy, self.have = self.left.pop(0)
            copy.wait()

    def rest(self):
        self.need(1 << 30)


def gelu_one(u):
    return u * (0.5 + 0.5 * jnp.tanh(u * (K0 + (K0 * K1) * (u * u))))


def gelu_both(u):
    sq = u * u
    th = jnp.tanh(u * (K0 + (K0 * K1) * sq))
    half = 0.5 + 0.5 * th
    return u * half, half + (0.5 * u) * (1.0 - th * th) * (K0 + (3.0 * K1 * K0) * sq)


def head_window(h, width):
    tile = min(h * HD // LANES, width // LANES - WIN // LANES)
    off = h * HD - tile * LANES
    lane = lax.broadcasted_iota(jnp.int32, (1, WIN), 1)
    return slice(tile * LANES, tile * LANES + WIN), (lane >= off) & (lane < off + HD)


def shape(dims, dtype):
    return jax.ShapeDtypeStruct(dims, dtype)


def past(kernel, inputs, after):
    return lambda *refs: kernel(*refs[:inputs], *refs[inputs + len(after) :])


def call(kernel, name, outs, ins, scratch, args, flops, limit=60, after=(), cost=None):
    moved = sum(4 * math.prod(a.shape) for a in (*args, *outs))
    return pl.pallas_call(
        past(kernel, len(args), after),
        out_shape=tuple(outs),
        in_specs=[*ins, *[ANY] * len(after)],
        out_specs=tuple([VMEM] * len(outs)),
        scratch_shapes=scratch,
        compiler_params=pltpu.CompilerParams(vmem_limit_bytes=limit * 2**20),
        cost_estimate=pl.CostEstimate(flops=int(flops * (cost or COST)), bytes_accessed=int(moved * (cost or COST)), transcendentals=0),
        name=name,
    )(*args, *after)


def pack(flags, heads, up, down, pair, quarter):
    span, part = heads[0].shape
    units = up.shape[1]
    h = span // 2
    hu = (units + 31) // 32 * 16

    def kernel(flag_ref, *refs):
        pair_ref, out, give_ref, mine_ref, *held, sem = refs[6:]
        copies = [pltpu.make_async_copy(a, b, sem.at[i]) for i, (a, b) in enumerate(zip(refs[:6], held))]
        for copy in copies:
            copy.start()
        refs = held
        got = pair_ref.shape[0]
        first = flag_ref[3] == 0
        one, two = pair_ref[:, 0, :], pair_ref[:, 1, :]
        mine_ref[...] = jnp.zeros_like(mine_ref)
        mine_ref[:got] = jnp.where(first, one, two)
        give_ref[...] = jnp.zeros_like(give_ref)
        give_ref[:got] = low16(jnp.where(first, two, one))
        wait_all(copies)
        for i, ref in enumerate(refs[:4]):
            out[i * h : (i + 1) * h, :part] = ref[:h, :]
            out[i * h : (i + 1) * h, part:] = ref[h:, :]
        for i, ref in enumerate(refs[4:6]):
            base = 4 * h + i * hu
            rows = low16(up32(ref[...]).T)
            out[base : base + hu, :part] = rows[:hu]
            out[base : base + units - hu, part:] = rows[hu:]
            out[base + units - hu : base + hu, part:] = jnp.zeros((2 * hu - units, part), BF)

    total = 4 * h + 2 * hu
    width = pair.shape[2]
    outs = [shape((total, 2 * part), BF), shape((quarter, width), BF), shape((quarter, width), F32)]
    scratch = [pltpu.VMEM(a.shape, BF) for a in (*heads, up, down)] + [pltpu.SemaphoreType.DMA((6,))]
    args = [flags, *[in_hbm(a) for a in (*heads, up, down)], pair]
    got = call(kernel, "pack", outs, [SMEM] + [ANY] * 6 + [VMEM], scratch, args, 0, 34)
    return *got, (0, 4 * h, 4 * h + hu), hu


def put_together(name, pieces, flags, groups, h, after=()):
    count = len(pieces)
    parts = [(i, *p) for i, piece in enumerate(pieces) for p in piece]
    part = parts[0][1].shape[1] // 2
    width = part * count

    def kernel(flag_ref, *refs):
        out, held, sem = refs[len(parts) :]
        copies, at = [], [0] * count
        for j, (ref, (i, _, row, rows)) in enumerate(zip(refs, parts)):
            copies.append(pltpu.make_async_copy(ref.at[row : row + rows], held.at[i, at[i] : at[i] + rows], sem.at[j]))
            at[i] += rows
        for copy in copies:
            copy.start()
        wait_all(copies)
        first = flag_ref[0] == 0
        for i in range(count):
            for g in range(groups):
                rows = slice(g * h, (g + 1) * h)
                piece = jnp.where(first, held[i, rows], held[1 - i, rows]) if count == 2 else held[i, rows]
                out[g, :h, i * part : (i + 1) * part] = piece[:, :part]
                out[g, h:, i * part : (i + 1) * part] = piece[:, part:]

    scratch = [pltpu.VMEM((count, groups * h, 2 * part), BF), pltpu.SemaphoreType.DMA((len(parts),))]
    outs = [shape((groups, 2 * h, width), BF)]
    args = [flags, *[in_hbm(p[1]) for p in parts]]
    return call(kernel, name, outs, [SMEM] + [ANY] * len(parts), scratch, args, 0, 24, after)[0]


def head_copies(pieces, core, kinds, whole, sems, base):
    span, width = pieces[0].shape[1], pieces[0].shape[2]
    out = []
    for n, kind in enumerate(kinds):
        group = []
        for i, piece in enumerate(pieces):
            c = core if i < 2 else 1 - core
            at = pl.multiple_of(n * width + (2 * (i % 2) + c) * span, span)
            sem = sems.at[base + 4 * n + i]
            group.append(pltpu.make_async_copy(piece.at[kind], whole.at[pl.ds(at, span)], sem))
        out.append(group)
    return out


def wait_all(copies):
    for copy in copies:
        copy.wait()


def attend(q, kv, bias, mix, rest, lse_ref):
    rows, width = q.shape
    lane = lax.broadcasted_iota(jnp.int32, (1, LANES), 1)
    for h in range(width // HD):
        win, live = head_window(h, width)
        keys = jnp.where(live, kv[:, win], jnp.zeros((), BF))
        vals = kv[:, width + win.start : width + win.stop]
        s = dot_t(q[:, win], keys) * (SCALE * LOG2E) + bias
        top = jnp.max(s, axis=-1, keepdims=True)
        p = jnp.exp2(s - top)
        total = jnp.sum(p, axis=-1, keepdims=True)
        o = dot(low16(p), vals) * (1.0 / total)
        o_low = low16(o)
        mix[:, win] = jnp.where(live, o_low, mix[:, win])
        if rest is not None:
            rest[:, win] = jnp.where(live, low16(o - up32(o_low)), rest[:, win])
            lse_ref[...] = jnp.where(lane == h, top + jnp.log2(total), lse_ref[...])


def feed_up(normed, pieces, after=()):
    rows, width = normed.shape
    units = sum(piece.shape[0] for piece in pieces)
    n = len(pieces)

    def kernel(nb_ref, *refs):
        act, w, sem = refs[n:]
        arrivals = Arrivals(span_copies(refs[:n], w, sem, 0))
        arrivals.start()
        for at, k in spans(units, 512):
            arrivals.need(at + k)
            act[:, at : at + k] = low16(gelu_one(dot_t(nb_ref[...], w[at : at + k, :])))

    scratch = [pltpu.VMEM((units, width), BF), pltpu.SemaphoreType.DMA((n,))]
    outs = [shape((rows, units), BF)]
    return call(kernel, "feed_up", outs, [VMEM] + [ANY] * n, scratch, [normed, *pieces], 2 * rows * width * units, 30, after)[0]


def feed_down(base, act, pieces, out_type, after=()):
    rows, width = base.shape
    units = act.shape[1]
    n = len(pieces)

    def kernel(base_ref, act_ref, *refs):
        out, w, sem = refs[n:]
        arrivals = Arrivals(span_copies(refs[:n], w, sem, 0))
        arrivals.start()
        arrivals.rest()
        for at, k in spans(width, 256):
            out[:, at : at + k] = (base_ref[:, at : at + k] + dot(act_ref[...], w[:, at : at + k])).astype(out.dtype)

    scratch = [pltpu.VMEM((units, width), BF), pltpu.SemaphoreType.DMA((n,))]
    outs = [shape((rows, width), out_type)]
    args = [base, act, *pieces]
    return call(kernel, "feed_down", outs, [VMEM, VMEM] + [ANY] * n, scratch, args, 2 * rows * width * units, 30, after)[0]


def project(nall, w, q, kv):
    rows, width = q.shape
    for at, n in spans(width, 512):
        q[:, at : at + n] = low16(dot_t(nall[:rows], w[width + at : width + at + n, :]))
    for at, n in spans(2 * width, 512):
        kv[:, at : at + n] = low16(dot_t(nall[...], w[2 * width + at : 2 * width + at + n, :]))


def layer_first(flags, rows32, far, bias, gains, heads):
    rows, width = rows32.shape

    def kernel(flag_ref, bias_ref, gain_ref, x_ref, far_ref, *refs):
        heads_r, hid_ref, nb_ref, w, nall, q, kv, mix, sem = refs[:4], *refs[4:]
        groups = head_copies(heads_r, flag_ref[1], (3, 0, 1, 2), w, sem, 0)
        for group in groups:
            for copy in group:
                copy.start()
        gain_a, gain_b = gain_ref[0:1, :], gain_ref[1:2, :]
        nall[:rows] = low16(norm_parts(x_ref[...])[0] * gain_a)
        nall[rows:] = low16(norm_parts(up32(far_ref[...]))[0] * gain_a)
        for group in groups:
            wait_all(group)
        project(nall, w, q, kv)
        mix[...] = jnp.zeros_like(mix)
        attend(q, kv, bias_ref[0:1, :], mix, None, None)
        hidden = x_ref[...] + dot(mix[...], w[:width, :])
        hid_ref[...] = hidden
        nb_ref[...] = low16(norm_parts(hidden)[0] * gain_b)

    scratch = [
        pltpu.VMEM((4 * width, width), BF),
        pltpu.VMEM((2 * rows, width), BF),
        pltpu.VMEM((rows, width), BF),
        pltpu.VMEM((2 * rows, 2 * width), BF),
        pltpu.VMEM((rows, width), BF),
        pltpu.SemaphoreType.DMA((16,)),
    ]
    outs = [shape((rows, width), F32), shape((rows, width), BF)]
    ins = [SMEM] + [VMEM] * 4 + [ANY] * 4
    flops = 16 * rows * 2 * rows * WIN * 4 + 12 * rows * width * width
    return call(kernel, "layer_first", outs, ins, scratch, [flags, bias, gains, rows32, far, *heads], flops, 44, (), 0.001)


def settle(flags, after, heads, ups, downs):
    kinds, span, width = heads[0].shape
    units = 4 * ups[0].shape[0]

    def kernel(flag_ref, *refs):
        wh, wu, wd, token, sem = refs[13:]
        copies = sum(head_copies(refs[:4], flag_ref[1], (3, 0, 1, 2), wh, sem, 0), [])
        copies += [copy for copy, _ in span_copies(refs[4:8], wu, sem, 16) + span_copies(refs[8:12], wd, sem, 20)]
        for copy in copies:
            copy.start()
        token[...] = jnp.zeros_like(token)
        wait_all(copies)

    pieces = [pltpu.with_memory_space_constraint(a, pltpu.HBM) for a in (*heads, *ups, *downs)]
    wh, wu, wd, token = pl.pallas_call(
        kernel,
        out_shape=(
            pltpu.VMEM((kinds * 4 * span, width), BF),
            pltpu.VMEM((units, width), BF),
            pltpu.VMEM((units, width), BF),
            shape((8, LANES), F32),
        ),
        in_specs=[SMEM] + [ANY] * 13,
        out_specs=(ANY, ANY, ANY, VMEM),
        scratch_shapes=[pltpu.SemaphoreType.DMA((24,))],
        compiler_params=pltpu.CompilerParams(vmem_limit_bytes=ROOM * 2**20),
        cost_estimate=pl.CostEstimate(flops=0, bytes_accessed=int(60 * COST * 2**20), transcendentals=0),
        name="settle",
    )(flags, *pieces, after)
    return [pltpu.with_memory_space_constraint(a, pltpu.VMEM) for a in (wh, wu, wd)], token


def feed(normed, hidden, w_up, w_down, act, slope_out, out):
    for at, n in spans(w_up.shape[0], 512):
        u = dot_t(normed, w_up[at : at + n, :])
        if slope_out is None:
            act[:, at : at + n] = low16(gelu_one(u))
        else:
            a, slope = gelu_both(u)
            act[:, at : at + n] = low16(a)
            slope_out[:, at : at + n] = low16(slope)
    for at, n in spans(w_down.shape[1], 256):
        out[:, at : at + n] = (hidden[:, at : at + n] + dot(act[...], w_down[:, at : at + n])).astype(out.dtype)


def layer_mid(flags, own, far, bias, gains, w_heads, w_up, w_down, after=()):
    rows, width = own.shape
    units = w_up.shape[0]

    def kernel(bias_ref, gain_ref, wh, wu, wd, own_ref, far_ref, out_ref, x_ref, q, kv, mix, hid_ref, nall, act):
        gain_a, gain_b = gain_ref[0:1, :], gain_ref[1:2, :]
        x_ref[...] = up32(own_ref[...])
        nall[:rows] = low16(norm_parts(x_ref[...])[0] * gain_a)
        nall[rows:] = low16(norm_parts(up32(far_ref[...]))[0] * gain_a)
        project(nall, wh, q, kv)
        mix[...] = jnp.zeros_like(mix)
        attend(q, kv, bias_ref[0:1, :], mix, None, None)
        hidden = x_ref[...] + dot(mix[...], wh[:width, :])
        hid_ref[...] = hidden
        feed(low16(norm_parts(hidden)[0] * gain_b), hid_ref, wu, wd, act, None, out_ref)

    scratch = [
        pltpu.VMEM((rows, width), F32),
        pltpu.VMEM((rows, width), BF),
        pltpu.VMEM((2 * rows, 2 * width), BF),
        pltpu.VMEM((rows, width), BF),
        pltpu.VMEM((rows, width), F32),
        pltpu.VMEM((2 * rows, width), BF),
        pltpu.VMEM((rows, units), BF),
    ]
    flops = 16 * rows * 2 * rows * WIN * 4 + 12 * rows * width * width + 4 * rows * width * units
    args = [bias, gains, w_heads, w_up, w_down, own, far]
    return call(kernel, "layer_mid", [shape((rows, width), BF)], [VMEM] * 7, scratch, args, flops, ROOM, after)[0]


def last_project(flags, sources, gains, w_heads):
    rows, width = sources[0].shape
    sections = len(sources) // 2

    def kernel(flag_ref, gain_ref, wh, *refs):
        src, refs = refs[: len(sources)], refs[len(sources) :]
        x_ref, na_ref, q, kv, nall, sem = refs

        def load(i, go):
            own, far = src[2 * i], src[2 * i + 1]
            near = pltpu.make_async_copy(own, x_ref if own.dtype == F32 else na_ref, sem.at[0])
            other = pltpu.make_async_copy(far, nall.at[rows:], sem.at[1])
            for copy in (near, other):
                if go:
                    copy.start()
                else:
                    copy.wait()
            if not go and own.dtype != F32:
                x_ref[...] = up32(na_ref[...])

        for go in (True, False):
            for i in range(sections):
                pl.when(flag_ref[2] == i)(lambda i=i, go=go: load(i, go))
        gain_a = gain_ref[0:1, :]
        normed = low16(norm_parts(x_ref[...])[0] * gain_a)
        na_ref[...] = normed
        nall[:rows] = normed
        nall[rows:] = low16(norm_parts(up32(nall[rows:]))[0] * gain_a)
        project(nall, wh, q, kv)

    row32, row16 = shape((rows, width), F32), shape((rows, width), BF)
    outs = [row32, row16, row16, shape((2 * rows, 2 * width), BF)]
    scratch = [pltpu.VMEM((2 * rows, width), BF), pltpu.SemaphoreType.DMA((2,))]
    ins = [SMEM, VMEM, VMEM] + [ANY] * len(sources)
    args = [flags, gains, w_heads, *[in_hbm(a) for a in sources]]
    return call(kernel, "last_project", outs, ins, scratch, args, 10 * rows * width * width, 12)


def last_attention(q, kv, bias, x, gains, w_heads, after=()):
    rows, width = q.shape

    def kernel(q_ref, kv_ref, bias_ref, x_ref, gain_ref, wh, mix, rest_ref, lse_ref, hid_ref, nb_ref):
        mix[...] = jnp.zeros_like(mix)
        lse_ref[...] = jnp.zeros_like(lse_ref)
        rest_ref[...] = jnp.zeros_like(rest_ref)
        attend(q_ref, kv_ref, bias_ref[0:1, :], mix, rest_ref, lse_ref)
        hidden = x_ref[...] + dot(mix[...], wh[:width, :])
        hid_ref[...] = hidden
        nb_ref[...] = low16(norm_parts(hidden)[0] * gain_ref[1:2, :])

    row32, row16 = shape((rows, width), F32), shape((rows, width), BF)
    outs = [row16, row16, shape((rows, LANES), F32), row32, row16]
    flops = 16 * rows * 2 * rows * WIN * 4 + 2 * rows * width * width
    return call(kernel, "last_attention", outs, [VMEM] * 6, [], [q, kv, bias, x, gains, w_heads], flops, 18, after)


def feed_turn(hidden, normed, dy_own, dy_got, gains, w_heads, w_up, w_down):
    rows, width = hidden.shape
    units = w_up.shape[0]

    half = dy_own.shape[0]

    def kernel(hid_ref, nb_ref, own_ref, got_ref, gain_ref, wh, wu, wd, out_ref, slope_ref, hg_ref, do_ref, dy_ref, act, nbg):
        dy_ref[:half] = own_ref[...]
        dy_ref[half:] = up32(got_ref[...])
        feed(nb_ref[...], hid_ref, wu, wd, act, slope_ref, out_ref)
        feed_grads(low16(dy_ref[...]), slope_ref, wu, wd, act, nbg)
        unit, inverse = norm_parts(hid_ref[...])
        hidden_grad = dy_ref[...] + norm_back(nbg[...], unit, inverse, gain_ref[1:2, :])
        hg_ref[...] = hidden_grad
        do_ref[...] = low16(dot_t(low16(hidden_grad), wh[:width, :]))

    row32 = shape((rows, width), F32)
    outs = [row32, shape((rows, units), BF), row32, shape((rows, width), BF), row32]
    scratch = [pltpu.VMEM((rows, units), BF), pltpu.VMEM((rows, width), F32)]
    flops = 8 * rows * width * units
    args = [hidden, normed, dy_own, dy_got, gains, w_heads, w_up, w_down]
    return call(kernel, "feed_turn", outs, [VMEM] * 8, scratch, args, flops, 22)


def feed_grads(low, slope_ref, w_up, w_down, inner, out, ups=()):
    for at, n in spans(w_up.shape[0], 512):
        inner[:, at : at + n] = low16(dot_t(low, w_down[at : at + n, :]) * up32(slope_ref[:, at : at + n]))
    wait_all(ups)
    for at, n in spans(w_up.shape[1], 256):
        out[:, at : at + n] = dot(inner[...], w_up[:, at : at + n])


def feed_back(mode, flags, sources, slope, hidden, gains, w_heads, w_ups, w_down, after=()):
    last = mode == "last"
    rows, width = hidden.shape
    units = w_down.shape[0]
    n_up = len(w_ups)

    def kernel(flag_ref, gain_ref, hid_ref, slope_ref, wh, wd, *refs):
        *refs, wu, up_sem = refs
        ups = [copy for copy, _ in span_copies(refs[:n_up], wu, up_sem, 0)]
        for copy in ups:
            copy.start()
        refs = refs[n_up:]
        src, refs = refs[: len(sources)], refs[len(sources) :]
        hg_ref, do_ref, refs = refs[0], refs[1], refs[2:]
        if last:
            ml_ref, gs_ref, ig, nbg, dy_ref, low, sem = refs

            def load(a, go):
                copy = pltpu.make_async_copy(a, dy_ref if a.dtype == F32 else low, sem.at[0])
                if go:
                    copy.start()
                    return
                copy.wait()
                if a.dtype == F32:
                    low[...] = low16(dy_ref[...])
                else:
                    dy_ref[...] = up32(low[...])

            for go in (True, False):
                for i, a in enumerate(src):
                    pl.when(flag_ref[2] == len(src) - 1 - i)(lambda a=a, go=go: load(a, go))
        else:
            ig, nbg, dy_ref, low = refs
            dy_ref[...] = src[0][...].astype(F32)
            low[...] = low16(src[0][...])
        feed_grads(low[...], slope_ref, wu, wd, ig, nbg, ups)
        unit, inverse = norm_parts(hid_ref[...])
        grad = nbg[...]
        if last:
            gs_ref[...] = jnp.sum(grad * unit, axis=0, keepdims=True)
        hidden_grad = dy_ref[...] + norm_back(grad, unit, inverse, gain_ref[1:2, :])
        hg_ref[...] = hidden_grad
        mix_low = low16(hidden_grad)
        if last:
            ml_ref[...] = mix_low
        do_ref[...] = low16(dot_t(mix_low, wh[:width, :]))

    sources = [in_hbm(a) if last else a for a in sources]
    args = [flags, gains, hidden, slope, w_heads, w_down, *[in_hbm(a) for a in w_ups], *sources]
    outs = [shape((rows, width), F32), shape((rows, width), BF)]
    if last:
        outs += [shape((rows, width), BF), shape((1, width), F32)]
    scratch = [
        pltpu.VMEM((rows, units), BF),
        pltpu.VMEM((rows, width), F32),
        pltpu.VMEM((rows, width), F32),
        pltpu.VMEM((rows, width), BF),
    ]
    if last:
        scratch.append(pltpu.SemaphoreType.DMA((1,)))
    scratch += [pltpu.VMEM((units, width), BF), pltpu.SemaphoreType.DMA((n_up,))]
    ins = [SMEM] + [VMEM] * 5 + [ANY] * n_up + [ANY if last else VMEM] * len(sources)
    flops = 4 * rows * width * units + 2 * rows * width * width
    return call(kernel, "feed_back_" + mode, outs, ins, scratch, args, flops, 24, after)


def attention_back(q, kv_all, do, mix, mix_rest, lse, bias, after=()):
    rows, width = q.shape
    keys_n = 2 * rows

    def kernel(q_ref, kv, do_ref, o_ref, rest_ref, lse_ref, bias_ref, dq_ref, dkv_own, dkv_far, qt, dt, dkt, dvt):
        bias_row = bias_ref[0:1, :]
        qt[...] = q_ref[...].T
        dt[...] = do_ref[...].T
        dq_ref[...] = jnp.zeros_like(dq_ref)
        zero = jnp.zeros((), BF)
        parts = ([], [])
        for h in range(width // HD):
            win, live = head_window(h, width)
            keys = jnp.where(live, kv[:, win], zero)
            vals = jnp.where(live, kv[:, width + win.start : width + win.stop], zero)
            d_out = do_ref[:, win]
            whole = up32(o_ref[:, win]) + up32(rest_ref[:, win])
            row_dot = jnp.sum(jnp.where(live, up32(d_out) * whole, 0.0), axis=-1, keepdims=True)
            s = dot_t(q_ref[:, win], keys) * (SCALE * LOG2E) + bias_row
            p = jnp.exp2(s - lse_ref[:, h : h + 1])
            ds = low16(p * (dot_t(d_out, vals) - row_dot))
            dq = dot(ds, keys) * SCALE
            dq_ref[:, win] = jnp.where(live, low16(dq), dq_ref[:, win])
            row = h % 2 * HD
            pair = slice((h - h % 2) * HD, (h - h % 2 + 2) * HD)
            parts[0].append(low16(dot(qt[pair, :][row : row + HD], ds) * SCALE))
            parts[1].append(low16(dot(dt[pair, :][row : row + HD], low16(p))))
            if h % 2:
                dkt[pair, :] = jnp.concatenate(parts[0], axis=0)
                dvt[pair, :] = jnp.concatenate(parts[1], axis=0)
                parts = ([], [])
        dk = dkt[...].T
        dv = dvt[...].T
        dkv_own[:, :width] = dk[:rows]
        dkv_own[:, width:] = dv[:rows]
        dkv_far[:, :width] = dk[rows:]
        dkv_far[:, width:] = dv[rows:]

    outs = [shape((rows, width), BF), shape((rows, 2 * width), BF), shape((rows, 2 * width), BF)]
    scratch = [
        pltpu.VMEM((width, rows), BF),
        pltpu.VMEM((width, rows), BF),
        pltpu.VMEM((width, keys_n), BF),
        pltpu.VMEM((width, keys_n), BF),
    ]
    flops = 16 * rows * keys_n * WIN * 10
    return call(kernel, "attention_back", outs, [VMEM] * 7, scratch, [q, kv_all, do, mix, mix_rest, lse, bias], flops, 17, after)


def qkv_back(full, flags, dq, own, got, x, hidden_grad, gains, w_heads, after=()):
    rows, width = dq.shape
    span = width // 4

    def kernel(flag_ref, gain_ref, dq_ref, own_ref, got_ref, x_ref, hg_ref, w, *refs):
        if full:
            dx_ref, low_ref, keep_ref, give_ref, gs_ref, grads, nag = refs
        else:
            low_ref, grads, nag = refs
        grads[:, :width] = dq_ref[...]
        grads[:, width:] = low16(up32(own_ref[...]) + up32(got_ref[...]))
        if full:
            mine = flag_ref[1] == 0
            for i in range(3):
                for xr in (0, 1):
                    at = i * width + 2 * xr * span
                    lo = grads[:, at : at + span]
                    hi = grads[:, at + span : at + 2 * span]
                    to = xr * 3 * span + i * span
                    keep_ref[:, to : to + span] = jnp.where(mine, lo, hi)
                    give_ref[:, to : to + span] = jnp.where(mine, hi, lo)
        for at, n in spans(width, 256):
            nag[:, at : at + n] = dot(grads[...], w[width:, at : at + n])
        unit, inverse = norm_parts(x_ref[...])
        grad = nag[...]
        if full:
            gs_ref[...] = jnp.sum(grad * unit, axis=0, keepdims=True)
        dx = hg_ref[...] + norm_back(grad, unit, inverse, gain_ref[0:1, :])
        low_ref[...] = low16(dx)
        if full:
            dx_ref[...] = dx

    outs = [shape((rows, width), BF)]
    if full:
        outs = [shape((rows, width), F32)] + outs
        outs += [shape((rows, 6 * span), BF), shape((rows, 6 * span), BF), shape((1, width), F32)]
    scratch = [pltpu.VMEM((rows, 3 * width), BF), pltpu.VMEM((rows, width), F32)]
    args = [flags, gains, dq, own, got, x, hidden_grad, w_heads]
    return call(kernel, "qkv_back", outs, [SMEM] + [VMEM] * 7, scratch, args, 6 * rows * width * width, 11, after)


def halves_of(total):
    steps = max(1, total // 736)
    return steps, total // steps


def halves_specs(steps, block, cols):
    return [
        pl.BlockSpec((block, cols), lambda i: (jnp.minimum(i, steps - 1), 0)),
        pl.BlockSpec((block, cols), lambda i: (jnp.maximum(i, steps) - steps, 0)),
    ]


def unit_forward(normed_four, normed_far, w_up, after=()):
    total, width = normed_four.shape
    n = w_up.shape[0]
    half, block = halves_of(total)

    def kernel(a_ref, b_ref, wu_ref, act_ref, slope_ref, token):
        token[...] = jnp.zeros_like(token)

        def rows(nb_ref):
            for at, k in spans(n, 512):
                act, slope = gelu_both(dot_t(nb_ref[...], wu_ref[at : at + k, :]))
                act_ref[:, at : at + k] = low16(act)
                slope_ref[:, at : at + k] = low16(slope)

        pl.when(pl.program_id(0) < half)(lambda: rows(a_ref))
        pl.when(pl.program_id(0) >= half)(lambda: rows(b_ref))

    by_rows = pl.BlockSpec((block, n), lambda i: (i, 0))
    return pl.pallas_call(
        past(kernel, 3, after),
        grid=(2 * half,),
        in_specs=[*halves_specs(half, block, width), VMEM, *[ANY] * len(after)],
        out_specs=(by_rows, by_rows, pl.BlockSpec((8, LANES), lambda i: (0, 0))),
        out_shape=(pltpu.HBM((2 * total, n), BF), pltpu.HBM((2 * total, n), BF), shape((8, LANES), F32)),
        compiler_params=pltpu.CompilerParams(vmem_limit_bytes=18 * 2**20),
        cost_estimate=pl.CostEstimate(flops=int(5.6 * COST * total * width * n), bytes_accessed=int(12 * COST * total * width), transcendentals=0),
        name="unit_forward",
    )(normed_four, normed_far, w_up, *after)


def pick_cols(a, which, part):
    picked = a[:, :part]
    for i in range(1, a.shape[1] // part):
        picked = jnp.where(which == i, a[:, i * part : (i + 1) * part], picked)
    return picked


def unit_sums(name, flags, sides, saved, w_down, units, part, after=()):
    total, width = sides[0][0].shape
    n = saved.shape[1]
    steps = max(1, total // 736)
    block = total // steps
    all_steps = steps * len(sides)
    kinds = len(sides[0])
    flat = [a for side in sides for a in side]
    with_w = w_down is not None

    def kernel(flag_ref, *refs):
        if with_w:
            wd_ref, refs = refs[0], refs[1:]
        saved_hbm, refs = refs[0], refs[1:]
        rows_hbm, refs = refs[: len(flat)], refs[len(flat) :]
        out, token, held, sems = refs[0], refs[1], refs[2 : 3 + kinds], refs[3 + kinds]
        token[...] = jnp.zeros_like(token)

        def into(i):
            rows = slice(i % steps * block, (i % steps + 1) * block)
            sources = [rows_hbm[i // steps * kinds + j].at[rows] for j in range(kinds)]
            sources.append(saved_hbm.at[i * block : (i + 1) * block])
            return [pltpu.make_async_copy(a, b.at[i % 2], sems.at[j, i % 2]) for j, (a, b) in enumerate(zip(sources, held))]

        for copy in into(0):
            copy.start()
        for i in range(all_steps):
            if i + 1 < all_steps:
                for copy in into(i + 1):
                    copy.start()
            wait_all(into(i))
            turned = pick_cols(held[0][i % 2], flag_ref[0], part).T
            for at, k in spans(n, 512):
                right = held[kinds][i % 2, :, at : at + k]
                if with_w:
                    right = low16(dot_t(held[1][i % 2], wd_ref[at : at + k, :]) * up32(right))
                real = min(k, units - at)
                cols = slice(at, at + real)
                got = dot(turned, right)[:, :real]
                out[:, cols] = got if i == 0 else out[:, cols] + got

    scratch = [pltpu.VMEM((2, block, width), BF)] * kinds + [pltpu.VMEM((2, block, n), BF)]
    scratch.append(pltpu.SemaphoreType.DMA((kinds + 1, 2)))
    args = [flags, *([w_down] if with_w else []), in_hbm(saved), *[in_hbm(a) for a in flat]]
    ins = [SMEM] + [VMEM] * with_w + [ANY] * (1 + len(flat))
    flops = (4 if with_w else 2) * total * len(sides) * width * n
    outs = [shape((part, units), F32), shape((8, LANES), F32)]
    return call(kernel, name, outs, ins, scratch, args, flops, 40, after, 0.2)


def join(name, pieces, after=()):
    n = len(pieces)

    def kernel(*refs):
        out, at = refs[n], 0
        for ref in refs[:n]:
            out[at : at + ref.shape[0]] = ref[...]
            at += ref.shape[0]

    rows = sum(a.shape[0] for a in pieces)
    return call(kernel, name, [pltpu.HBM((rows, pieces[0].shape[1]), BF)], [VMEM] * n, [], list(pieces), 0, 16, after)[0]


def plane_blocks(name, flags, left, right, after=()):
    rows = left[0].shape[0]
    part = right[0].shape[1] // 2
    span = left[0].shape[1] // 2
    h = span // 2
    cut = half_cut(h)

    def kernel(flag_ref, l0, l1, r0, r1, *refs):
        outs, ls, rs, sem = refs[:5], *refs[5:]
        copies = [
            pltpu.make_async_copy(a, c.at[at : at + rows], sem.at[i])
            for i, (a, c, at) in enumerate(((l0, ls, 0), (l1, ls, rows), (r0, rs, 0), (r1, rs, rows)))
        ]
        for copy in copies:
            copy.start()
        wait_all(copies)
        first = flag_ref[0] == 0
        lo, hi = rs[:, :part], rs[:, part:]
        shares = (jnp.where(first, lo, hi), jnp.where(first, hi, lo))
        for yr in (0, 1):
            for xr in (0, 1):
                got = t_dot(ls[:, xr * span : (xr + 1) * span], shares[yr])
                if yr == 0 and xr == 0:
                    outs[0][...] = got
                    continue
                for side in (0, 1):
                    cols = slice(side * part, (side + 1) * part)
                    top, bottom = low16(got[side * h : side * h + cut]), low16(got[side * h + cut : (side + 1) * h])
                    if xr and yr:
                        outs[1][cut:, cols] = top
                        outs[2][h - cut :, cols] = bottom
                    elif xr:
                        outs[1][:cut, cols] = top
                        outs[3][:, cols] = bottom
                    else:
                        outs[2][: h - cut, cols] = bottom
                        outs[4][:, cols] = top

    outs = [shape((span, part), F32)]
    outs += [shape((n, 2 * part), BF) for n in (2 * cut, 2 * (h - cut), h - cut, cut)]
    scratch = [pltpu.VMEM((2 * rows, 2 * span), BF), pltpu.VMEM((2 * rows, 2 * part), BF), pltpu.SemaphoreType.DMA((4,))]
    args = [flags, *left, *right]
    flops = 16 * rows * span * part
    return call(kernel, name, outs, [SMEM] + [ANY] * 4, scratch, args, flops, 24, after)


def scatter_middle(name, beside, above, via_x, via_y, after=()):
    rest, double = beside.shape
    cut = above.shape[0]

    def kernel(beside_ref, above_ref, vx, vy, to_y, to_x):
        to_y[...] = low16(up32(above_ref[...]) + up32(vx[cut:, :]))
        to_x[...] = low16(up32(beside_ref[...]) + up32(vy[rest:, :]))

    outs = [shape((cut, double), BF), shape((rest, double), BF)]
    to_y, to_x = call(kernel, name, outs, [VMEM] * 4, [], [beside, above, via_x, via_y], 0, 16, after)
    return swap_y(to_y), swap_x(to_x)


def scatter_end(name, own, via_x, via_y, over_y, over_x, count, after=()):
    span, part = own.shape
    h = span // 2
    cut = half_cut(h)
    rest = h - cut
    each = span // count

    def kernel(own_ref, vx, vy, oy, ox, *refs):
        outs, total = refs[:count], refs[count]
        for side in (0, 1):
            cols = slice(side * part, (side + 1) * part)
            base = side * h
            total[base : base + cut] = own_ref[base : base + cut, :] + up32(vx[:cut, cols]) + up32(oy[:, cols])
            total[base + cut : base + h] = own_ref[base + cut : base + h, :] + up32(vy[:rest, cols]) + up32(ox[:, cols])
        for i, out in enumerate(outs):
            out[...] = total[i * each : (i + 1) * each]

    outs = [shape((each, part), F32)] * count
    scratch = [pltpu.VMEM((span, part), F32)]
    return call(kernel, name, outs, [VMEM] * 5, scratch, [own, via_x, via_y, over_y, over_x], 0, 24, after)


def gather_gains(shard, moves, dp_idx, x_idx, core):
    if not two_rows():
        return lax.all_gather(shard, ("dp", "tensor"), axis=1, tiled=True)
    beside, above, across = moves

    def pair(index, a, b):
        return jnp.where(index == 0, jnp.concatenate((a, b), axis=1), jnp.concatenate((b, a), axis=1))

    four = jnp.concatenate((shard, beside, above, across), axis=1)
    other = swap_core(four)
    n = shard.shape[1]
    by_core = [pair(core, four[:, i * n : (i + 1) * n], other[:, i * n : (i + 1) * n]) for i in range(4)]
    return pair(dp_idx, pair(x_idx, *by_core[:2]), pair(x_idx, *by_core[2:]))


def ties(*arrays):
    return list(lax.optimization_barrier(arrays))


def tie(a, *others):
    return ties(a, *others)[0]


def local(images, valid_len, query_weight, key_weight, value_weight, output_weight, up_weight, down_weight, norm_gains, cotangent):
    section = lax.axis_index("section")
    sections = lax.axis_size("section")
    dp_idx = lax.axis_index("dp")
    dp = lax.axis_size("dp")
    tensor_idx = lax.axis_index("tensor")
    x_idx, core = tensor_idx // 2, tensor_idx % 2
    per_dp, quarter, width = images.shape
    assert per_dp == 2 and lax.axis_size("tensor") == 4
    padded_quarter = (quarter + 7) // 8 * 8
    flags = jnp.stack((dp_idx, core, section, x_idx)).astype(jnp.int32)

    def pad_rows(a):
        return jnp.pad(a, ((0, padded_quarter - quarter), (0, 0)))

    def mine(a):
        return pad_rows(lax.dynamic_index_in_dim(a, x_idx, 0, keepdims=False))

    def theirs(a):
        return pad_rows(low16(lax.dynamic_index_in_dim(a, 1 - x_idx, 0, keepdims=False)))

    def give_back(rows):
        return swap_x(low16(rows[padded_quarter:]))

    def both_images(rows, got, after=()):
        def kernel(flag_ref, own_ref, got_ref, out, token):
            token[...] = jnp.zeros_like(token)
            first = flag_ref[3] == 0
            own, other = own_ref[:quarter], up32(got_ref[...])[:quarter]
            out[:, 0, :] = jnp.where(first, own, other)
            out[:, 1, :] = jnp.where(first, other, own)

        outs = [shape((quarter, 2, width), F32), shape((8, LANES), F32)]
        return call(kernel, "both_images", outs, [SMEM, VMEM, VMEM], [], [flags, rows, got], 0, 16, after)

    rows = 2 * padded_quarter
    valid = lax.dynamic_index_in_dim(valid_len, x_idx, 0, keepdims=False)
    spot = jnp.arange(padded_quarter)
    live = [
        (spot < quarter) & ((2 * xx + cc) * quarter + spot < valid) for cc in (core, 1 - core) for xx in (x_idx, 1 - x_idx)
    ]
    bias = jnp.where(jnp.concatenate(live), 0.0, -1e30).astype(F32)[None, :]
    bias = jnp.broadcast_to(bias, (8, bias.shape[1]))

    span = query_weight.shape[2]
    units = up_weight.shape[2]
    part = width // dp
    plane = two_rows()

    gain_moves = [move(norm_gains[0]) for move in (swap_x, swap_y, swap_both)] if plane else []
    turned = [jnp.transpose(w[0]) for w in (query_weight, key_weight, value_weight)]
    packed, give_rows, keep_rows, (at_heads, at_up, at_down), h_units = pack(
        flags, [*turned, output_weight[0]], up_weight[0], jnp.transpose(down_weight[0]), jnp.transpose(images, (1, 0, 2)),
        padded_quarter,
    )
    h_heads = span // 2
    if plane:
        from_x, from_y = swap_x(packed), swap_y(packed)
        img_got = swap_x(give_rows)
        at = 2 * h_heads
        over_heads = [(swap_x(from_y[:at]), 0, at), (swap_y(from_x[at:at_up]), 0, at)]
        up_on, down_on = from_y[at_up:at_down], from_x[at_down:]
        over_up, over_down = [(swap_x(up_on), 0, h_units)], [(swap_y(down_on), 0, h_units)]
        cuts = [up_on, down_on]
        near = lambda row, rows: [[(packed, row, rows)], [(from_y, row, rows)]]
        far = lambda row, rows, over: [[(from_x, row, rows)], over]
    else:
        whole = lax.all_gather(packed, "dp")
        other = swap_x(whole)
        over_heads = over_up = over_down = None
        cuts = []
        img_got = swap_x(give_rows)
        near = lambda row, rows: [[(whole[i], row, rows)] for i in range(dp)]
        far = lambda row, rows, over: [[(other[i], row, rows)] for i in range(dp)]
    gains = gather_gains(norm_gains[0], gain_moves, dp_idx, x_idx, core)
    first_rows = jnp.concatenate((keep_rows, up32(img_got)), axis=0)
    first_far = swap_core(low16(first_rows))
    heads_near = put_together("heads_near", near(at_heads, 4 * h_heads), flags, 4, h_heads)
    up_near = put_together("up_near", near(at_up, h_units), flags, 1, h_units, [heads_near])[0]
    down_near = put_together("down_near", near(at_down, h_units), flags, 1, h_units, [heads_near])[0]
    heads_far = put_together("heads_far", far(at_heads, 4 * h_heads, over_heads), flags, 4, h_heads, [up_near, down_near, *cuts])
    heads = [heads_near, heads_far, swap_core(heads_near), swap_core(heads_far)]
    hidden, normed_b = layer_first(flags, first_rows, first_far, bias, gains, heads)
    up_near = [up_near, swap_core(up_near)]
    down_near = [down_near, swap_core(down_near)]
    act_near = feed_up(normed_b, up_near)
    half_out = feed_down(hidden, act_near, down_near, F32)
    up_far = put_together("up_far", far(at_up, h_units, over_up), flags, 1, h_units, [half_out])[0]
    up_far = [up_far, swap_core(up_far)]
    down_far = put_together("down_far", far(at_down, h_units, over_down), flags, 1, h_units, [half_out])[0]
    down_far = [down_far, swap_core(down_far)]
    act_far = feed_up(normed_b, up_far)
    out = feed_down(half_out, act_far, down_far, BF)

    def fetch(after):
        return settle(flags, after, heads, up_near + up_far, down_near + down_far)

    sources = [first_rows, first_far]
    for tick in range(1, sections):
        got = shift(out, 1)
        if tick == 1:
            weights, token = fetch(out)
            got, token = ties(got, token)
        sources += [got, swap_core(got)]
        if tick + 1 < sections:
            out = layer_mid(flags, *sources[-2:], bias, gains, *weights, [token] if tick == 1 else [])
            if tick == 1:
                cot_got = swap_x(theirs(cotangent))
    x, normed_a, q, kv = last_project(flags, sources, gains, weights[0])
    mix, mix_rest, lse, hidden, normed_b = last_attention(q, kv, bias, x, gains, weights[0])
    out, slope, hidden_grad, do, dy = feed_turn(hidden, normed_b, mine(cotangent), cot_got, gains, *weights)

    sources = [dy]
    acts_got = give_back(out)

    def core_halves(a):
        lo = jnp.concatenate((a[:, :span], a[:, 2 * span : 3 * span]), axis=1)
        hi = jnp.concatenate((a[:, span : 2 * span], a[:, 3 * span :]), axis=1)
        return jnp.where(core == 0, lo, hi), jnp.where(core == 0, hi, lo)

    at = half_cut(rows)

    at = half_cut(rows)
    for tick in range(sections):
        last = tick + 1 == sections
        if last:
            dy_low = low16(sources[0])
            for i, a in enumerate(sources[1:]):
                dy_low = jnp.where(section == sections - 2 - i, a, dy_low)
            if plane:
                dy_x0, dy_y1 = swap_x(dy_low[:at]), swap_y(dy_low[at:])
        if tick:
            mode = "last" if last else "mid"
            used, after = (sources, [unit_done]) if last else (sources[-1:], [acts_got] if tick == 1 else [acts_done, nb_x1, nb_y0])
            results = feed_back(mode, flags, used, slope, hidden, gains, weights[0], up_near + up_far, weights[2], after)
            hidden_grad, do = results[:2]
        if last:
            mix_low, gain_sum_b = results[2:]
            mix_got, ml_far = swap_core(mix_give), swap_core(mix_low)
        after = []
        if plane and tick == 1:
            after = [nb_x0, nb_y1]
        if plane and tick == 2:
            after = [nb_d0, nb_d1]
        if plane and last:
            dy_d0, dy_d1 = swap_y(dy_x0), swap_x(dy_y1)
            after = [dy_x0, dy_y1]
        dq, dkv, dkv_far = attention_back(q, kv, do, mix, mix_rest, lse, bias, after)
        dkv_got = swap_core(dkv_far)
        after = []
        if plane and last:
            o_parts = plane_blocks("output_grads", flags, (mix_keep, mix_got), (mix_low, ml_far), [dq])
            o_via = swap_x(o_parts[1]), swap_y(o_parts[2])
            dy_rest = tie(dy_low, dq)
            dy_x1, dy_y0 = swap_x(dy_rest[at:]), swap_y(dy_rest[:at])
            after = [o_parts[4], dy_d0, dy_d1]
        if plane and tick == 2:
            nb_four = join("join_normed", [normed_b, nb_x0, nb_x1, nb_y0, nb_y1, nb_d0, nb_d1], [dq])
            after = [nb_four]
        back = qkv_back(last, flags, dq, dkv, dkv_got, x, hidden_grad, gains, weights[0], after)
        if last:
            break
        low = back[0]
        if plane and tick == 2:
            nb_four, low = ties(nb_four, low)
        got = shift(low, -1)
        if tick == 0:
            nb_x0 = nb_x1 = nb_y0 = nb_y1 = normed_b
            if plane:
                nb_x0, nb_y1 = swap_x(normed_b[:at]), swap_y(normed_b[at:])
        elif tick == 1:
            if plane:
                nb_x1, nb_y0 = swap_x(normed_b[at:]), swap_y(normed_b[:at])
                nb_d0, nb_d1 = swap_y(nb_x0), swap_x(nb_y1)
            acts, acts_done = both_images(out, acts_got)
            mix_keep, mix_give = core_halves(mix)
            na_far = swap_core(normed_a)
        elif tick == 2:
            if plane:
                nb_far = swap_core(nb_four)
            else:
                nb_all = lax.all_gather(normed_b, ("dp", "tensor"), axis=0, tiled=True)
                nb_four, nb_far = jnp.split(nb_all, 2)
            act_all, slope_all, unit_done = unit_forward(nb_four, nb_far, up_near[0], [mix_keep, mix_give, na_far])
            got, unit_done = ties(got, unit_done)
        sources.append(got)
    dx, _, keep, give, gain_sum_a = back

    got = swap_core(give)
    grads_got = give_back(dx)
    gain_sums = jnp.concatenate((gain_sum_a, gain_sum_b), axis=0)
    if plane:
        gain_moves = [move(gain_sums) for move in (swap_x, swap_y, swap_both)]
        qkv_parts = plane_blocks("qkv_grads", flags, (keep, got), (normed_a, na_far))
        via = swap_x(qkv_parts[1]), swap_y(qkv_parts[2])
        dy_four = join("join_dy", [dy_low, dy_x0, dy_x1, dy_y0, dy_y1, dy_d0, dy_d1], [qkv_parts[0]])
        dy_far = swap_core(dy_four)
        sides = [(nb_four, dy_four), (nb_far, dy_far)]
        grad_up, up_done = unit_sums("up_grads", flags, sides, slope_all, down_near[0], units, part, [qkv_parts[0]])
        over = scatter_middle("qkv_middle", *qkv_parts[3:], *via, [up_done])
        o_over = scatter_middle("output_middle", *o_parts[3:], *o_via, [up_done])
        grad_down, down_done = unit_sums("down_grads", flags, [(dy_four,), (dy_far,)], act_all, None, units, part, [up_done, *gain_moves])
        gain_sums = gain_sums + gain_moves[0] + gain_moves[1] + gain_moves[2]
        gain_sums = gain_sums + swap_core(gain_sums)
        (grad_o,) = scatter_end("output_end", o_parts[0], *o_via, *o_over, 1, [down_done])
        grad_heads = scatter_end("qkv_end", qkv_parts[0], *via, *over, 3, [down_done])
        gain_shard = lax.dynamic_slice_in_dim(gain_sums, (dp_idx * 4 + tensor_idx) * (width // 8), width // 8, 1)
        grads_after = [down_done]
    else:
        dy_all = lax.all_gather(dy_low, ("dp", "tensor"), axis=0, tiled=True)
        dy_four, dy_far = jnp.split(dy_all, 2)
        grad_up, _ = unit_sums("up_grads", flags, [(nb_four, dy_four), (nb_far, dy_far)], slope_all, down_near[0], units, part)
        grad_down, _ = unit_sums("down_grads", flags, [(dy_four,), (dy_far,)], act_all, None, units, part)
        grads_after = []
        both = lambda a, b: jnp.concatenate((a, b), axis=0)
        g = t_dot(both(keep, got), both(normed_a, na_far))
        g = g[: 3 * span] + up32(swap_x(low16(g[3 * span :])))
        g = up32(lax.psum_scatter(low16(g), "dp", scatter_dimension=1, tiled=True))
        grad_heads = [g[i * span : (i + 1) * span] for i in range(3)]
        g = t_dot(both(mix_keep, swap_core(mix_give)), both(mix_low, swap_core(mix_low)))
        g = g[:span] + up32(swap_x(low16(g[span:])))
        grad_o = up32(lax.psum_scatter(low16(g), "dp", scatter_dimension=1, tiled=True))
        gain_shard = lax.psum_scatter(gain_sums, ("dp", "tensor"), scatter_dimension=1, tiled=True)
    grads, _ = both_images(dx, grads_got, grads_after)

    return (
        jnp.transpose(acts, (1, 0, 2))[None],
        jnp.transpose(grads, (1, 0, 2))[None],
        *[jnp.transpose(g)[None] for g in grad_heads],
        grad_o[None],
        grad_up[None],
        jnp.transpose(grad_down)[None],
        gain_shard[None],
    )


def solution(mesh):
    return jax.shard_map(
        local,
        mesh=mesh,
        in_specs=(
            P("dp", "tensor", None),
            P("dp"),
            P("section", "dp", "tensor"),
            P("section", "dp", "tensor"),
            P("section", "dp", "tensor"),
            P("section", "tensor", "dp"),
            P("section", "dp", "tensor"),
            P("section", "tensor", "dp"),
            P("section", None, ("dp", "tensor")),
            P("dp", "tensor", None),
        ),
        out_specs=(
            P("section", "dp", "tensor", None),
            P("section", "dp", "tensor", None),
            P("section", "dp", "tensor"),
            P("section", "dp", "tensor"),
            P("section", "dp", "tensor"),
            P("section", "tensor", "dp"),
            P("section", "dp", "tensor"),
            P("section", "tensor", "dp"),
            P("section", None, ("dp", "tensor")),
        ),
        check_vma=False,
    )
```
